32 devices in a mesh: row: 16 (over z, y, x), col: 2 (over core).
Axes of the slice: x: 2, y: 2, z: 4, core: 2. Of those that a mesh axis runs over, the one named last changes fastest.
Arguments:
- tile_values: float32 [16, 2, 64, 128, 128], P('row', 'col'), may hold values from -0.09375 to 0.09375
- tile_row: int32 [16, 2, 64], P('row', 'col'), may hold values from 0 to 7
- tile_col: int32 [16, 2, 64], P('row', 'col'), may hold values from 0 to 63
- counts: int32 [16, 2], P('row', 'col'), may hold values from 21 to 64, as said below
- diagonal: float32 [16384], P(('row', 'col')), may hold values from 1 to 3
- current: float32 [8, 16384], P(None, ('row', 'col')), may hold values from -6 to 6
- previous: float32 [8, 16384], P(None, ('row', 'col')), may hold values from -6 to 6
- previous_image: float32 [8, 16384], P(None, ('row', 'col')), may hold values from -6 to 6
Outputs:
- image: float32 [8, 16384], P(None, ('row', 'col'))
- residual: float32 [8, 16384], P(None, ('row', 'col'))
- residual_image: float32 [8, 16384], P(None, ('row', 'col'))
- reduced: float32 [24, 24], replicated
The draws below stay inside these ranges and needn't reach their ends.
Inputs may be any that keep to these rules, and one draw needn't show every extreme that they name: `counts`: every device has between 21 and 64 live slots; in every draw one device has exactly 64 and one exactly 21.
All inputs are finite; a program needn't handle non-finite values.
Results may differ from the reference program's by a relative error of at most 0.0003.
Values sent between devices are 32-bit elements; how exact they have to be, the bound alone decides.
No kernel may reach another device: no remote copies, remote signals or barrier semaphores. Data moves between devices by JAX's collectives and lax.ppermute only.
A program may use at most 64 MiB of HBM per device.

```python
import jax
import jax.numpy as jnp
from jax import lax

K = 8
TILE = 128
VT = 4
SLOTS = 64
NDIM = 16384
N_ROW = 16
N_COL = 2


def draw_counts(key, part):
    owners = N_ROW * N_COL
    least_count = SLOTS // 3
    spread = SLOTS - least_count
    first_key, second_key, pick_key = jax.random.split(key, 3)
    first_draw = jax.random.randint(first_key, (owners,), 0, spread + 1, dtype=jnp.int32)
    second_draw = jax.random.randint(second_key, (owners,), 0, spread + 1, dtype=jnp.int32)
    values = least_count + first_draw * second_draw // spread
    picked = jax.random.permutation(pick_key, owners)
    values = values.at[picked[0]].set(SLOTS).at[picked[1]].set(least_count)
    return values.astype(jnp.int32).reshape(N_ROW, N_COL)


def place_ends(drawn, key, low, high):
    longest = drawn.shape.index(max(drawn.shape))
    spots = []
    for shift in (0, 1):
        where = [jax.random.randint(jax.random.fold_in(key, axis), (), 0, length) for axis, length in enumerate(drawn.shape)]
        where[longest] = (where[longest] + shift) % drawn.shape[longest]
        spots.append(tuple(where))
    return drawn.at[spots[0]].set(low).at[spots[1]].set(high)


def level_of(key, shape, cuts, smallest, largest):
    gain, own = 1.0, jax.random.fold_in(key, 6)
    for dim, parts in cuts:
        draws = jnp.exp(jax.random.uniform(jax.random.fold_in(own, dim), (parts,), jnp.float32, smallest / len(cuts), largest / len(cuts)))
        gain = gain * jnp.repeat(draws, shape[dim] // parts).reshape([-1 if axis == dim else 1 for axis in range(len(shape))])
    return gain


def gaussian(stream_key, extent, scale, limit, shards=(), held_as=jnp.bfloat16):
    result = jax.random.normal(stream_key, extent, jnp.float32) * scale
    if len(shards) > 0:
        result = level_of(stream_key, extent, shards, -0.22, 0.18) * result
    return jnp.clip(result, min=-limit, max=limit).astype(held_as)


def setup_inputs(seed: int = 0) -> dict:
    arg_keys = jax.random.split(jax.random.key(seed), 9)
    return {
        "tile_values": gaussian(arg_keys[0], (N_ROW, N_COL, SLOTS, TILE, TILE), (2 * SLOTS * TILE // VT) ** -0.5, 0.09375, ((0, 16), (1, 2)), jnp.float32),
        "tile_row": place_ends(jax.random.randint(arg_keys[1], (N_ROW, N_COL, SLOTS), 0, N_COL * VT), jax.random.fold_in(arg_keys[1], 1), 0, (N_COL * VT) - 1).astype(jnp.int32),
        "tile_col": place_ends(jax.random.randint(arg_keys[2], (N_ROW, N_COL, SLOTS), 0, N_ROW * VT), jax.random.fold_in(arg_keys[2], 1), 0, (N_ROW * VT) - 1).astype(jnp.int32),
        "counts": draw_counts(jax.random.fold_in(arg_keys[8], 71), 0),
        "diagonal": jnp.clip(1.0 + 2.0 * jax.random.uniform(arg_keys[4], (NDIM,), jnp.float32) ** level_of(arg_keys[4], (NDIM,), ((0, 32),), -0.2, 0.2), 1.0, 3.0),
        "current": gaussian(arg_keys[5], (K, NDIM), 1.0, 6.0, ((1, 32),), jnp.float32),
        "previous": gaussian(arg_keys[6], (K, NDIM), 1.0, 6.0, ((1, 32),), jnp.float32),
        "previous_image": gaussian(arg_keys[7], (K, NDIM), 1.0, 6.0, ((1, 32),), jnp.float32),
    }


highest = lax.Precision.HIGHEST

def apply_operator(vectors, diagonal, tile_values, tile_row, tile_col, counts):
    vector_count = vectors.shape[0]
    columns = vectors.reshape(vector_count, -1, TILE)
    owners = N_ROW * N_COL
    owner_ids = jnp.arange(owners, dtype=jnp.int32)
    flat_tiles = tile_values.reshape(owners, SLOTS, TILE, TILE)
    flat_rows = tile_row.reshape(owners, SLOTS)
    flat_cols = tile_col.reshape(owners, SLOTS)
    flat_counts = counts.reshape(owners)
    slot_ids = jnp.arange(SLOTS, dtype=jnp.int32)

    def one_device(running_sum, device_item):
        blocks, rows_here, cols_here, live_count, owner = device_item
        row_owner = owner // N_COL
        col_owner = owner % N_COL
        global_rows = row_owner * (N_COL * VT) + rows_here
        global_cols = (cols_here // VT * N_COL + col_owner) * VT + cols_here % VT
        weight = (slot_ids < live_count).astype(jnp.float32)[None, :, None]
        direct = jnp.einsum('sij,ksj->ksi', blocks, columns[:, global_cols, :], precision=highest) * weight
        mirror = jnp.einsum('sij,ksi->ksj', blocks, columns[:, global_rows, :], precision=highest) * weight
        running_sum = running_sum.at[:, global_rows, :].add(direct)
        running_sum = running_sum.at[:, global_cols, :].add(mirror)
        return (running_sum, None)
    zero_sum = jnp.zeros_like(columns)
    running_sum, unused = lax.scan(one_device, zero_sum, (flat_tiles, flat_rows, flat_cols, flat_counts, owner_ids))
    return diagonal[None, :] * vectors + running_sum.reshape(vector_count, -1)

def dot_rows(left, right):
    return jnp.dot(left, right.T, precision=highest)

def reference(tile_values, tile_row, tile_col, counts, diagonal, current, previous, previous_image):
    image = apply_operator(current, diagonal, tile_values, tile_row, tile_col, counts)
    small_gram = dot_rows(current, current)
    small_proj = dot_rows(current, image)
    factor = jnp.linalg.cholesky(small_gram)
    ritz_matrix = jax.scipy.linalg.cho_solve((factor, True), small_proj)
    residual = image - jnp.dot(ritz_matrix.T, current, precision=highest)
    residual_image = apply_operator(residual, diagonal, tile_values, tile_row, tile_col, counts)
    search_basis = jnp.concatenate([current, residual, previous], 0)
    basis_image = jnp.concatenate([image, residual_image, previous_image], 0)
    correlation = dot_rows(search_basis, search_basis)
    mixed_terms = dot_rows(search_basis, basis_image)
    pencil = 0.5 * (mixed_terms + mixed_terms.T)
    lower_factor = jnp.linalg.cholesky(correlation)
    half_solve = jax.scipy.linalg.solve_triangular(lower_factor, pencil, lower=True)
    reduced = jax.scipy.linalg.solve_triangular(lower_factor, half_solve.T, lower=True)
    return (image, residual, residual_image, reduced)
```

```python
import functools
import math

import jax
import jax.numpy as jnp
from jax import lax
from jax.experimental import pallas as pl
from jax.experimental.pallas import tpu as pltpu
from jax.sharding import PartitionSpec as P

f32 = jnp.float32
bf16 = jnp.bfloat16
highest = lax.Precision.HIGHEST
LANES = 128
in_vmem = pl.BlockSpec(memory_space=pltpu.VMEM)
in_smem = pl.BlockSpec(memory_space=pltpu.SMEM)
params = pltpu.CompilerParams(vmem_limit_bytes=40 * 2**20)


def call(kernel, name, out_shape, operands, specs, scratch=()):
    return pl.pallas_call(
        kernel,
        out_shape=out_shape,
        in_specs=specs,
        out_specs=jax.tree.map(lambda _: in_vmem, out_shape),
        scratch_shapes=scratch,
        compiler_params=params,
        name=name,
    )(*operands)


def shape(*dims):
    return jax.ShapeDtypeStruct(dims, f32)


def halves(values):
    high = values.astype(bf16)
    return high, (values - high.astype(f32)).astype(bf16)


def times_transpose(left, right, precision=None):
    return lax.dot_general(
        left, right, (((1,), (1,)), ((), ())), preferred_element_type=f32, precision=precision
    )


def times(left, right, precision=None):
    return lax.dot_general(
        left, right, (((1,), (0,)), ((), ())), preferred_element_type=f32, precision=precision
    )


def tile_of(ref, t):
    return ref[:, t * LANES : (t + 1) * LANES]


def spread_kernel(x_ref, p_ref, spread_ref, own_ref):
    for t in range(own_ref.shape[0]):
        pair = jnp.concatenate([tile_of(x_ref, t), tile_of(p_ref, t)], axis=0)
        own_ref[t] = pair
        for r in range(spread_ref.shape[0]):
            spread_ref[r, t] = pair


def fill_row_block(block_ref, own_ref, other_ref, here, paired):
    tiles = own_ref.shape[0]
    if paired:
        for t in range(tiles):
            block_ref[here * tiles + t] = own_ref[t]
            block_ref[(1 - here) * tiles + t] = other_ref[t]
    else:
        for c in range(other_ref.shape[0]):
            for t in range(tiles):
                block_ref[c * tiles + t] = other_ref[c, t]


def hand_row_sums(row_sum, keep_ref, send_ref, here, paired):
    tiles = keep_ref.shape[0]
    if paired:
        for t in range(tiles):
            keep_ref[t] = row_sum[here * tiles + t]
            send_ref[t] = row_sum[(1 - here) * tiles + t]
    else:
        keep_ref[...] = jnp.zeros_like(keep_ref)
        for c in range(send_ref.shape[0]):
            for t in range(tiles):
                send_ref[c, t] = row_sum[c * tiles + t]


def visit_slots(live, rows, cols, blocks, column_halves, row_halves, row_sums, column_sum):
    slots = blocks.shape[0]
    group = math.gcd(slots, 16)
    count = 8 * len(row_sums)

    def visit(index, _):
        products = []
        for s in range(group):
            slot = index * group + s
            a = rows[slot]
            b = cols[slot]
            high, low = halves(blocks[slot])
            x = column_halves[b]
            u = row_halves[a]
            weight = jnp.where(slot < live, 1.0, 0.0).astype(f32)
            direct = times_transpose(
                jnp.concatenate([x, x], axis=1), jnp.concatenate([high, low], axis=1)
            )
            mirror = times(jnp.concatenate([u, u], axis=1), jnp.concatenate([high, low], axis=0))
            products.append(
                (
                    a,
                    b,
                    (direct[:count] + direct[count:]) * weight,
                    (mirror[:8] + mirror[8:]) * weight,
                )
            )
        for a, b, direct, mirror in products:
            for n, row_sum in enumerate(row_sums):
                row_sum[a] += direct[8 * n : 8 * n + 8]
            column_sum[b] += mirror
        return 0

    lax.fori_loop(0, (live + group - 1) // group, visit, 0)


def first_kernel(
    paired, live, rows, cols, here, blocks, gathered, own, other,
    keep, send, previous_sum, column_sum,
    column_halves, row_block, row_halves, row_sum,
):
    here = here[0]
    for j in range(gathered.shape[0]):
        high, low = halves(gathered[j])
        column_halves[j] = jnp.concatenate([high, low], axis=0)
    fill_row_block(row_block, own, other, here, paired)
    for j in range(row_block.shape[0]):
        high, low = halves(row_block[j, 0:8])
        row_halves[j] = jnp.concatenate([high, low], axis=0)
    row_sum[...] = jnp.zeros_like(row_sum)
    previous_sum[...] = jnp.zeros_like(previous_sum)
    column_sum[...] = jnp.zeros_like(column_sum)
    visit_slots(
        live[0], rows, cols, blocks, column_halves, row_halves, [row_sum, previous_sum], column_sum
    )
    hand_row_sums(row_sum, keep, send, here, paired)


def owned_sum(t, diagonal, vectors, keep, received, parts, paired):
    total = tile_of(diagonal, t) * vectors + keep[t]
    if paired:
        total = total + received[t]
    else:
        for c in range(received.shape[0]):
            total = total + received[c, t]
    columns = [parts[r, t] for r in range(parts.shape[0])]
    while len(columns) > 1:
        columns = [sum(columns[n : n + 2]) for n in range(0, len(columns), 2)]
    return total + columns[0]


def image_kernel(paired, diagonal, x_ref, keep, received, parts, image, own, spread):
    for t in range(own.shape[0]):
        value = owned_sum(t, diagonal, tile_of(x_ref, t), keep, received, parts, paired)
        image[:, t * LANES : (t + 1) * LANES] = value
        own[t] = value
        for r in range(spread.shape[0]):
            spread[r, t] = value


def second_kernel(
    paired, live, rows, cols, here, blocks, gathered, own, other, pair_own, pair_other, previous_sum,
    diagonal, x_ref, y_ref, p_ref, q_ref,
    keep, send, payload,
    column_halves, row_block, pair_block, row_halves, row_sum, column_sum,
):
    here = here[0]
    for j in range(gathered.shape[0]):
        high, low = halves(gathered[j])
        column_halves[j] = jnp.concatenate([high, low], axis=0)
    fill_row_block(row_block, own, other, here, paired)
    fill_row_block(pair_block, pair_own, pair_other, here, paired)
    for j in range(row_block.shape[0]):
        high, low = halves(row_block[j])
        row_halves[j] = jnp.concatenate([high, low], axis=0)
    row_sum[...] = jnp.zeros_like(row_sum)
    column_sum[...] = jnp.zeros_like(column_sum)
    visit_slots(live[0], rows, cols, blocks, column_halves, row_halves, [row_sum], column_sum)
    hand_row_sums(row_sum, keep, send, here, paired)
    tiles = own.shape[0]
    for r in range(payload.shape[0]):
        for t in range(tiles):
            payload[r, t] = column_sum[r * tiles + t]
    x, y, p, q = x_ref[...], y_ref[...], p_ref[...], q_ref[...]
    raw = jnp.concatenate([x, y, p, q], axis=0)
    outer = times_transpose(jnp.concatenate([x, y, p], axis=0), raw, highest)
    own_rows = times_transpose(diagonal[...] * y, jnp.concatenate([y, p], axis=0), highest)
    images = jnp.concatenate([row_sum[j] for j in range(row_sum.shape[0])], axis=1)
    images_previous = jnp.concatenate([previous_sum[j] for j in range(row_sum.shape[0])], axis=1)
    block_y = jnp.concatenate([row_block[j] for j in range(row_sum.shape[0])], axis=1)
    block_p = jnp.concatenate([pair_block[j, 8:16] for j in range(row_sum.shape[0])], axis=1)
    stored = times_transpose(images, jnp.concatenate([block_y, block_p], axis=0), highest)
    stored_previous = times_transpose(block_y, images_previous, highest)
    yz = 2.0 * stored[:, 0:8] + own_rows[:, 0:8]
    zp = stored[:, 8:16] + own_rows[:, 8:16] + stored_previous
    gram = jnp.concatenate(
        [
            outer[0:8, 0:24],
            outer[0:8, 8:16],
            outer[8:16, 8:16],
            outer[0:8, 24:32] + outer[8:16, 16:24],
            outer[8:16, 16:24],
            yz,
            outer[8:16, 24:32] + zp,
            outer[16:24, 16:24],
            outer[16:24, 24:32],
            jnp.zeros((8, LANES - 88), f32),
        ],
        axis=1,
    )
    for r in range(payload.shape[0]):
        payload[r, tiles] = gram


def gather_sum_kernel(paired, diagonal, y_ref, keep, received, parts, z_ref, gram):
    tiles = keep.shape[0]
    for t in range(tiles):
        z_ref[:, t * LANES : (t + 1) * LANES] = owned_sum(
            t, diagonal, tile_of(y_ref, t), keep, received, parts, paired
        )
    gram[...] = sum(parts[r, tiles] for r in range(parts.shape[0]))


def finish_kernel(x_ref, y_ref, z_ref, mine, theirs, residual, residual_image, reduced):
    gram = mine[...] + theirs[...]
    turned = gram.T

    def block(n):
        return gram[:, 8 * n : 8 * n + 8]

    def flipped(n):
        return turned[8 * n : 8 * n + 8, :]

    xx, xy, xp, xy_again, yy, mixed, yp, yz, zp, pp, pq = range(11)
    unit = (
        lax.broadcasted_iota(jnp.int32, (24, 24), 0) == lax.broadcasted_iota(jnp.int32, (24, 24), 1)
    ).astype(f32)
    work = jnp.concatenate(
        [
            jnp.concatenate(
                [gram[:, 0:24], 0.5 * (block(xy) + flipped(xy)), block(yy), 0.5 * block(mixed)], axis=1
            ),
            jnp.concatenate(
                [
                    flipped(xy), block(yy), block(yp),
                    block(yy), 0.5 * (block(yz) + flipped(yz)), 0.5 * block(zp),
                ],
                axis=1,
            ),
            jnp.concatenate(
                [
                    flipped(xp), flipped(yp), block(pp),
                    0.5 * flipped(mixed), 0.5 * flipped(zp), 0.5 * (block(pq) + flipped(pq)),
                ],
                axis=1,
            ),
        ],
        axis=0,
    )
    work = jnp.concatenate([work, unit, jnp.zeros((24, LANES - 72), f32)], axis=1)
    row_ids = lax.broadcasted_iota(jnp.int32, (24, 1), 0)
    ritz = None
    for k in range(24):
        if k == 8:
            ritz = work[8:16, 48:56]
        if k < 23:
            pivot_row = work[k : k + 1, :] / work[k : k + 1, k : k + 1]
            factor = jnp.where(row_ids > k, work[:, k : k + 1], 0.0)
            work = work - factor * pivot_row
    diagonal = jnp.sum(work[:, 0:24] * unit, axis=1, keepdims=True)
    scale = lax.rsqrt(diagonal)
    scaled = work * scale
    reduced[...] = times_transpose(scaled[:, 24:48], scaled[:, 48:72], highest)
    r = y_ref[...]
    s = z_ref[...]
    for j in range(8):
        r = r + ritz[:, j : j + 1] * x_ref[j : j + 1, :]
        s = s + ritz[:, j : j + 1] * y_ref[j : j + 1, :]
    residual[...] = r
    residual_image[...] = s


def local(tile_values, tile_row, tile_col, counts, diagonal, current, previous, previous_image, *, sizes):
    n_row, n_col = sizes
    slots, side = tile_values.shape[2], tile_values.shape[-1]
    width = current.shape[1]
    tiles = width // side
    paired = n_col == 2
    blocks = pltpu.with_memory_space_constraint(
        tile_values.reshape(slots, side, side), pltpu.VMEM
    )
    rows_here = tile_row.reshape(slots)
    cols_here = tile_col.reshape(slots)
    live = counts.reshape(1)
    here = lax.axis_index("col").reshape(1).astype(jnp.int32)
    diagonal = diagonal.reshape(1, width)

    def to_rows(values):
        return lax.all_to_all(values, "row", 0, 0, tiled=True)

    def from_columns(values):
        if paired:
            return lax.ppermute(values, "col", [(0, 1), (1, 0)])
        return lax.all_gather(values, "col", axis=0)

    def sums_to_columns(values):
        if paired:
            return lax.ppermute(values, "col", [(0, 1), (1, 0)])
        return lax.all_to_all(values, "col", 0, 0, tiled=True)

    send_shape = shape(tiles, 8, side) if paired else shape(n_col, tiles, 8, side)
    row_tiles = n_col * tiles
    column_tiles = n_row * tiles

    spread, pair_own = call(
        spread_kernel,
        "spread_vectors",
        [shape(n_row, tiles, 16, side), shape(tiles, 16, side)],
        [current, previous],
        [in_vmem] * 2,
    )
    pair_other = from_columns(pair_own)
    gathered = to_rows(spread).reshape(column_tiles, 16, side)
    keep, send, previous_sum, column_sum = call(
        functools.partial(first_kernel, paired),
        "apply_to_current",
        [shape(tiles, 8, side), send_shape, shape(row_tiles, 8, side), shape(column_tiles, 8, side)],
        [live, rows_here, cols_here, here, blocks, gathered, pair_own, pair_other],
        [in_smem] * 4 + [in_vmem] * 4,
        [
            pltpu.VMEM((column_tiles, 32, side), bf16),
            pltpu.VMEM((row_tiles, 16, side), f32),
            pltpu.VMEM((row_tiles, 16, side), bf16),
            pltpu.VMEM((row_tiles, 8, side), f32),
        ],
    )
    received = sums_to_columns(send)
    parts = to_rows(column_sum.reshape(n_row, tiles, 8, side))
    image, own, spread = call(
        functools.partial(image_kernel, paired),
        "sum_image",
        [shape(8, width), shape(tiles, 8, side), shape(n_row, tiles, 8, side)],
        [diagonal, current, keep, received, parts],
        [in_vmem] * 5,
    )
    other = from_columns(own)
    gathered = to_rows(spread).reshape(column_tiles, 8, side)
    keep, send, payload = call(
        functools.partial(second_kernel, paired),
        "apply_to_image",
        [shape(tiles, 8, side), send_shape, shape(n_row, tiles + 1, 8, side)],
        [
            live, rows_here, cols_here, here, blocks, gathered, own, other, pair_own, pair_other,
            previous_sum, diagonal, current, image, previous, previous_image,
        ],
        [in_smem] * 4 + [in_vmem] * 12,
        [
            pltpu.VMEM((column_tiles, 16, side), bf16),
            pltpu.VMEM((row_tiles, 8, side), f32),
            pltpu.VMEM((row_tiles, 16, side), f32),
            pltpu.VMEM((row_tiles, 16, side), bf16),
            pltpu.VMEM((row_tiles, 8, side), f32),
            pltpu.VMEM((column_tiles, 8, side), f32),
        ],
    )
    received = sums_to_columns(send)
    parts = to_rows(payload)
    twice, gram = call(
        functools.partial(gather_sum_kernel, paired),
        "sum_second_image",
        [shape(8, width), shape(8, LANES)],
        [diagonal, image, keep, received, parts],
        [in_vmem] * 5,
    )
    if paired:
        theirs = lax.ppermute(gram, "col", [(0, 1), (1, 0)])
    else:
        theirs = lax.psum(gram, "col") - gram
    residual, residual_image, reduced = call(
        finish_kernel,
        "finish",
        [shape(8, width), shape(8, width), shape(24, 24)],
        [current, image, twice, gram, theirs],
        [in_vmem] * 5,
    )
    return (image, residual, residual_image, reduced)


def solution(mesh):
    return jax.shard_map(
        functools.partial(local, sizes=(mesh.shape["row"], mesh.shape["col"])),
        mesh=mesh,
        in_specs=(
            P("row", "col", None, None, None),
            P("row", "col", None),
            P("row", "col", None),
            P("row", "col"),
            P(("row", "col")),
            P(None, ("row", "col")),
            P(None, ("row", "col")),
            P(None, ("row", "col")),
        ),
        out_specs=(P(None, ("row", "col")), P(None, ("row", "col")), P(None, ("row", "col")), P()),
        check_vma=False,
    )
```

```python
import functools
import math

import jax
import jax.numpy as jnp
from jax import lax
from jax.experimental import pallas as pl
from jax.experimental.pallas import tpu as pltpu
from jax.sharding import PartitionSpec as P

f32 = jnp.float32
bf16 = jnp.bfloat16
highest = lax.Precision.HIGHEST
LANES = 128
in_vmem = pl.BlockSpec(memory_space=pltpu.VMEM)
in_smem = pl.BlockSpec(memory_space=pltpu.SMEM)
in_hbm = pl.BlockSpec(memory_space=pltpu.HBM)
params = pltpu.CompilerParams(vmem_limit_bytes=32 * 2**20)


def call(kernel, name, out_shape, operands, specs, scratch=()):
    return pl.pallas_call(
        kernel,
        out_shape=out_shape,
        in_specs=specs,
        out_specs=jax.tree.map(lambda _: in_vmem, out_shape),
        scratch_shapes=scratch,
        compiler_params=params,
        name=name,
    )(*operands)


def shape(*dims, dtype=f32):
    return jax.ShapeDtypeStruct(dims, dtype)


def halves(values):
    high = values.astype(bf16)
    return high, (values - high.astype(f32)).astype(bf16)


def stacked_halves(values):
    return jnp.concatenate(halves(values), axis=0)


def times_transpose(left, right, precision=None):
    return lax.dot_general(
        left, right, (((1,), (1,)), ((), ())), preferred_element_type=f32, precision=precision
    )


def times(left, right, precision=None):
    return lax.dot_general(
        left, right, (((1,), (0,)), ((), ())), preferred_element_type=f32, precision=precision
    )


def lanes(t):
    return slice(t * LANES, (t + 1) * LANES)


def balanced_sum(terms):
    while len(terms) > 1:
        terms = [sum(terms[n : n + 2]) for n in range(0, len(terms), 2)]
    return terms[0]


def row_block_tiles(t, own, other, paired):
    if paired:
        return [(0, own[:, lanes(t)]), (1, other[:, lanes(t)])]
    return [(c, other[c, :, lanes(t)]) for c in range(other.shape[0])]


class Places:
    def __init__(self, ref, slots, row_tiles, column_tiles, paired):
        self.ref, self.slots, self.live, self.here = ref, slots, ref[0], ref[1]
        self.row_tiles, self.column_tiles = row_tiles, column_tiles
        self.row_shift = ref[1] * (row_tiles // 2) if paired else 0
        self.column_shift = ref[2] * (column_tiles // 2)

    def row(self, slot):
        return lax.rem(self.ref[3 + slot] + self.row_shift, self.row_tiles)

    def column(self, slot):
        return lax.rem(self.ref[3 + self.slots + slot] + self.column_shift, self.column_tiles)

    def weight(self, slot):
        return jnp.where(slot < self.live, 1.0, 0.0).astype(f32)


def group_of(slots):
    return math.gcd(slots, 16)


class Stream:
    def __init__(self, places, blocks, staged, semaphores):
        self.places, self.blocks, self.staged, self.semaphores = places, blocks, staged, semaphores
        self.group = group_of(blocks.shape[0])

    def copy(self, index):
        part = pl.ds(index * self.group, self.group)
        return pltpu.make_async_copy(
            self.blocks.at[part], self.staged.at[part], self.semaphores.at[index]
        )

    def start(self):
        for index in range(self.blocks.shape[0] // self.group):
            @pl.when(index * self.group < self.places.live)
            def _(index=index):
                self.copy(index).start()

    def loop(self, visit):
        def step(index, _):
            self.copy(index).wait()
            visit([index * self.group + s for s in range(self.group)])
            return 0

        lax.fori_loop(0, (self.places.live + self.group - 1) // self.group, step, 0)


def stream_scratch(slots, side):
    return [
        pltpu.VMEM((slots, side, side), f32),
        pltpu.SemaphoreType.DMA((slots // group_of(slots),)),
    ]


def visit_transposed(slots, places, tile, row_halves, column_sum):
    count = column_sum.shape[1]
    products = []
    for slot in slots:
        u = row_halves[places.row(slot)]
        pair = tile(slot)
        both = jnp.concatenate([pair[:, :LANES], pair[:, LANES:]], axis=0)
        product = times(jnp.concatenate([u, u], axis=1), both)
        products.append((product[:count] + product[count:]) * places.weight(slot))
    for slot, product in zip(slots, products):
        column_sum[places.column(slot)] += product


def visit_direct(slots, places, tile, column_halves, row_sum):
    products = []
    for slot in slots:
        x = column_halves[places.column(slot)]
        product = times_transpose(jnp.concatenate([x, x], axis=1), tile(slot))
        products.append((product[:8] + product[8:]) * places.weight(slot))
    for slot, product in zip(slots, products):
        row_sum[places.row(slot)] += product


def tile_from(staged):
    return lambda slot: jnp.concatenate(halves(staged[slot]), axis=1)


def loop_held(places, held, visit):
    group = group_of(held.shape[0])

    def step(index, _):
        visit([index * group + s for s in range(group)])
        return 0

    lax.fori_loop(0, (places.live + group - 1) // group, step, 0)


def transposed_current_kernel(
    paired, places, blocks, own, other, column_sum, held, staged, semaphores, row_halves
):
    places = Places(places, blocks.shape[0], row_halves.shape[0], column_sum.shape[0], paired)
    stream = Stream(places, blocks, staged, semaphores)
    stream.start()
    tiles = own.shape[-1] // LANES
    for t in range(tiles):
        for c, values in row_block_tiles(t, own, other, paired):
            row_halves[c * tiles + t] = stacked_halves(values)
    column_sum[...] = jnp.zeros_like(column_sum)

    def split(slot):
        pair = jnp.concatenate(halves(staged[slot]), axis=1)
        held[slot] = pair
        return pair

    stream.loop(lambda slots: visit_transposed(slots, places, split, row_halves, column_sum))


def assemble_kernel(own, partner, column_sum, payload):
    tiles = own.shape[-1] // LANES
    near = payload.shape[0]
    for n in range(near):
        for t in range(tiles):
            payload[n, t] = own[:, lanes(t)]
            payload[n, tiles + t] = partner[:, lanes(t)]
            payload[n, 2 * tiles + t] = column_sum[n * tiles + t]
            payload[n, 3 * tiles + t] = column_sum[(near + n) * tiles + t]


def assemble_image_kernel(own, partner, column_sum, payload):
    tiles = own.shape[0] - 1
    near = payload.shape[0]
    gram = own[tiles] + partner[tiles]
    for n in range(near):
        for t in range(tiles):
            payload[n, t] = own[t]
            payload[n, tiles + t] = partner[t]
            payload[n, 2 * tiles + t] = column_sum[n * tiles + t, 0:8]
            payload[n, 3 * tiles + t] = column_sum[(near + n) * tiles + t, 0:8]
        payload[n, 4 * tiles] = gram


def partner_sums_kernel(parts, previous, sums):
    near = parts.shape[0]
    tiles = parts.shape[1] // 4
    for t in range(tiles):
        sums[t] = balanced_sum([parts[n, 3 * tiles + t] for n in range(near)])
        sums[tiles + t] = previous[:, lanes(t)]


def fill_column_set(column_halves, parts):
    near = parts.shape[0]
    tiles = parts.shape[1] // 4
    for n in range(near):
        for t in range(tiles):
            column_halves[n * tiles + t] = stacked_halves(parts[n, t])
            column_halves[(near + n) * tiles + t] = stacked_halves(parts[n, tiles + t])


def direct_held_kernel(paired, places, held, parts, row_sum, column_halves):
    places = Places(places, held.shape[0], row_sum.shape[0], column_halves.shape[0], paired)
    fill_column_set(column_halves, parts)
    row_sum[...] = jnp.zeros_like(row_sum)
    loop_held(
        places,
        held,
        lambda slots: visit_direct(slots, places, lambda slot: held[slot], column_halves, row_sum),
    )


def direct_kernel(paired, places, blocks, parts, row_sum, staged, semaphores, column_halves):
    places = Places(places, blocks.shape[0], row_sum.shape[0], column_halves.shape[0], paired)
    stream = Stream(places, blocks, staged, semaphores)
    stream.start()
    fill_column_set(column_halves, parts)
    row_sum[...] = jnp.zeros_like(row_sum)
    stream.loop(
        lambda slots: visit_direct(slots, places, tile_from(staged), column_halves, row_sum)
    )


def combine_kernel(paired, parts, received, row_sum, diagonal, vectors, previous, both, *rows):
    near = parts.shape[0]
    tiles = parts.shape[1] // 4
    for t in range(tiles):
        total = (
            diagonal[:, lanes(t)] * vectors[:, lanes(t)]
            + received[t]
            + balanced_sum([parts[n, 2 * tiles + t] for n in range(near)])
        )
        if paired:
            both[:, lanes(t)] = total + row_sum[t]
            both[:, lanes(tiles + t)] = row_sum[tiles + t]
            both[:, lanes(2 * tiles + t)] = previous[:, lanes(t)]
        else:
            both[:, lanes(t)] = total
            for c in range(rows[0].shape[0]):
                rows[0][c, :, lanes(t)] = row_sum[c * tiles + t]


def image_kernel(paired, mine, theirs, x_ref, p_ref, q_ref, own, other, ship):
    width = x_ref.shape[-1]
    if paired:
        y = mine[:, :width] + theirs[:, width : 2 * width]
        other[...] = theirs[:, :width] + mine[:, width : 2 * width]
    else:
        y = mine[...] + theirs[...]
        other[...] = jnp.zeros_like(other)
    own[...] = y
    x, p, q = x_ref[...], p_ref[...], q_ref[...]
    outer = times_transpose(
        jnp.concatenate([x, y, p], axis=0), jnp.concatenate([x, y, p, q], axis=0), highest
    )
    tiles = width // LANES
    for t in range(tiles):
        ship[t] = y[:, lanes(t)]
    ship[tiles] = jnp.concatenate(
        [
            outer[0:8, 0:24],
            outer[0:8, 24:32] + outer[8:16, 16:24],
            outer[8:16, 8:32],
            outer[16:24, 16:32],
            jnp.zeros((8, LANES - 72), f32),
        ],
        axis=1,
    )


def transposed_image_kernel(
    paired, places, held, own, other, p_ref, p_other, column_sum, sum_halves, row_halves
):
    places = Places(places, held.shape[0], row_halves.shape[0], column_sum.shape[0], paired)
    width = own.shape[-1]
    tiles = width // LANES
    if paired:
        p_other = p_other[:, 2 * width :]
    for t in range(tiles):
        for (c, values), (_, previous) in zip(
            row_block_tiles(t, own, other, paired), row_block_tiles(t, p_ref, p_other, paired)
        ):
            row_halves[c * tiles + t] = stacked_halves(jnp.concatenate([values, previous], axis=0))
    column_sum[...] = jnp.zeros_like(column_sum)
    loop_held(
        places,
        held,
        lambda slots: visit_transposed(
            slots, places, lambda slot: held[slot], row_halves, column_sum
        ),
    )
    for j in range(column_sum.shape[0]):
        sum_halves[j] = stacked_halves(column_sum[j])


def inner_kernel(parts, sum_halves, diagonal, y_ref, p_ref, received, spread, sums, gram):
    near = parts.shape[0]
    tiles = y_ref.shape[-1] // LANES
    column_set = [
        stacked_halves(parts[n, first + t])
        for first in (0, tiles)
        for n in range(near)
        for t in range(tiles)
    ]
    cross = times_transpose(
        jnp.concatenate(column_set, axis=1),
        jnp.concatenate([sum_halves[j] for j in range(sum_halves.shape[0])], axis=1),
    )
    stored = cross[0:8, 0:16] + cross[8:16, 0:16] + cross[0:8, 16:32]
    scaled = diagonal[...] * y_ref[...]

    def summed(tile):
        return balanced_sum([parts[n, tile] for n in range(near)])

    for_partner = [summed(3 * tiles + t) for t in range(tiles)]
    for t in range(tiles):
        sums[t] = for_partner[t]
    gram[...] = summed(4 * tiles)
    for_own = jnp.concatenate([summed(2 * tiles + t) for t in range(tiles)], axis=1)
    yz = times_transpose(scaled, 0.5 * y_ref[...], highest)
    zp = times_transpose(
        jnp.concatenate([scaled + for_own, *for_partner], axis=1),
        jnp.concatenate([p_ref[...]] + [received[tiles + t] for t in range(tiles)], axis=1),
        highest,
    )
    total = stored + jnp.concatenate([yz, zp], axis=1)
    total = jnp.concatenate([total, jnp.zeros((8, LANES - 16), f32)], axis=1)
    for n in range(spread.shape[0]):
        spread[n] = total


def eliminate_kernel(mine, theirs, ritz, inverse, pencil):
    gram = mine[...] + theirs[...]
    turned = gram.T

    def block(n):
        return gram[:, 8 * n : 8 * n + 8]

    def flipped(n):
        return turned[8 * n : 8 * n + 8, :]

    xx, xy, xp, mixed, yy, yp, yq, pp, pq = range(9)
    nothing = jnp.zeros((8, 8), f32)
    unit = (
        lax.broadcasted_iota(jnp.int32, (24, 24), 0) == lax.broadcasted_iota(jnp.int32, (24, 24), 1)
    ).astype(f32)
    work = jnp.concatenate(
        [
            gram[:, 0:24],
            jnp.concatenate([flipped(xy), block(yy), block(yp)], axis=1),
            jnp.concatenate([flipped(xp), flipped(yp), block(pp)], axis=1),
        ],
        axis=0,
    )
    work = jnp.concatenate([work, unit, jnp.zeros((24, LANES - 48), f32)], axis=1)
    pencil[...] = 0.5 * jnp.concatenate(
        [
            jnp.concatenate([block(xy) + flipped(xy), 2.0 * block(yy), block(mixed)], axis=1),
            jnp.concatenate([2.0 * block(yy), nothing, block(yq)], axis=1),
            jnp.concatenate([flipped(mixed), flipped(yq), block(pq) + flipped(pq)], axis=1),
        ],
        axis=0,
    )
    row_ids = lax.broadcasted_iota(jnp.int32, (24, 1), 0)
    for k in range(23):
        if k == 8:
            ritz[...] = work[8:16, 24:32]
        pivot_row = work[k : k + 1, :] / work[k : k + 1, k : k + 1]
        factor = jnp.where(row_ids > k, work[:, k : k + 1], 0.0)
        work = work - factor * pivot_row
    inverse[...] = work[:, 24:48] * lax.rsqrt(jnp.sum(work[:, 0:24] * unit, axis=1, keepdims=True))


def residual_kernel(paired, ritz, x_ref, y_ref, mine, theirs, image, residual, residual_image):
    width = x_ref.shape[-1]
    r = y_ref[...]
    image[...] = r
    s = mine[:, :width] + (theirs[:, width : 2 * width] if paired else theirs[...])
    for j in range(8):
        factor = ritz[:, j : j + 1]
        r = r + factor * x_ref[j : j + 1, :]
        s = s + factor * y_ref[j : j + 1, :]
    residual[...] = r
    residual_image[...] = s


def reduce_kernel(inverse, pencil, parts, reduced):
    total = balanced_sum([parts[n] for n in range(parts.shape[0])])
    turned = total.T
    yz = total[:, 0:8] + turned[0:8, :]
    zp = 0.5 * total[:, 8:16]
    pz = 0.5 * turned[8:16, :]
    nothing = jnp.zeros((8, 8), f32)
    full = pencil[...] + jnp.concatenate(
        [
            jnp.zeros((8, 24), f32),
            jnp.concatenate([nothing, yz, zp], axis=1),
            jnp.concatenate([nothing, pz, nothing], axis=1),
        ],
        axis=0,
    )
    lower = inverse[...]
    reduced[...] = times_transpose(times(lower, full, highest), lower, highest)


def local(tile_values, tile_row, tile_col, counts, diagonal, current, previous, previous_image, *, sizes):
    near, n_col = sizes
    slots, side = tile_values.shape[2], tile_values.shape[-1]
    width = current.shape[1]
    tiles = width // side
    paired = n_col == 2
    row_tiles = n_col * tiles
    column_tiles = 2 * near * tiles
    blocks = pltpu.with_memory_space_constraint(
        tile_values.reshape(slots, side, side), pltpu.HBM
    )
    places = jnp.concatenate(
        [
            counts.reshape(1),
            lax.axis_index("col").reshape(1).astype(jnp.int32),
            lax.axis_index("half").reshape(1).astype(jnp.int32),
            tile_row.reshape(slots),
            tile_col.reshape(slots),
        ]
    )
    diagonal = diagonal.reshape(1, width)

    def swap(values, axis="col"):
        return lax.ppermute(values, axis, [(0, 1), (1, 0)])

    def to_partner(values):
        return swap(values, "half")

    def to_near(values):
        return lax.all_to_all(values, "near", 0, 0, tiled=True)

    def from_columns(values):
        return swap(values) if paired else lax.all_gather(values, "col", axis=0)

    def row_sums_shared(parts, received, row_sum, vectors):
        operands = [parts, received, row_sum, diagonal, vectors, previous]
        specs = [in_vmem] * 6
        kernel = functools.partial(combine_kernel, paired)
        if paired:
            mine = call(kernel, "combine", shape(8, 3 * width), operands, specs)
            return mine, swap(mine)
        mine, rows = call(
            kernel, "combine", [shape(8, width), shape(n_col, 8, width)], operands, specs
        )
        return mine, jnp.sum(lax.all_to_all(rows, "col", 0, 0, tiled=True), axis=0)

    other = from_columns(current)
    partner = to_partner(current)
    column_sum, held = call(
        functools.partial(transposed_current_kernel, paired),
        "transposed_current",
        [shape(column_tiles, 8, side), shape(slots, side, 2 * side, dtype=bf16)],
        [places, blocks, current, other],
        [in_smem, in_hbm] + [in_vmem] * 2,
        stream_scratch(slots, side) + [pltpu.VMEM((row_tiles, 16, side), bf16)],
    )
    payload = call(
        assemble_kernel,
        "assemble_current",
        shape(near, 4 * tiles, 8, side),
        [current, partner, column_sum],
        [in_vmem] * 3,
    )
    parts = to_near(payload)
    sums = call(
        partner_sums_kernel, "partner_sums", shape(2 * tiles, 8, side), [parts, previous], [in_vmem] * 2
    )
    received = to_partner(sums)
    row_sum = call(
        functools.partial(direct_held_kernel, paired),
        "direct_current",
        shape(row_tiles, 8, side),
        [places, held, parts],
        [in_smem] + [in_vmem] * 2,
        [pltpu.VMEM((column_tiles, 16, side), bf16)],
    )
    mine, theirs = row_sums_shared(parts, received, row_sum, current)
    own, other, ship = call(
        functools.partial(image_kernel, paired),
        "image",
        [shape(8, width), shape(8, width), shape(tiles + 1, 8, side)],
        [mine, theirs, current, previous, previous_image],
        [in_vmem] * 5,
    )
    previous_other = theirs
    if not paired:
        other = lax.all_gather(own, "col", axis=0)
        previous_other = lax.all_gather(previous, "col", axis=0)
    partner_ship = to_partner(ship)
    column_sum, sum_halves = call(
        functools.partial(transposed_image_kernel, paired),
        "transposed_image",
        [shape(column_tiles, 16, side), shape(column_tiles, 32, side, dtype=bf16)],
        [places, held, own, other, previous, previous_other],
        [in_smem] + [in_vmem] * 5,
        [pltpu.VMEM((row_tiles, 32, side), bf16)],
    )
    payload = call(
        assemble_image_kernel,
        "assemble_image",
        shape(near, 4 * tiles + 1, 8, side),
        [ship, partner_ship, column_sum],
        [in_vmem] * 3,
    )
    parts = to_near(payload)
    spread, sums, gram = call(
        inner_kernel,
        "inner_products",
        [shape(2 * near * n_col, 8, LANES), shape(tiles, 8, side), shape(8, LANES)],
        [parts, sum_halves, diagonal, own, previous, received],
        [in_vmem] * 6,
    )
    inner_parts = lax.all_to_all(spread, ("half", "near", "col"), 0, 0, tiled=True)
    received = to_partner(sums)
    their_gram = swap(gram) if paired else lax.psum(gram, "col") - gram
    row_sum = call(
        functools.partial(direct_kernel, paired),
        "direct_image",
        shape(row_tiles, 8, side),
        [places, blocks, parts],
        [in_smem, in_hbm, in_vmem],
        stream_scratch(slots, side) + [pltpu.VMEM((column_tiles, 16, side), bf16)],
    )
    ritz, inverse, pencil = call(
        eliminate_kernel,
        "eliminate",
        [shape(8, 8), shape(24, 24), shape(24, 24)],
        [gram, their_gram],
        [in_vmem] * 2,
    )
    mine, theirs = row_sums_shared(parts, received, row_sum, own)
    image, residual, residual_image = call(
        functools.partial(residual_kernel, paired),
        "residuals",
        [shape(8, width)] * 3,
        [ritz, current, own, mine, theirs],
        [in_vmem] * 5,
    )
    reduced = call(
        reduce_kernel, "reduce", shape(24, 24), [inverse, pencil, inner_parts], [in_vmem] * 3
    )
    return (image, residual, residual_image, reduced)


def solution(mesh):
    n_row, n_col = mesh.shape["row"], mesh.shape["col"]
    near = n_row // 2
    cut = jax.sharding.Mesh(mesh.devices.reshape(2, near, n_col), ("half", "near", "col"))
    row = ("half", "near")
    vectors = P(None, ("half", "near", "col"))
    return jax.shard_map(
        functools.partial(local, sizes=(near, n_col)),
        mesh=cut,
        in_specs=(
            P(row, "col", None, None, None),
            P(row, "col", None),
            P(row, "col", None),
            P(row, "col"),
            P(("half", "near", "col")),
            vectors,
            vectors,
            vectors,
        ),
        out_specs=(vectors, vectors, vectors, P()),
        check_vma=False,
    )
```

```python
import functools
import math

import jax
import jax.numpy as jnp
from jax import lax
from jax.experimental import pallas as pl
from jax.experimental.pallas import tpu as pltpu
from jax.sharding import PartitionSpec as P

f32 = jnp.float32
bf16 = jnp.bfloat16
highest = lax.Precision.HIGHEST
LANES = 128
in_vmem = pl.BlockSpec(memory_space=pltpu.VMEM)
in_smem = pl.BlockSpec(memory_space=pltpu.SMEM)
in_hbm = pl.BlockSpec(memory_space=pltpu.HBM)
params = pltpu.CompilerParams(vmem_limit_bytes=32 * 2**20)


def cost_of(micros):
    return pl.CostEstimate(flops=0, bytes_accessed=1, transcendentals=0)


def call(kernel, name, out_shape, operands, specs, scratch=(), micros=0.1):
    return pl.pallas_call(
        kernel,
        out_shape=out_shape,
        in_specs=specs,
        out_specs=jax.tree.map(
            lambda out: in_vmem if isinstance(out, jax.ShapeDtypeStruct) else in_smem, out_shape
        ),
        scratch_shapes=scratch,
        compiler_params=params,
        cost_estimate=cost_of(micros),
        name=name,
    )(*operands)


def kept_in_hbm(values):
    return pltpu.with_memory_space_constraint(values, pltpu.HBM)


def shape(*dims, dtype=f32):
    return jax.ShapeDtypeStruct(dims, dtype)


def halves(values):
    high = values.astype(bf16)
    return high, (values - high.astype(f32)).astype(bf16)


def stacked_halves(values):
    return jnp.concatenate(halves(values), axis=0)


def times_transpose(left, right, precision=None):
    return lax.dot_general(
        left, right, (((1,), (1,)), ((), ())), preferred_element_type=f32, precision=precision
    )


def times(left, right, precision=None):
    return lax.dot_general(
        left, right, (((1,), (0,)), ((), ())), preferred_element_type=f32, precision=precision
    )


def lanes(t):
    return slice(t * LANES, (t + 1) * LANES)


def balanced_sum(terms):
    while len(terms) > 1:
        terms = [sum(terms[n : n + 2]) for n in range(0, len(terms), 2)]
    return terms[0]


def row_block_tiles(t, own, other, paired):
    if paired:
        return [(0, own[:, lanes(t)]), (1, other[:, lanes(t)])]
    return [(c, other[c, :, lanes(t)]) for c in range(other.shape[0])]


class Places:
    def __init__(self, refs, slots, row_tiles, column_tiles, paired):
        counts, self.rows, self.columns = refs
        self.live = counts[0, 0]
        self.row_tiles, self.column_tiles = row_tiles, column_tiles
        self.row_shift = lax.axis_index("col") * (row_tiles // 2) if paired else 0
        self.column_shift = lax.axis_index("half") * (column_tiles // 2)

    def row(self, slot):
        return lax.rem(self.rows[0, 0, slot] + self.row_shift, self.row_tiles)

    def column(self, slot):
        return lax.rem(self.columns[0, 0, slot] + self.column_shift, self.column_tiles)

    def weight(self, slot):
        return jnp.where(slot < self.live, 1.0, 0.0).astype(f32)


def group_of(slots):
    return math.gcd(slots, 16)


class Stream:
    def __init__(self, blocks, staged, semaphores):
        self.blocks, self.staged, self.semaphores = blocks, staged, semaphores
        self.group = group_of(blocks.shape[0])
        for index in range(blocks.shape[0] // self.group):
            self.copy(index).start()

    def copy(self, index):
        part = pl.ds(index * self.group, self.group)
        return pltpu.make_async_copy(
            self.blocks.at[part], self.staged.at[part], self.semaphores.at[index]
        )

    def loop(self, live, visit):
        def step(index, _):
            self.copy(index).wait()
            visit([index * self.group + s for s in range(self.group)])
            return 0

        def leave(index, _):
            self.copy(index).wait()
            return 0

        groups = (live + self.group - 1) // self.group
        lax.fori_loop(0, groups, step, 0)
        lax.fori_loop(groups, self.blocks.shape[0] // self.group, leave, 0)


def stream_scratch(slots, side):
    return [
        pltpu.VMEM((slots, side, side), f32),
        pltpu.SemaphoreType.DMA((slots // group_of(slots),)),
    ]


def visit_transposed(slots, places, tile, row_halves, column_sum):
    count = column_sum.shape[1]
    products = []
    for slot in slots:
        u = row_halves[places.row(slot)]
        pair = tile(slot)
        both = jnp.concatenate([pair[:, :LANES], pair[:, LANES:]], axis=0)
        product = times(jnp.concatenate([u, u], axis=1), both)
        products.append((product[:count] + product[count:]) * places.weight(slot))
    for slot, product in zip(slots, products):
        column_sum[places.column(slot)] += product


def visit_direct(slots, places, tile, column_halves, row_sum):
    products = []
    for slot in slots:
        x = column_halves[places.column(slot)]
        product = times_transpose(jnp.concatenate([x, x], axis=1), tile(slot))
        products.append((product[:8] + product[8:]) * places.weight(slot))
    for slot, product in zip(slots, products):
        row_sum[places.row(slot)] += product


def tile_from(staged):
    return lambda slot: jnp.concatenate(halves(staged[slot]), axis=1)


def loop_held(places, held, visit):
    group = group_of(held.shape[0])

    def step(index, _):
        visit([index * group + s for s in range(group)])
        return 0

    lax.fori_loop(0, (places.live + group - 1) // group, step, 0)


def transposed_current_kernel(
    paired, *refs
):
    counts, rows, columns, blocks, x_ref, other, *refs = refs
    rows_held, columns_held, column_sum, held, own, semaphore, staged, semaphores, row_halves = refs
    copies = [
        pltpu.make_async_copy(source, target, semaphore.at[n])
        for n, (source, target) in enumerate(
            [(rows, rows_held), (columns, columns_held), (x_ref, own)]
        )
    ]
    for copy in copies:
        copy.start()
    stream = Stream(blocks, staged, semaphores)
    for copy in copies:
        copy.wait()
    refs = counts, rows_held, columns_held
    places = Places(refs, blocks.shape[0], row_halves.shape[0], column_sum.shape[0], paired)
    tiles = own.shape[-1] // LANES
    for t in range(tiles):
        for c, values in row_block_tiles(t, own, other, paired):
            row_halves[c * tiles + t] = stacked_halves(values)
    column_sum[...] = jnp.zeros_like(column_sum)

    def split(slot):
        pair = jnp.concatenate(halves(staged[slot]), axis=1)
        held[slot] = pair
        return pair

    stream.loop(places.live, lambda slots: visit_transposed(slots, places, split, row_halves, column_sum))


def assemble_kernel(own, partner, column_sum, payload):
    tiles = own.shape[-1] // LANES
    near = payload.shape[0]
    for n in range(near):
        for t in range(tiles):
            payload[n, t] = own[:, lanes(t)]
            payload[n, tiles + t] = partner[:, lanes(t)]
            payload[n, 2 * tiles + t] = column_sum[n * tiles + t]
            payload[n, 3 * tiles + t] = column_sum[(near + n) * tiles + t]


def assemble_image_kernel(own, partner, column_sum, payload):
    tiles = own.shape[0] - 1
    near = payload.shape[0]
    gram = own[tiles] + partner[tiles]
    for n in range(near):
        for t in range(tiles):
            payload[n, t] = own[t]
            payload[n, tiles + t] = partner[t]
            payload[n, 2 * tiles + t] = column_sum[n * tiles + t, 0:8]
            payload[n, 3 * tiles + t] = column_sum[(near + n) * tiles + t, 0:8]
        payload[n, 4 * tiles] = gram


def first_partner_sums_kernel(parts, previous, sums):
    near = parts.shape[0]
    tiles = parts.shape[1] // 4
    for t in range(tiles):
        sums[t] = balanced_sum([parts[n, 3 * tiles + t] for n in range(near)])
        sums[tiles + t] = previous[:, lanes(t)]
    for t in range(2 * tiles, sums.shape[0]):
        sums[t] = jnp.zeros_like(sums[t])


def partner_sums_kernel(parts, sums, gram):
    near = parts.shape[0]
    tiles = parts.shape[1] // 4
    for t in range(tiles):
        sums[t] = balanced_sum([parts[n, 3 * tiles + t] for n in range(near)])
    gram[...] = balanced_sum([parts[n, 4 * tiles] for n in range(near)])


def fill_column_set(column_halves, parts):
    near = parts.shape[0]
    tiles = parts.shape[1] // 4
    for n in range(near):
        for t in range(tiles):
            column_halves[n * tiles + t] = stacked_halves(parts[n, t])
            column_halves[(near + n) * tiles + t] = stacked_halves(parts[n, tiles + t])


def direct_held_kernel(paired, counts, rows, columns, held, parts, row_sum, column_halves):
    refs = counts, rows, columns
    places = Places(refs, held.shape[0], row_sum.shape[0], column_halves.shape[0], paired)
    fill_column_set(column_halves, parts)
    row_sum[...] = jnp.zeros_like(row_sum)
    loop_held(
        places,
        held,
        lambda slots: visit_direct(slots, places, lambda slot: held[slot], column_halves, row_sum),
    )


def direct_kernel(
    paired, counts, rows, columns, blocks, parts,
    row_sum, rest,
    staged, semaphores, column_halves,
):
    refs = counts, rows, columns
    places = Places(refs, blocks.shape[0], row_sum.shape[0], column_halves.shape[0], paired)
    stream = Stream(blocks, staged, semaphores)
    fill_column_set(column_halves, parts)
    row_sum[...] = jnp.zeros_like(row_sum)
    stream.loop(
        places.live, lambda slots: visit_direct(slots, places, tile_from(staged), column_halves, row_sum)
    )
    for t in range(rest.shape[0]):
        rest[t] = row_sum[row_sum.shape[0] - rest.shape[0] + t]


def half_result(t, parts, diagonal, vectors):
    near = parts.shape[0]
    tiles = parts.shape[1] // 4
    return diagonal[:, lanes(t)] * vectors[:, lanes(t)] + balanced_sum(
        [parts[n, 2 * tiles + t] for n in range(near)]
    )


def combine_kernel(paired, parts, row_sum, diagonal, vectors, previous, mine, rows):
    tiles = parts.shape[1] // 4
    for t in range(tiles):
        total = half_result(t, parts, diagonal, vectors)
        if paired:
            mine[:, lanes(t)] = total + row_sum[t]
            rows[:, lanes(t)] = row_sum[tiles + t]
            rows[:, lanes(tiles + t)] = previous[:, lanes(t)]
        else:
            mine[:, lanes(t)] = total
            for c in range(rows.shape[0]):
                rows[c, :, lanes(t)] = row_sum[c * tiles + t]


def base_kernel(mine, rows, their_mine, their_rows, own, other):
    width = own.shape[-1]
    own[...] = mine[...] + their_rows[:, :width]
    other[...] = their_mine[...] + rows[:, :width]


def image_kernel(base, received, x_ref, p_ref, q_ref, image, ship):
    tiles = image.shape[-1] // LANES
    y = base[...] + jnp.concatenate([received[t] for t in range(tiles)], axis=1)
    image[...] = y
    x, p, q = x_ref[...], p_ref[...], q_ref[...]
    outer = times_transpose(
        jnp.concatenate([x, y, p], axis=0), jnp.concatenate([x, y, p, q], axis=0), highest
    )
    for t in range(tiles):
        ship[t] = y[:, lanes(t)]
    ship[tiles] = jnp.concatenate(
        [
            outer[0:8, 0:24],
            outer[0:8, 24:32] + outer[8:16, 16:24],
            outer[8:16, 8:32],
            outer[16:24, 16:32],
            jnp.zeros((8, LANES - 72), f32),
        ],
        axis=1,
    )


def transposed_image_kernel(
    paired, counts, rows, columns, held, own, base_other, sums_other, p_ref, p_other,
    column_sum, sum_halves,
    row_halves,
):
    refs = counts, rows, columns
    places = Places(refs, held.shape[0], row_halves.shape[0], column_sum.shape[0], paired)
    width = own.shape[-1]
    tiles = width // LANES
    other = base_other
    if paired:
        other = base_other[...] + jnp.concatenate([sums_other[t] for t in range(tiles)], axis=1)
        p_other = p_other[:, width:]
    for t in range(tiles):
        for (c, values), (_, previous) in zip(
            row_block_tiles(t, own, other, paired), row_block_tiles(t, p_ref, p_other, paired)
        ):
            row_halves[c * tiles + t] = stacked_halves(jnp.concatenate([values, previous], axis=0))
    column_sum[...] = jnp.zeros_like(column_sum)
    loop_held(
        places,
        held,
        lambda slots: visit_transposed(
            slots, places, lambda slot: held[slot], row_halves, column_sum
        ),
    )
    for j in range(column_sum.shape[0]):
        sum_halves[j] = stacked_halves(column_sum[j])


def inner_kernel(parts, sum_halves, diagonal, y_ref, p_ref, for_partner, first_received, spread):
    near = parts.shape[0]
    tiles = y_ref.shape[-1] // LANES
    column_set = [
        stacked_halves(parts[n, first + t])
        for first in (0, tiles)
        for n in range(near)
        for t in range(tiles)
    ]
    cross = times_transpose(
        jnp.concatenate(column_set, axis=1),
        jnp.concatenate([sum_halves[j] for j in range(sum_halves.shape[0])], axis=1),
    )
    stored = cross[0:8, 0:16] + cross[8:16, 0:16] + cross[0:8, 16:32]
    scaled = diagonal[...] * y_ref[...]
    halved = jnp.concatenate([half_result(t, parts, diagonal, y_ref) for t in range(tiles)], axis=1)
    yz = times_transpose(scaled, 0.5 * y_ref[...], highest)
    zp = times_transpose(
        jnp.concatenate([halved] + [for_partner[t] for t in range(tiles)], axis=1),
        jnp.concatenate([p_ref[...]] + [first_received[tiles + t] for t in range(tiles)], axis=1),
        highest,
    )
    total = stored + jnp.concatenate([yz, zp], axis=1)
    total = jnp.concatenate([total, jnp.zeros((8, LANES - 16), f32)], axis=1)
    for n in range(spread.shape[0]):
        spread[n] = total


def eliminate_kernel(mine, theirs, ritz, inverse, pencil):
    gram = mine[...] + theirs[...]
    turned = gram.T

    def block(n):
        return gram[:, 8 * n : 8 * n + 8]

    def flipped(n):
        return turned[8 * n : 8 * n + 8, :]

    xx, xy, xp, mixed, yy, yp, yq, pp, pq = range(9)
    nothing = jnp.zeros((8, 8), f32)
    unit = (
        lax.broadcasted_iota(jnp.int32, (24, 24), 0) == lax.broadcasted_iota(jnp.int32, (24, 24), 1)
    ).astype(f32)
    work = jnp.concatenate(
        [
            gram[:, 0:24],
            jnp.concatenate([flipped(xy), block(yy), block(yp)], axis=1),
            jnp.concatenate([flipped(xp), flipped(yp), block(pp)], axis=1),
        ],
        axis=0,
    )
    work = jnp.concatenate([work, unit, jnp.zeros((24, LANES - 48), f32)], axis=1)
    pencil[...] = 0.5 * jnp.concatenate(
        [
            jnp.concatenate([block(xy) + flipped(xy), 2.0 * block(yy), block(mixed)], axis=1),
            jnp.concatenate([2.0 * block(yy), nothing, block(yq)], axis=1),
            jnp.concatenate([flipped(mixed), flipped(yq), block(pq) + flipped(pq)], axis=1),
        ],
        axis=0,
    )
    row_ids = lax.broadcasted_iota(jnp.int32, (24, 1), 0)
    for k in range(0, 24, 2):
        if k == 8:
            ritz[...] = work[8:16, 24:32]
        row, next_row = work[k : k + 1, :], work[k + 1 : k + 2, :]
        column = jnp.broadcast_to(work[:, k : k + 1], work.shape)
        next_column = jnp.broadcast_to(work[:, k + 1 : k + 2], work.shape)
        first, cross, second = column[k : k + 1], column[k + 1 : k + 2], next_column[k + 1 : k + 2]
        scale = 1.0 / first
        next_scale = first / (first * second - cross * cross)
        ratio = cross * scale
        work = (
            work
            - jnp.where(row_ids > k, column, 0.0) * (row * scale)
            - jnp.where(row_ids > k + 1, next_column - column * ratio, 0.0)
            * ((next_row - ratio * row) * next_scale)
        )
    inverse[...] = work[:, 24:48] * lax.rsqrt(jnp.sum(work[:, 0:24] * unit, axis=1, keepdims=True))


def residual_kernel(
    paired, ritz, x_ref, y_ref, parts, received, row_sum, theirs, diagonal,
    image, residual, residual_image,
):
    image[...] = y_ref[...]
    for t in range(theirs.shape[0]):
        r = y_ref[:, lanes(t)]
        s = half_result(t, parts, diagonal, y_ref) + received[t] + theirs[t]
        if paired:
            s = s + row_sum[t]
        for j in range(8):
            factor = ritz[:, j : j + 1]
            r = r + factor * x_ref[j : j + 1, lanes(t)]
            s = s + factor * y_ref[j : j + 1, lanes(t)]
        residual[:, lanes(t)] = r
        residual_image[:, lanes(t)] = s


def reduce_kernel(inverse, pencil, parts, reduced):
    total = balanced_sum([parts[n] for n in range(parts.shape[0])])
    turned = total.T
    yz = total[:, 0:8] + turned[0:8, :]
    zp = 0.5 * total[:, 8:16]
    pz = 0.5 * turned[8:16, :]
    nothing = jnp.zeros((8, 8), f32)
    full = pencil[...] + jnp.concatenate(
        [
            jnp.zeros((8, 24), f32),
            jnp.concatenate([nothing, yz, zp], axis=1),
            jnp.concatenate([nothing, pz, nothing], axis=1),
        ],
        axis=0,
    )
    lower = inverse[...]
    reduced[...] = times_transpose(times(lower, full, highest), lower, highest)


def local(tile_values, tile_row, tile_col, counts, diagonal, current, previous, previous_image, *, sizes):
    near, n_col = sizes
    slots, side = tile_values.shape[2], tile_values.shape[-1]
    width = current.shape[1]
    tiles = width // side
    paired = n_col == 2
    row_tiles = n_col * tiles
    column_tiles = 2 * near * tiles
    blocks = kept_in_hbm(tile_values.reshape(slots, side, side))
    places = [counts, tile_row, tile_col]
    diagonal = diagonal.reshape(1, width)

    def swap(values, axis="col"):
        return lax.ppermute(values, axis, [(0, 1), (1, 0)])

    def to_partner(values):
        return swap(values, "half")

    def to_near(values):
        return lax.all_to_all(values, "near", 0, 0, tiled=True)

    def from_columns(values):
        return swap(values) if paired else lax.all_gather(values, "col", axis=0)

    other = from_columns(current)
    partner = to_partner(current)
    *held_places, column_sum, held = call(
        functools.partial(transposed_current_kernel, paired),
        "transposed_current",
        [pltpu.SMEM(part.shape, part.dtype) for part in places[1:]]
        + [shape(column_tiles, 8, side), shape(slots, side, 2 * side, dtype=bf16)],
        [counts, *map(kept_in_hbm, places[1:]), blocks, kept_in_hbm(current), other],
        [in_smem] + [in_hbm] * 4 + [in_vmem],
        [pltpu.VMEM((8, width), f32), pltpu.SemaphoreType.DMA((3,))]
        + stream_scratch(slots, side)
        + [pltpu.VMEM((row_tiles, 16, side), bf16)],
        micros=3.0,
    )
    places[1:] = [pltpu.with_memory_space_constraint(part, pltpu.SMEM) for part in held_places]
    payload = call(
        assemble_kernel,
        "assemble_current",
        shape(near, 4 * tiles, 8, side),
        [current, partner, column_sum],
        [in_vmem] * 3,
    )
    parts = to_near(payload)
    sums = call(
        first_partner_sums_kernel,
        "partner_sums",
        shape(2 * tiles + 1, 8, side),
        [parts, previous],
        [in_vmem] * 2,
    )
    first_received = to_partner(sums)
    row_sum = call(
        functools.partial(direct_held_kernel, paired),
        "direct_current",
        shape(row_tiles, 8, side),
        [*places, held, parts],
        [in_smem] * 3 + [in_vmem] * 2,
        [pltpu.VMEM((column_tiles, 16, side), bf16)],
        micros=2.2,
    )
    mine, rows = call(
        functools.partial(combine_kernel, paired),
        "combine",
        [shape(8, width), shape(8, 2 * width) if paired else shape(n_col, 8, width)],
        [parts, row_sum, diagonal, current, previous],
        [in_vmem] * 5,
    )
    if paired:
        previous_other = swap(rows)
        base, base_other = call(
            base_kernel,
            "base",
            [shape(8, width)] * 2,
            [mine, rows, swap(mine), previous_other],
            [in_vmem] * 4,
        )
        sums_other = swap(first_received[:tiles])
    else:
        base = mine + jnp.sum(lax.all_to_all(rows, "col", 0, 0, tiled=True), axis=0)
        sums_other = first_received
        previous_other = lax.all_gather(previous, "col", axis=0)
    image, ship = call(
        image_kernel,
        "image",
        [shape(8, width), shape(tiles + 1, 8, side)],
        [base, first_received, current, previous, previous_image],
        [in_vmem] * 5,
    )
    partner_ship = to_partner(ship)
    if not paired:
        base_other = lax.all_gather(image, "col", axis=0)
    column_sum, sum_halves = call(
        functools.partial(transposed_image_kernel, paired),
        "transposed_image",
        [shape(column_tiles, 16, side), shape(column_tiles, 32, side, dtype=bf16)],
        [*places, held, image, base_other, sums_other, previous, previous_other],
        [in_smem] * 3 + [in_vmem] * 6,
        [pltpu.VMEM((row_tiles, 32, side), bf16)],
        micros=1.8,
    )
    payload = call(
        assemble_image_kernel,
        "assemble_image",
        shape(near, 4 * tiles + 1, 8, side),
        [ship, partner_ship, column_sum],
        [in_vmem] * 3,
    )
    parts = to_near(payload)
    for_partner, gram = call(
        partner_sums_kernel,
        "partner_sums",
        [shape(tiles, 8, side), shape(8, LANES)],
        [parts],
        [in_vmem],
    )
    received = to_partner(for_partner)
    their_gram = swap(gram) if paired else lax.psum(gram, "col") - gram
    spread = call(
        inner_kernel,
        "inner_products",
        shape(2 * near * n_col, 8, LANES),
        [parts, sum_halves, diagonal, image, previous, for_partner, first_received],
        [in_vmem] * 7,
        micros=1.1,
    )
    inner_parts = lax.all_to_all(spread, ("half", "near", "col"), 0, 0, tiled=True)
    row_sum, rest = call(
        functools.partial(direct_kernel, paired),
        "direct_image",
        [shape(row_tiles, 8, side), shape(tiles if paired else row_tiles, 8, side)],
        [*places, blocks, parts],
        [in_smem] * 3 + [in_hbm, in_vmem],
        stream_scratch(slots, side) + [pltpu.VMEM((column_tiles, 16, side), bf16)],
        micros=3.4,
    )
    if paired:
        theirs = swap(rest)
    else:
        rest = rest.reshape(n_col, tiles, 8, side)
        theirs = jnp.sum(lax.all_to_all(rest, "col", 0, 0, tiled=True), axis=0)
    ritz, inverse, pencil = call(
        eliminate_kernel,
        "eliminate",
        [shape(8, 8), shape(24, 24), shape(24, 24)],
        [gram, their_gram],
        [in_vmem] * 2,
        micros=2.1,
    )
    image, residual, residual_image = call(
        functools.partial(residual_kernel, paired),
        "residuals",
        [shape(8, width)] * 3,
        [ritz, current, image, parts, received, row_sum, theirs, diagonal],
        [in_vmem] * 8,
        micros=0.7,
    )
    reduced = call(
        reduce_kernel,
        "reduce",
        shape(24, 24),
        [inverse, pencil, inner_parts],
        [in_vmem] * 3,
        micros=1.0,
    )
    return (image, residual, residual_image, reduced)


def solution(mesh):
    n_row, n_col = mesh.shape["row"], mesh.shape["col"]
    near = n_row // 2
    cut = jax.sharding.Mesh(mesh.devices.reshape(2, near, n_col), ("half", "near", "col"))
    row = ("half", "near")
    vectors = P(None, ("half", "near", "col"))
    return jax.shard_map(
        functools.partial(local, sizes=(near, n_col)),
        mesh=cut,
        in_specs=(
            P(row, "col", None, None, None),
            P(row, "col", None),
            P(row, "col", None),
            P(row, "col"),
            P(("half", "near", "col")),
            vectors,
            vectors,
            vectors,
        ),
        out_specs=(vectors, vectors, vectors, P()),
        check_vma=False,
    )
```

```python
import functools
import math

import jax
import jax.numpy as jnp
from jax import lax
from jax.experimental import pallas as pl
from jax.experimental.pallas import tpu as pltpu
from jax.sharding import PartitionSpec as P

f32 = jnp.float32
bf16 = jnp.bfloat16
highest = lax.Precision.HIGHEST
LANES = 128
in_vmem = pl.BlockSpec(memory_space=pltpu.VMEM)
in_smem = pl.BlockSpec(memory_space=pltpu.SMEM)
in_hbm = pl.BlockSpec(memory_space=pltpu.HBM)
params = pltpu.CompilerParams(vmem_limit_bytes=32 * 2**20)


def cost_of(micros):
    return pl.CostEstimate(flops=0, bytes_accessed=1, transcendentals=0)


def call(kernel, name, out_shape, operands, specs, scratch=(), micros=0.1):
    return pl.pallas_call(
        kernel,
        out_shape=out_shape,
        in_specs=specs,
        out_specs=jax.tree.map(
            lambda out: in_vmem if isinstance(out, jax.ShapeDtypeStruct) else in_smem, out_shape
        ),
        scratch_shapes=scratch,
        compiler_params=params,
        cost_estimate=cost_of(micros),
        name=name,
    )(*operands)


def kept_in_hbm(values):
    return pltpu.with_memory_space_constraint(values, pltpu.HBM)


def shape(*dims, dtype=f32):
    return jax.ShapeDtypeStruct(dims, dtype)


def halves(values):
    high = values.astype(bf16)
    return high, (values - high.astype(f32)).astype(bf16)


def stacked_halves(values):
    high = values.astype(bf16).astype(f32)
    return jnp.concatenate([high, values - high], axis=0).astype(bf16)


def times_transpose(left, right, precision=None):
    return lax.dot_general(
        left, right, (((1,), (1,)), ((), ())), preferred_element_type=f32, precision=precision
    )


def times(left, right, precision=None):
    return lax.dot_general(
        left, right, (((1,), (0,)), ((), ())), preferred_element_type=f32, precision=precision
    )


def lanes(t):
    return slice(t * LANES, (t + 1) * LANES)


def balanced_sum(terms):
    while len(terms) > 1:
        terms = [sum(terms[n : n + 2]) for n in range(0, len(terms), 2)]
    return terms[0]


def row_block_tiles(t, own, other, paired):
    if paired:
        return [(0, own[:, lanes(t)]), (1, other[:, lanes(t)])]
    return [(c, other[c, :, lanes(t)]) for c in range(other.shape[0])]


class Places:
    def __init__(self, refs, row_tiles, column_tiles, tiles, paired):
        counts, self.rows, self.columns = refs
        self.live = counts[0, 0]
        here = lax.axis_index("col")
        self.row_mask = here * tiles if paired else 0
        self.column_mask = lax.axis_index("half") * (column_tiles // 2) + lax.rem(here, 2) * (
            column_tiles // 4
        )

    def row(self, slot):
        return lax.bitwise_xor(self.rows[0, 0, slot], self.row_mask)

    def column(self, slot):
        return lax.bitwise_xor(self.columns[0, 0, slot], self.column_mask)

    def weight(self, slot):
        return jnp.where(slot < self.live, 1.0, 0.0).astype(f32)


def group_of(slots):
    return math.gcd(slots, 16)


class Stream:
    def __init__(self, blocks, staged, semaphores):
        self.blocks, self.staged, self.semaphores = blocks, staged, semaphores
        self.group = group_of(staged.shape[0])
        self.groups = staged.shape[0] // self.group
        for index in range(self.groups):
            self.copy(index).start()

    def copy(self, index):
        part = pl.ds(index * self.group, self.group)
        return pltpu.make_async_copy(
            self.blocks.at[part], self.staged.at[part], self.semaphores.at[index]
        )

    def loop(self, live, visit):
        def step(index, _):
            self.copy(index).wait()
            visit([index * self.group + s for s in range(self.group)])
            return 0

        def leave(index, _):
            self.copy(index).wait()
            return 0

        groups = jnp.minimum((live + self.group - 1) // self.group, self.groups)
        lax.fori_loop(0, groups, step, 0)
        lax.fori_loop(groups, self.groups, leave, 0)


def stream_scratch(slots, side):
    return [
        pltpu.VMEM((slots, side, side), f32),
        pltpu.SemaphoreType.DMA((slots // group_of(slots),)),
    ]


def visit_transposed(slots, places, tile, row_halves, column_sum):
    count = column_sum.shape[1]
    products = []
    for slot in slots:
        u = row_halves[places.row(slot)]
        pair = tile(slot)
        both = jnp.concatenate([pair[:, :LANES], pair[:, LANES:]], axis=0)
        product = times(jnp.concatenate([u, u], axis=1), both)
        products.append((product[:count] + product[count:]) * places.weight(slot))
    for slot, product in zip(slots, products):
        column_sum[places.column(slot)] += product


def visit_direct(slots, places, tile, column_halves, row_sum):
    products = []
    for slot in slots:
        x = column_halves[places.column(slot)]
        product = times_transpose(jnp.concatenate([x, x], axis=1), tile(slot))
        products.append((product[:8] + product[8:]) * places.weight(slot))
    for slot, product in zip(slots, products):
        row_sum[places.row(slot)] += product


def tile_from(staged):
    return lambda slot: jnp.concatenate(halves(staged[slot]), axis=1)


def loop_held(places, held, visit, first=0):
    group = math.gcd(held.shape[0], 32)

    def step(index, _):
        visit([first + index * group + s for s in range(group)])
        return 0

    lax.fori_loop(0, (jnp.maximum(places.live - first, 0) + group - 1) // group, step, 0)


def transposed_current_kernel(
    paired, *refs
):
    counts, rows, columns, blocks, x_ref, other, *refs = refs
    rows_held, columns_held, column_sum, held, own, semaphore, staged, semaphores, row_halves = refs
    copies = [
        pltpu.make_async_copy(source, target, semaphore.at[n])
        for n, (source, target) in enumerate(
            [(rows, rows_held), (columns, columns_held), (x_ref, own)]
        )
    ]
    for copy in copies:
        copy.start()
    stream = Stream(blocks, staged, semaphores)
    for copy in copies:
        copy.wait()
    refs = counts, rows_held, columns_held
    places = Places(refs, row_halves.shape[0], column_sum.shape[0], own.shape[-1] // LANES, paired)
    tiles = own.shape[-1] // LANES
    for t in range(tiles):
        for c, values in row_block_tiles(t, own, other, paired):
            row_halves[c * tiles + t] = stacked_halves(values)
    column_sum[...] = jnp.zeros_like(column_sum)

    def split(slot):
        pair = jnp.concatenate(halves(staged[slot]), axis=1)
        held[slot] = pair
        return pair

    stream.loop(places.live, lambda slots: visit_transposed(slots, places, split, row_halves, column_sum))


def assemble_kernel(own, partner, column_sum, payload):
    tiles = own.shape[-1] // LANES
    near = payload.shape[0]
    for n in range(near):
        for t in range(tiles):
            payload[n, t] = own[:, lanes(t)]
            payload[n, tiles + t] = partner[:, lanes(t)]
            payload[n, 2 * tiles + t] = column_sum[n * tiles + t]
            payload[n, 3 * tiles + t] = column_sum[(near + n) * tiles + t]


def assemble_image_kernel(
    own, base_partner, sums, received, column_sum, x_ref, x_partner, p_ref, payload, partner_image
):
    tiles = own.shape[-1] // LANES
    near = payload.shape[0]
    partner = [base_partner[t] + sums[t] for t in range(tiles)]
    basis = jnp.concatenate(
        [
            jnp.concatenate([x_ref[...], x_partner[...]], axis=1),
            jnp.concatenate([own[...]] + partner, axis=1),
            jnp.concatenate([p_ref[...]] + [received[tiles + t] for t in range(tiles)], axis=1),
        ],
        axis=0,
    )
    for t in range(tiles):
        partner_image[:, lanes(t)] = partner[t]
    outer = times_transpose(basis, basis, highest)
    gram = jnp.concatenate(
        [outer[0:8], outer[8:16, 8:24], outer[16:24, 16:24], jnp.zeros((8, LANES - 48), f32)], axis=1
    )
    for n in range(near):
        for t in range(tiles):
            payload[n, t] = own[:, lanes(t)]
            payload[n, tiles + t] = partner[t]
            payload[n, 2 * tiles + t] = column_sum[n * tiles + t, 0:8]
            payload[n, 3 * tiles + t] = column_sum[(near + n) * tiles + t, 0:8]
        payload[n, 4 * tiles] = gram


def first_partner_sums_kernel(parts, previous, sums):
    near = parts.shape[0]
    tiles = parts.shape[1] // 4
    for t in range(tiles):
        sums[t] = balanced_sum([parts[n, 3 * tiles + t] for n in range(near)])
        sums[tiles + t] = previous[:, lanes(t)]
    sums[2 * tiles] = jnp.zeros_like(sums[2 * tiles])


def partner_sums_kernel(parts, sums, gram):
    near = parts.shape[0]
    tiles = parts.shape[1] // 4
    for t in range(tiles):
        sums[t] = balanced_sum([parts[n, 3 * tiles + t] for n in range(near)])
    gram[...] = balanced_sum([parts[n, 4 * tiles] for n in range(near)])


def fill_column_set(column_halves, parts):
    near = parts.shape[0]
    tiles = parts.shape[1] // 4
    for n in range(near):
        for t in range(tiles):
            column_halves[n * tiles + t] = stacked_halves(parts[n, t])
            column_halves[(near + n) * tiles + t] = stacked_halves(parts[n, tiles + t])


def direct_held_kernel(paired, counts, rows, columns, held, parts, row_sum, column_halves):
    refs = counts, rows, columns
    places = Places(refs, row_sum.shape[0], column_halves.shape[0], parts.shape[1] // 4, paired)
    fill_column_set(column_halves, parts)
    row_sum[...] = jnp.zeros_like(row_sum)
    loop_held(
        places,
        held,
        lambda slots: visit_direct(slots, places, lambda slot: held[slot], column_halves, row_sum),
    )


def direct_kernel(
    paired, counts, rows, columns, blocks, parts, kept, mine, theirs,
    row_sum, rest, gram,
    staged, semaphores, column_halves,
):
    refs = counts, rows, columns
    places = Places(refs, row_sum.shape[0], column_halves.shape[0], parts.shape[1] // 4, paired)
    stream = Stream(blocks, staged, semaphores)
    gram[...] = mine[...] + theirs[...]
    fill_column_set(column_halves, parts)
    row_sum[...] = jnp.zeros_like(row_sum)
    first = staged.shape[0]
    loop_held(
        places,
        kept,
        lambda slots: visit_direct(
            slots, places, lambda slot: kept[slot - first], column_halves, row_sum
        ),
        first,
    )
    stream.loop(
        places.live,
        lambda slots: visit_direct(slots, places, tile_from(staged), column_halves, row_sum),
    )
    for t in range(rest.shape[0]):
        rest[t] = row_sum[row_sum.shape[0] - rest.shape[0] + t]


def half_result(t, parts, diagonal, vectors):
    near = parts.shape[0]
    tiles = parts.shape[1] // 4
    return diagonal[:, lanes(t)] * vectors[:, lanes(t)] + balanced_sum(
        [parts[n, 2 * tiles + t] for n in range(near)]
    )


def combine_kernel(paired, parts, row_sum, diagonal, vectors, mine, *rows):
    tiles = parts.shape[1] // 4
    for t in range(tiles):
        total = half_result(t, parts, diagonal, vectors)
        if paired:
            mine[t] = total + row_sum[t]
            mine[tiles + t] = row_sum[tiles + t]
        else:
            mine[:, lanes(t)] = total
            for c in range(rows[0].shape[0]):
                rows[0][c, :, lanes(t)] = row_sum[c * tiles + t]


def base_kernel(mine, theirs, own, other):
    tiles = own.shape[0] - 1
    for t in range(tiles):
        own[t] = mine[t] + theirs[tiles + t]
        other[:, lanes(t)] = theirs[t] + mine[tiles + t]
    own[tiles] = jnp.zeros_like(own[tiles])


def image_kernel(base, received, image):
    for t in range(image.shape[-1] // LANES):
        image[:, lanes(t)] = base[t] + received[t]


def transposed_image_kernel(
    paired, counts, rows, columns, held, own, base_other, sums_other, p_ref, p_other, diagonal,
    x_ref, q_ref,
    column_sum, sum_halves, late, kept,
    row_halves,
):
    refs = counts, rows, columns
    places = Places(refs, row_halves.shape[0], column_sum.shape[0], own.shape[-1] // LANES, paired)
    width = own.shape[-1]
    tiles = width // LANES
    other = base_other
    if paired:
        other = base_other[...] + jnp.concatenate([sums_other[t] for t in range(tiles)], axis=1)
    for t in range(tiles):
        for (c, values), (_, previous) in zip(
            row_block_tiles(t, own, other, paired), row_block_tiles(t, p_ref, p_other, paired)
        ):
            row_halves[c * tiles + t] = stacked_halves(jnp.concatenate([values, previous], axis=0))
    column_sum[...] = jnp.zeros_like(column_sum)
    loop_held(
        places,
        held,
        lambda slots: visit_transposed(
            slots, places, lambda slot: held[slot], row_halves, column_sum
        ),
    )
    for j in range(column_sum.shape[0]):
        sum_halves[j] = stacked_halves(column_sum[j, 8:16])

    def keep(index, _):
        part = pl.ds(index * 8, 8)
        kept[part] = held[pl.ds(kept.shape[0] + index * 8, 8)]
        return 0

    lax.fori_loop(0, kept.shape[0] // 8, keep, 0)
    y, p, q = own[...], p_ref[...], q_ref[...]
    rows = jnp.concatenate([x_ref[...], y, p], axis=0)
    terms = times_transpose(
        rows, jnp.concatenate([0.5 * q, 0.5 * diagonal[...] * y], axis=0), highest
    )
    image_previous = times_transpose(0.5 * diagonal[...] * y, p, highest)
    nothing = jnp.zeros((8, 16), f32)
    late[...] = jnp.concatenate(
        [
            nothing,
            terms[0:8, 0:8],
            nothing[:, 0:8],
            terms[8:16, 8:16],
            terms[8:16, 0:8] + image_previous,
            nothing,
            terms[16:24, 0:8],
            jnp.zeros((8, LANES - 72), f32),
        ],
        axis=1,
    )


def three_products(left, right):
    rows, columns = left.shape[0] // 2, right.shape[0] // 2
    cross = times_transpose(left, right)
    return cross[:rows, :columns] + cross[rows:, :columns] + cross[:rows, columns:]


def inner_kernel(
    parts, sum_halves, late, y_ref, y_partner, p_ref, for_partner, first_received, spread
):
    near = parts.shape[0]
    tiles = parts.shape[1] // 4
    column_set = [
        stacked_halves(parts[n, first + t])
        for first in (0, tiles)
        for n in range(near)
        for t in range(tiles)
    ]
    gathered = three_products(
        jnp.concatenate(column_set, axis=1),
        jnp.concatenate([sum_halves[j] for j in range(sum_halves.shape[0])], axis=1),
    )
    own = [balanced_sum([parts[n, 2 * tiles + t] for n in range(near)]) for t in range(tiles)]
    pair = three_products(
        stacked_halves(jnp.concatenate(own + [for_partner[t] for t in range(tiles)], axis=1)),
        stacked_halves(
            jnp.concatenate(
                [
                    jnp.concatenate([y_ref[...], y_partner[...]], axis=1),
                    0.5
                    * jnp.concatenate(
                        [p_ref[...]] + [first_received[tiles + t] for t in range(tiles)], axis=1
                    ),
                ],
                axis=0,
            )
        ),
    )
    total = late[...] + jnp.concatenate(
        [
            jnp.zeros((8, 32), f32),
            pair[:, 0:8],
            pair[:, 8:16] + 0.5 * gathered,
            jnp.zeros((8, LANES - 48), f32),
        ],
        axis=1,
    )
    for n in range(spread.shape[0]):
        spread[n] = total


def eliminate_kernel(gram, x_ref, y_ref, ritz, inverse, pencil, image, residual):
    image[...] = y_ref[...]
    gram = gram[...]
    turned = gram.T

    def block(n):
        return gram[:, 8 * n : 8 * n + 8]

    def flipped(n):
        return turned[8 * n : 8 * n + 8, :]

    xx, xy, xp, yy, yp, pp = range(6)
    nothing = jnp.zeros((8, 8), f32)
    unit = (
        lax.broadcasted_iota(jnp.int32, (24, 24), 0) == lax.broadcasted_iota(jnp.int32, (24, 24), 1)
    ).astype(f32)
    work = jnp.concatenate(
        [
            gram[:, 0:24],
            jnp.concatenate([flipped(xy), block(yy), block(yp)], axis=1),
            jnp.concatenate([flipped(xp), flipped(yp), block(pp)], axis=1),
        ],
        axis=0,
    )
    work = jnp.concatenate([work, unit, jnp.zeros((24, LANES - 48), f32)], axis=1)
    pencil[...] = 0.5 * jnp.concatenate(
        [
            jnp.concatenate([block(xy) + flipped(xy), 2.0 * block(yy), block(yp)], axis=1),
            jnp.concatenate([2.0 * block(yy), nothing, nothing], axis=1),
            jnp.concatenate([flipped(yp), nothing, nothing], axis=1),
        ],
        axis=0,
    )
    row_ids = lax.broadcasted_iota(jnp.int32, (24, 1), 0)
    for k in range(0, 24, 2):
        if k == 8:
            factors = work[8:16, 24:32]
            ritz[...] = factors
            r = y_ref[...]
            for j in range(8):
                r = r + factors[:, j : j + 1] * x_ref[j : j + 1, :]
            residual[...] = r
        row, next_row = work[k : k + 1, :], work[k + 1 : k + 2, :]
        column = jnp.broadcast_to(work[:, k : k + 1], work.shape)
        next_column = jnp.broadcast_to(work[:, k + 1 : k + 2], work.shape)
        first, cross, second = column[k : k + 1], column[k + 1 : k + 2], next_column[k + 1 : k + 2]
        scale = 1.0 / first
        next_scale = first / (first * second - cross * cross)
        ratio = cross * scale
        work = (
            work
            - jnp.where(row_ids > k, column, 0.0) * (row * scale)
            - jnp.where(row_ids > k + 1, next_column - column * ratio, 0.0)
            * ((next_row - ratio * row) * next_scale)
        )
    inverse[...] = work[:, 24:48] * lax.rsqrt(jnp.sum(work[:, 0:24] * unit, axis=1, keepdims=True))


def finish_kernel(
    paired, inverse, pencil, inner_parts, ritz, y_ref, parts, received, row_sum, theirs, diagonal,
    residual_image, reduced,
):
    total = balanced_sum([inner_parts[n] for n in range(inner_parts.shape[0])])
    late = jnp.concatenate([total[:, 0:24], total[:, 24:48], total[:, 48:72]], axis=0)
    lower = inverse[...]
    left = times(lower, pencil[...] + late, highest) + times_transpose(lower, late, highest)
    reduced[...] = times_transpose(left, lower, highest)
    for t in range(theirs.shape[0]):
        s = half_result(t, parts, diagonal, y_ref) + received[t] + theirs[t]
        if paired:
            s = s + row_sum[t]
        for j in range(8):
            s = s + ritz[:, j : j + 1] * y_ref[j : j + 1, lanes(t)]
        residual_image[:, lanes(t)] = s


def local(tile_values, tile_row, tile_col, counts, diagonal, current, previous, previous_image, *, sizes):
    near, n_col = sizes
    slots, side = tile_values.shape[2], tile_values.shape[-1]
    width = current.shape[1]
    tiles = width // side
    paired = n_col == 2
    row_tiles = n_col * tiles
    column_tiles = 2 * near * tiles
    blocks = kept_in_hbm(tile_values.reshape(slots, side, side))
    places = [counts, tile_row, tile_col]
    diagonal = diagonal.reshape(1, width)

    def swap(values, axis="col"):
        return lax.ppermute(values, axis, [(0, 1), (1, 0)])

    def to_partner(values):
        return swap(values, "half")

    devices = ("half", "near", "col")

    def to_near(values):
        groups = [
            [(h * near + (p + c % 2 * (near // 2)) % near) * n_col + c for p in range(near)]
            for h in range(2)
            for c in range(n_col)
        ]
        return lax.all_to_all(values, devices, 0, 0, tiled=True, axis_index_groups=groups)

    def from_columns(values):
        return swap(values) if paired else lax.all_gather(values, "col", axis=0)

    other = from_columns(current)
    partner = to_partner(current)
    *held_places, column_sum, held = call(
        functools.partial(transposed_current_kernel, paired),
        "transposed_current",
        [pltpu.SMEM(part.shape, part.dtype) for part in places[1:]]
        + [shape(column_tiles, 8, side), shape(slots, side, 2 * side, dtype=bf16)],
        [counts, *map(kept_in_hbm, places[1:]), blocks, kept_in_hbm(current), other],
        [in_smem] + [in_hbm] * 4 + [in_vmem],
        [pltpu.VMEM((8, width), f32), pltpu.SemaphoreType.DMA((3,))]
        + stream_scratch(slots, side)
        + [pltpu.VMEM((row_tiles, 16, side), bf16)],
        micros=3.0,
    )
    places[1:] = [pltpu.with_memory_space_constraint(part, pltpu.SMEM) for part in held_places]
    payload = call(
        assemble_kernel,
        "assemble_current",
        shape(near, 4 * tiles, 8, side),
        [current, partner, column_sum],
        [in_vmem] * 3,
    )
    parts = to_near(payload)
    sums = call(
        first_partner_sums_kernel,
        "partner_sums",
        shape(2 * tiles + 1, 8, side),
        [parts, previous],
        [in_vmem] * 2,
    )
    first_received = to_partner(sums)
    row_sum = call(
        functools.partial(direct_held_kernel, paired),
        "direct_current",
        shape(row_tiles, 8, side),
        [*places, held, parts],
        [in_smem] * 3 + [in_vmem] * 2,
        [pltpu.VMEM((column_tiles, 16, side), bf16)],
        micros=2.2,
    )
    combine = functools.partial(
        call,
        functools.partial(combine_kernel, paired),
        "combine",
        operands=[parts, row_sum, diagonal, current],
        specs=[in_vmem] * 4,
    )
    if paired:
        previous_other = swap(previous)
        mine = combine(out_shape=shape(2 * tiles, 8, side))
        base, base_other = call(
            base_kernel,
            "base",
            [shape(tiles + 1, 8, side), shape(8, width)],
            [mine, swap(mine)],
            [in_vmem] * 2,
        )
        sums_other = swap(first_received[:tiles])
    else:
        mine, rows = combine(out_shape=[shape(8, width), shape(n_col, 8, width)])
        base = mine + jnp.sum(lax.all_to_all(rows, "col", 0, 0, tiled=True), axis=0)
        base = base.reshape(8, tiles, side).transpose(1, 0, 2)
        sums_other = first_received
        previous_other = lax.all_gather(previous, "col", axis=0)
    base_partner = to_partner(base)
    image = call(image_kernel, "image", shape(8, width), [base, first_received], [in_vmem] * 2)
    if not paired:
        base_other = lax.all_gather(image, "col", axis=0)
    column_sum, sum_halves, late, kept = call(
        functools.partial(transposed_image_kernel, paired),
        "transposed_image",
        [
            shape(column_tiles, 16, side),
            shape(column_tiles, 16, side, dtype=bf16),
            shape(8, LANES),
            shape(slots // 2, side, 2 * side, dtype=bf16),
        ],
        [
            *places, held, image, base_other, sums_other, previous, previous_other, diagonal,
            current, previous_image,
        ],
        [in_smem] * 3 + [in_vmem] * 9,
        [pltpu.VMEM((row_tiles, 32, side), bf16)],
        micros=1.8,
    )
    payload, partner_image = call(
        assemble_image_kernel,
        "assemble_image",
        [shape(near, 4 * tiles + 1, 8, side), shape(8, width)],
        [
            image, base_partner, sums, first_received, column_sum, current, partner, previous,
        ],
        [in_vmem] * 8,
    )
    parts = to_near(payload)
    for_partner, gram = call(
        partner_sums_kernel,
        "partner_sums",
        [shape(tiles, 8, side), shape(8, LANES)],
        [parts],
        [in_vmem],
    )
    their_gram = swap(gram) if paired else lax.psum(gram, "col") - gram
    spread = call(
        inner_kernel,
        "inner_products",
        shape(2 * near * n_col, 8, LANES),
        [
            parts, sum_halves, late, image, partner_image, previous, for_partner, first_received,
        ],
        [in_vmem] * 8,
        micros=1.1,
    )
    everyone = [list(range(2 * near * n_col))[::-1]]
    inner_parts = lax.all_to_all(spread, devices, 0, 0, tiled=True, axis_index_groups=everyone)
    received = to_partner(for_partner)
    row_sum, rest, gram = call(
        functools.partial(direct_kernel, paired),
        "direct_image",
        [
            shape(row_tiles, 8, side),
            shape(tiles if paired else row_tiles, 8, side),
            shape(8, LANES),
        ],
        [*places, blocks, parts, kept, gram, their_gram],
        [in_smem] * 3 + [in_hbm] + [in_vmem] * 4,
        stream_scratch(slots // 2, side) + [pltpu.VMEM((column_tiles, 16, side), bf16)],
        micros=3.4,
    )
    if paired:
        theirs = swap(rest)
    else:
        rest = rest.reshape(n_col, tiles, 8, side)
        theirs = jnp.sum(lax.all_to_all(rest, "col", 0, 0, tiled=True), axis=0)
    ritz, inverse, pencil, image_out, residual = call(
        eliminate_kernel,
        "eliminate",
        [shape(8, 8), shape(24, 24), shape(24, 24), shape(8, width), shape(8, width)],
        [gram, current, image],
        [in_vmem] * 3,
        micros=1.3,
    )
    residual_image, reduced = call(
        functools.partial(finish_kernel, paired),
        "finish",
        [shape(8, width), shape(24, 24)],
        [
            inverse, pencil, inner_parts, ritz, image, parts, received, row_sum, theirs, diagonal,
        ],
        [in_vmem] * 10,
        micros=1.0,
    )
    return (image_out, residual, residual_image, reduced)


def solution(mesh):
    n_row, n_col = mesh.shape["row"], mesh.shape["col"]
    near = n_row // 2
    cut = jax.sharding.Mesh(mesh.devices.reshape(2, near, n_col), ("half", "near", "col"))
    row = ("half", "near")
    vectors = P(None, ("half", "near", "col"))
    return jax.shard_map(
        functools.partial(local, sizes=(near, n_col)),
        mesh=cut,
        in_specs=(
            P(row, "col", None, None, None),
            P(row, "col", None),
            P(row, "col", None),
            P(row, "col"),
            P(("half", "near", "col")),
            vectors,
            vectors,
            vectors,
        ),
        out_specs=(vectors, vectors, vectors, P()),
        check_vma=False,
    )
```

```python
import functools
import math

import jax
import jax.numpy as jnp
from jax import lax
from jax.experimental import pallas as pl
from jax.experimental.pallas import tpu as pltpu
from jax.sharding import PartitionSpec as P

f32 = jnp.float32
bf16 = jnp.bfloat16
highest = lax.Precision.HIGHEST
LANES = 128
in_vmem = pl.BlockSpec(memory_space=pltpu.VMEM)
in_smem = pl.BlockSpec(memory_space=pltpu.SMEM)
in_hbm = pl.BlockSpec(memory_space=pltpu.HBM)
params = pltpu.CompilerParams(vmem_limit_bytes=32 * 2**20)


def cost_of(micros):
    return pl.CostEstimate(flops=0, bytes_accessed=1, transcendentals=0)


def call(kernel, name, out_shape, operands, specs, scratch=(), micros=0.1):
    return pl.pallas_call(
        kernel,
        out_shape=out_shape,
        in_specs=specs,
        out_specs=jax.tree.map(
            lambda out: in_vmem if isinstance(out, jax.ShapeDtypeStruct) else in_smem, out_shape
        ),
        scratch_shapes=scratch,
        compiler_params=params,
        cost_estimate=cost_of(micros),
        name=name,
    )(*operands)


def kept_in_hbm(values):
    return pltpu.with_memory_space_constraint(values, pltpu.HBM)


def shape(*dims, dtype=f32):
    return jax.ShapeDtypeStruct(dims, dtype)


def halves(values):
    high = values.astype(bf16)
    return high, (values - high.astype(f32)).astype(bf16)


def stacked_halves(values):
    high = values.astype(bf16).astype(f32)
    return jnp.concatenate([high, values - high], axis=0).astype(bf16)


def times_transpose(left, right, precision=None):
    return lax.dot_general(
        left, right, (((1,), (1,)), ((), ())), preferred_element_type=f32, precision=precision
    )


def times(left, right, precision=None):
    return lax.dot_general(
        left, right, (((1,), (0,)), ((), ())), preferred_element_type=f32, precision=precision
    )


def lanes(t):
    return slice(t * LANES, (t + 1) * LANES)


def balanced_sum(terms):
    while len(terms) > 1:
        terms = [sum(terms[n : n + 2]) for n in range(0, len(terms), 2)]
    return terms[0]


def row_block_tiles(t, own, other, paired):
    if paired:
        return [(0, own[:, lanes(t)]), (1, other[:, lanes(t)])]
    return [(c, other[c, :, lanes(t)]) for c in range(other.shape[0])]


class Places:
    def __init__(self, refs, row_tiles, column_tiles, tiles, paired):
        counts, self.rows, self.columns = refs
        self.live = counts[0, 0]
        loop_step = step_of(self.rows.shape[-1])
        self.reach = (self.live + loop_step - 1) // loop_step * loop_step
        here = lax.axis_index("col")
        self.row_mask = here * tiles if paired else 0
        self.column_mask = lax.axis_index("half") * (column_tiles // 2) + lax.rem(here, 2) * (
            column_tiles // 4
        )

    def row(self, slot):
        return lax.bitwise_xor(self.rows[0, 0, slot], self.row_mask)

    def column(self, slot):
        return lax.bitwise_xor(self.columns[0, 0, slot], self.column_mask)

    def weight(self, slot):
        return jnp.where(slot < self.live, 1.0, 0.0).astype(f32)


def step_of(slots):
    return math.gcd(slots, 32)


def group_of(slots):
    return math.gcd(slots, 16)


class Stream:
    def __init__(self, blocks, staged, semaphores):
        self.blocks, self.staged, self.semaphores = blocks, staged, semaphores
        self.group = group_of(staged.shape[0])
        self.groups = staged.shape[0] // self.group
        for index in range(self.groups):
            self.copy(index).start()

    def copy(self, index):
        part = pl.ds(index * self.group, self.group)
        return pltpu.make_async_copy(
            self.blocks.at[part], self.staged.at[part], self.semaphores.at[index]
        )

    def loop(self, reach, visit):
        def step(index, _):
            self.copy(index).wait()
            visit([index * self.group + s for s in range(self.group)])
            return 0

        def leave(index, _):
            self.copy(index).wait()
            return 0

        groups = jnp.minimum(reach // self.group, self.groups)
        lax.fori_loop(0, groups, step, 0)
        lax.fori_loop(groups, self.groups, leave, 0)


def stream_scratch(slots, side):
    return [
        pltpu.VMEM((slots, side, side), f32),
        pltpu.SemaphoreType.DMA((slots // group_of(slots),)),
    ]


def visit_transposed(slots, places, tile, row_halves, column_sum):
    count = column_sum.shape[1]
    products = []
    for slot in slots:
        u = row_halves[places.row(slot)]
        pair = tile(slot)
        both = jnp.concatenate([pair[:, :LANES], pair[:, LANES:]], axis=0)
        product = times(jnp.concatenate([u, u], axis=1), both)
        products.append((product[:count] + product[count:]) * places.weight(slot))
    for slot, product in zip(slots, products):
        column_sum[places.column(slot)] += product


def visit_direct(slots, places, tile, column_halves, row_sum):
    products = []
    for slot in slots:
        x = column_halves[places.column(slot)]
        product = times_transpose(jnp.concatenate([x, x], axis=1), tile(slot))
        products.append((product[:8] + product[8:]) * places.weight(slot))
    for slot, product in zip(slots, products):
        row_sum[places.row(slot)] += product


def tile_from(staged):
    return lambda slot: jnp.concatenate(halves(staged[slot]), axis=1)


def loop_held(places, held, visit, first=0):
    group = step_of(held.shape[0])

    def step(index, _):
        visit([first + index * group + s for s in range(group)])
        return 0

    lax.fori_loop(0, jnp.maximum(places.reach - first, 0) // group, step, 0)


def transposed_current_kernel(
    paired, *refs
):
    inputs, (blocks, x_ref, other), outputs, refs = refs[:3], refs[3:6], refs[6:9], refs[9:]
    column_sum, held, own, semaphore, staged, semaphores, row_halves = refs
    copies = [
        pltpu.make_async_copy(source, target, semaphore.at[n])
        for n, (source, target) in enumerate(zip((*inputs, x_ref), (*outputs, own)))
    ]
    for copy in copies:
        copy.start()
    stream = Stream(blocks, staged, semaphores)
    for copy in copies:
        copy.wait()
    places = Places(outputs, row_halves.shape[0], column_sum.shape[0], own.shape[-1] // LANES, paired)
    tiles = own.shape[-1] // LANES
    for t in range(tiles):
        for c, values in row_block_tiles(t, own, other, paired):
            row_halves[c * tiles + t] = stacked_halves(values)
    column_sum[...] = jnp.zeros_like(column_sum)

    def split(slot):
        pair = jnp.concatenate(halves(staged[slot]), axis=1)
        held[slot] = pair
        return pair

    stream.loop(places.reach, lambda slots: visit_transposed(slots, places, split, row_halves, column_sum))


def assemble_kernel(own, partner, column_sum, payload):
    tiles = own.shape[-1] // LANES
    near = payload.shape[0]
    for n in range(near):
        for t in range(tiles):
            payload[n, t] = own[:, lanes(t)]
            payload[n, tiles + t] = partner[:, lanes(t)]
            payload[n, 2 * tiles + t] = column_sum[n * tiles + t]
            payload[n, 3 * tiles + t] = column_sum[(near + n) * tiles + t]


def assemble_image_kernel(
    own, base_partner, sums, received, column_sum, x_ref, x_partner, p_ref, payload
):
    tiles = own.shape[-1] // LANES
    near = payload.shape[0]
    partner = [base_partner[t] + sums[t] for t in range(tiles)]
    basis = jnp.concatenate(
        [
            jnp.concatenate([x_ref[...], x_partner[...]], axis=1),
            jnp.concatenate([own[...]] + partner, axis=1),
            jnp.concatenate([p_ref[...]] + [received[tiles + t] for t in range(tiles)], axis=1),
        ],
        axis=0,
    )
    outer = times_transpose(basis, basis, highest)
    gram = jnp.concatenate(
        [outer[0:8], outer[8:16, 8:24], outer[16:24, 16:24], jnp.zeros((8, LANES - 48), f32)], axis=1
    )
    for n in range(near):
        for t in range(tiles):
            payload[n, t] = own[:, lanes(t)]
            payload[n, tiles + t] = partner[t]
            payload[n, 2 * tiles + t] = column_sum[n * tiles + t, 0:8]
            payload[n, 3 * tiles + t] = column_sum[(near + n) * tiles + t, 0:8]
        payload[n, 4 * tiles] = gram


def first_partner_sums_kernel(parts, previous, sums):
    near = parts.shape[0]
    tiles = parts.shape[1] // 4
    for t in range(tiles):
        sums[t] = balanced_sum([parts[n, 3 * tiles + t] for n in range(near)])
        sums[tiles + t] = previous[:, lanes(t)]
    sums[2 * tiles] = jnp.zeros_like(sums[2 * tiles])


def partner_sums_kernel(parts, sums, gram):
    near = parts.shape[0]
    tiles = parts.shape[1] // 4
    for t in range(tiles):
        sums[t] = balanced_sum([parts[n, 3 * tiles + t] for n in range(near)])
    gram[...] = balanced_sum([parts[n, 4 * tiles] for n in range(near)])


def fill_column_set(column_halves, parts):
    near = parts.shape[0]
    tiles = parts.shape[1] // 4
    for n in range(near):
        for t in range(tiles):
            column_halves[n * tiles + t] = stacked_halves(parts[n, t])
            column_halves[(near + n) * tiles + t] = stacked_halves(parts[n, tiles + t])


def direct_held_kernel(paired, counts, rows, columns, held, parts, row_sum, column_halves):
    refs = counts, rows, columns
    places = Places(refs, row_sum.shape[0], column_halves.shape[0], parts.shape[1] // 4, paired)
    fill_column_set(column_halves, parts)
    row_sum[...] = jnp.zeros_like(row_sum)
    loop_held(
        places,
        held,
        lambda slots: visit_direct(slots, places, lambda slot: held[slot], column_halves, row_sum),
    )


def direct_kernel(
    paired, counts, rows, columns, blocks, parts, kept, mine, theirs,
    row_sum, rest, gram,
    staged, semaphores, column_halves,
):
    refs = counts, rows, columns
    places = Places(refs, row_sum.shape[0], column_halves.shape[0], parts.shape[1] // 4, paired)
    stream = Stream(blocks, staged, semaphores)
    gram[...] = mine[...] + theirs[...]
    fill_column_set(column_halves, parts)
    row_sum[...] = jnp.zeros_like(row_sum)
    first = staged.shape[0]
    loop_held(
        places,
        kept,
        lambda slots: visit_direct(
            slots, places, lambda slot: kept[slot - first], column_halves, row_sum
        ),
        first,
    )
    stream.loop(
        places.reach,
        lambda slots: visit_direct(slots, places, tile_from(staged), column_halves, row_sum),
    )
    for t in range(rest.shape[0]):
        rest[t] = row_sum[row_sum.shape[0] - rest.shape[0] + t]


def half_result(t, parts, diagonal, vectors):
    near = parts.shape[0]
    tiles = parts.shape[1] // 4
    return diagonal[:, lanes(t)] * vectors[:, lanes(t)] + balanced_sum(
        [parts[n, 2 * tiles + t] for n in range(near)]
    )


def combine_kernel(paired, parts, row_sum, diagonal, vectors, mine, *rows):
    tiles = parts.shape[1] // 4
    for t in range(tiles):
        total = half_result(t, parts, diagonal, vectors)
        if paired:
            mine[t] = total + row_sum[t]
            mine[tiles + t] = row_sum[tiles + t]
        else:
            mine[:, lanes(t)] = total
            for c in range(rows[0].shape[0]):
                rows[0][c, :, lanes(t)] = row_sum[c * tiles + t]


def base_kernel(mine, theirs, own, other):
    tiles = own.shape[0] - 1
    for t in range(tiles):
        own[t] = mine[t] + theirs[tiles + t]
        other[:, lanes(t)] = theirs[t] + mine[tiles + t]
    own[tiles] = jnp.zeros_like(own[tiles])


def image_kernel(base, received, image):
    for t in range(image.shape[-1] // LANES):
        image[:, lanes(t)] = base[t] + received[t]


def transposed_image_kernel(
    paired, counts, rows, columns, held, own, base_other, sums_other, p_ref, p_other, diagonal,
    x_ref, q_ref, received,
    column_sum, sum_halves, late, kept,
    row_halves,
):
    refs = counts, rows, columns
    places = Places(refs, row_halves.shape[0], column_sum.shape[0], own.shape[-1] // LANES, paired)
    width = own.shape[-1]
    tiles = width // LANES
    other = base_other
    if paired:
        other = base_other[...] + jnp.concatenate([sums_other[t] for t in range(tiles)], axis=1)
    for t in range(tiles):
        for (c, values), (_, previous) in zip(
            row_block_tiles(t, own, other, paired), row_block_tiles(t, p_ref, p_other, paired)
        ):
            row_halves[c * tiles + t] = stacked_halves(jnp.concatenate([values, previous], axis=0))
    column_sum[...] = jnp.zeros_like(column_sum)
    loop_held(
        places,
        held,
        lambda slots: visit_transposed(
            slots, places, lambda slot: held[slot], row_halves, column_sum
        ),
    )
    scale = jnp.where(lax.broadcasted_iota(jnp.int32, (16, 1), 0) < 8, 1.0, 0.5).astype(f32)
    count = column_sum.shape[0]
    for j in range(count):
        sum_halves[j] = stacked_halves(column_sum[j] * scale)
    for t in range(tiles):
        for n, previous in enumerate((p_ref[:, lanes(t)], received[tiles + t])):
            sum_halves[count + n * tiles + t] = stacked_halves(
                jnp.concatenate([jnp.zeros_like(previous), 0.5 * previous], axis=0)
            )

    def keep(index, _):
        part = pl.ds(index * 8, 8)
        kept[part] = held[pl.ds(kept.shape[0] + index * 8, 8)]
        return 0

    lax.fori_loop(0, kept.shape[0] // 8, keep, 0)
    y, p, q = own[...], p_ref[...], q_ref[...]
    rows = jnp.concatenate([x_ref[...], y, p], axis=0)
    terms = times_transpose(
        rows, jnp.concatenate([0.5 * q, 0.5 * diagonal[...] * y], axis=0), highest
    )
    image_previous = times_transpose(0.5 * diagonal[...] * y, p, highest)
    nothing = jnp.zeros((8, 16), f32)
    late[...] = jnp.concatenate(
        [
            nothing,
            terms[0:8, 0:8],
            nothing[:, 0:8],
            terms[8:16, 8:16],
            terms[8:16, 0:8] + image_previous,
            nothing,
            terms[16:24, 0:8],
            jnp.zeros((8, LANES - 72), f32),
        ],
        axis=1,
    )


def inner_kernel(parts, sum_halves, late, for_partner, spread):
    near = parts.shape[0]
    tiles = parts.shape[1] // 4
    left = [
        stacked_halves(parts[n, first + t])
        for first in (0, tiles)
        for n in range(near)
        for t in range(tiles)
    ]
    for t in range(tiles):
        left.append(stacked_halves(balanced_sum([parts[n, 2 * tiles + t] for n in range(near)])))
    for t in range(tiles):
        left.append(stacked_halves(for_partner[t]))
    cross = times_transpose(
        jnp.concatenate(left, axis=1),
        jnp.concatenate([sum_halves[j] for j in range(sum_halves.shape[0])], axis=1),
    )
    terms = cross[0:8, 0:16] + cross[8:16, 0:16] + cross[0:8, 16:32]
    total = late[...] + jnp.concatenate(
        [jnp.zeros((8, 32), f32), terms, jnp.zeros((8, LANES - 48), f32)], axis=1
    )
    for n in range(spread.shape[0]):
        spread[n] = total


def eliminate_kernel(gram, x_ref, y_ref, ritz, inverse, pencil, image, residual):
    image[...] = y_ref[...]
    gram = gram[...]
    turned = gram.T

    def block(n):
        return gram[:, 8 * n : 8 * n + 8]

    def flipped(n):
        return turned[8 * n : 8 * n + 8, :]

    xx, xy, xp, yy, yp, pp = range(6)
    nothing = jnp.zeros((8, 8), f32)
    unit = (
        lax.broadcasted_iota(jnp.int32, (24, 24), 0) == lax.broadcasted_iota(jnp.int32, (24, 24), 1)
    ).astype(f32)
    work = jnp.concatenate(
        [
            gram[:, 0:24],
            jnp.concatenate([flipped(xy), block(yy), block(yp)], axis=1),
            jnp.concatenate([flipped(xp), flipped(yp), block(pp)], axis=1),
        ],
        axis=0,
    )
    work = jnp.concatenate([work, unit, jnp.zeros((24, LANES - 48), f32)], axis=1)
    pencil[...] = 0.5 * jnp.concatenate(
        [
            jnp.concatenate([block(xy) + flipped(xy), 2.0 * block(yy), block(yp)], axis=1),
            jnp.concatenate([2.0 * block(yy), nothing, nothing], axis=1),
            jnp.concatenate([flipped(yp), nothing, nothing], axis=1),
        ],
        axis=0,
    )
    row_ids = lax.broadcasted_iota(jnp.int32, (24, 1), 0)
    for k in range(0, 24, 2):
        if k == 8:
            factors = work[8:16, 24:32]
            ritz[...] = factors
            r = y_ref[...]
            for j in range(8):
                r = r + factors[:, j : j + 1] * x_ref[j : j + 1, :]
            residual[...] = r
        row, next_row = work[k : k + 1, :], work[k + 1 : k + 2, :]
        column = jnp.broadcast_to(work[:, k : k + 1], work.shape)
        next_column = jnp.broadcast_to(work[:, k + 1 : k + 2], work.shape)
        first, cross, second = column[k : k + 1], column[k + 1 : k + 2], next_column[k + 1 : k + 2]
        scale = 1.0 / first
        next_scale = first / (first * second - cross * cross)
        ratio = cross * scale
        work = (
            work
            - jnp.where(row_ids > k, column, 0.0) * (row * scale)
            - jnp.where(row_ids > k + 1, next_column - column * ratio, 0.0)
            * ((next_row - ratio * row) * next_scale)
        )
    inverse[...] = work[:, 24:48] * lax.rsqrt(jnp.sum(work[:, 0:24] * unit, axis=1, keepdims=True))


def finish_kernel(
    paired, inverse, pencil, inner_parts, ritz, y_ref, parts, received, row_sum, theirs, diagonal,
    residual_image, reduced,
):
    total = balanced_sum([inner_parts[n] for n in range(inner_parts.shape[0])])
    late = jnp.concatenate([total[:, 0:24], total[:, 24:48], total[:, 48:72]], axis=0)
    lower = inverse[...]
    left = times(lower, pencil[...] + late, highest) + times_transpose(lower, late, highest)
    reduced[...] = times_transpose(left, lower, highest)
    for t in range(theirs.shape[0]):
        s = half_result(t, parts, diagonal, y_ref) + received[t] + theirs[t]
        if paired:
            s = s + row_sum[t]
        for j in range(8):
            s = s + ritz[:, j : j + 1] * y_ref[j : j + 1, lanes(t)]
        residual_image[:, lanes(t)] = s


def local(tile_values, tile_row, tile_col, counts, diagonal, current, previous, previous_image, *, sizes):
    near, n_col = sizes
    slots, side = tile_values.shape[2], tile_values.shape[-1]
    width = current.shape[1]
    tiles = width // side
    paired = n_col == 2
    row_tiles = n_col * tiles
    column_tiles = 2 * near * tiles
    blocks = kept_in_hbm(tile_values.reshape(slots, side, side))
    places = [counts, tile_row, tile_col]
    diagonal = diagonal.reshape(1, width)

    def swap(values, axis="col"):
        return lax.ppermute(values, axis, [(0, 1), (1, 0)])

    def to_partner(values):
        return swap(values, "half")

    devices = ("half", "near", "col")

    def to_near(values):
        groups = [
            [(h * near + (p + c % 2 * (near // 2)) % near) * n_col + c for p in range(near)]
            for h in range(2)
            for c in range(n_col)
        ]
        return lax.all_to_all(values, devices, 0, 0, tiled=True, axis_index_groups=groups)

    def from_columns(values):
        return swap(values) if paired else lax.all_gather(values, "col", axis=0)

    other = from_columns(current)
    partner = to_partner(current)
    *places, column_sum, held = call(
        functools.partial(transposed_current_kernel, paired),
        "transposed_current",
        [pltpu.SMEM(part.shape, part.dtype) for part in places]
        + [shape(column_tiles, 8, side), shape(slots, side, 2 * side, dtype=bf16)],
        [counts, *map(kept_in_hbm, places[1:]), blocks, kept_in_hbm(current), other],
        [pl.BlockSpec(memory_space=pl.ANY)] + [in_hbm] * 4 + [in_vmem],
        [pltpu.VMEM((8, width), f32), pltpu.SemaphoreType.DMA((4,))]
        + stream_scratch(slots, side)
        + [pltpu.VMEM((row_tiles, 16, side), bf16)],
        micros=3.0,
    )
    places = [pltpu.with_memory_space_constraint(part, pltpu.SMEM) for part in places]
    payload = call(
        assemble_kernel,
        "assemble_current",
        shape(near, 4 * tiles, 8, side),
        [current, partner, column_sum],
        [in_vmem] * 3,
    )
    parts = to_near(payload)
    sums = call(
        first_partner_sums_kernel,
        "partner_sums",
        shape(2 * tiles + 1, 8, side),
        [parts, previous],
        [in_vmem] * 2,
    )
    first_received = to_partner(sums)
    row_sum = call(
        functools.partial(direct_held_kernel, paired),
        "direct_current",
        shape(row_tiles, 8, side),
        [*places, held, parts],
        [in_smem] * 3 + [in_vmem] * 2,
        [pltpu.VMEM((column_tiles, 16, side), bf16)],
        micros=2.2,
    )
    combine = functools.partial(
        call,
        functools.partial(combine_kernel, paired),
        "combine",
        operands=[parts, row_sum, diagonal, current],
        specs=[in_vmem] * 4,
    )
    if paired:
        previous_other = swap(previous)
        mine = combine(out_shape=shape(2 * tiles, 8, side))
        base, base_other = call(
            base_kernel,
            "base",
            [shape(tiles + 1, 8, side), shape(8, width)],
            [mine, swap(mine)],
            [in_vmem] * 2,
        )
        sums_other = swap(first_received[:tiles])
    else:
        mine, rows = combine(out_shape=[shape(8, width), shape(n_col, 8, width)])
        base = mine + jnp.sum(lax.all_to_all(rows, "col", 0, 0, tiled=True), axis=0)
        base = base.reshape(8, tiles, side).transpose(1, 0, 2)
        sums_other = first_received
        previous_other = lax.all_gather(previous, "col", axis=0)
    base_partner = to_partner(base)
    image = call(image_kernel, "image", shape(8, width), [base, first_received], [in_vmem] * 2)
    if not paired:
        base_other = lax.all_gather(image, "col", axis=0)
    column_sum, sum_halves, late, kept = call(
        functools.partial(transposed_image_kernel, paired),
        "transposed_image",
        [
            shape(column_tiles, 16, side),
            shape(column_tiles + 2 * tiles, 32, side, dtype=bf16),
            shape(8, LANES),
            shape(slots // 2, side, 2 * side, dtype=bf16),
        ],
        [
            *places, held, image, base_other, sums_other, previous, previous_other, diagonal,
            current, previous_image, first_received,
        ],
        [in_smem] * 3 + [in_vmem] * 10,
        [pltpu.VMEM((row_tiles, 32, side), bf16)],
        micros=1.8,
    )
    payload = call(
        assemble_image_kernel,
        "assemble_image",
        shape(near, 4 * tiles + 1, 8, side),
        [
            image, base_partner, sums, first_received, column_sum, current, partner, previous,
        ],
        [in_vmem] * 8,
    )
    parts = to_near(payload)
    for_partner, gram = call(
        partner_sums_kernel,
        "partner_sums",
        [shape(tiles, 8, side), shape(8, LANES)],
        [parts],
        [in_vmem],
    )
    their_gram = swap(gram) if paired else lax.psum(gram, "col") - gram
    spread = call(
        inner_kernel,
        "inner_products",
        shape(2 * near * n_col, 8, LANES),
        [parts, sum_halves, late, for_partner],
        [in_vmem] * 4,
        micros=1.1,
    )
    everyone = [list(range(2 * near * n_col))[::-1]]
    inner_parts = lax.all_to_all(spread, devices, 0, 0, tiled=True, axis_index_groups=everyone)
    received = to_partner(for_partner)
    row_sum, rest, gram = call(
        functools.partial(direct_kernel, paired),
        "direct_image",
        [
            shape(row_tiles, 8, side),
            shape(tiles if paired else row_tiles, 8, side),
            shape(8, LANES),
        ],
        [*places, blocks, parts, kept, gram, their_gram],
        [in_smem] * 3 + [in_hbm] + [in_vmem] * 4,
        stream_scratch(slots // 2, side) + [pltpu.VMEM((column_tiles, 16, side), bf16)],
        micros=3.4,
    )
    if paired:
        theirs = swap(rest)
    else:
        rest = rest.reshape(n_col, tiles, 8, side)
        theirs = jnp.sum(lax.all_to_all(rest, "col", 0, 0, tiled=True), axis=0)
    ritz, inverse, pencil, image_out, residual = call(
        eliminate_kernel,
        "eliminate",
        [shape(8, 8), shape(24, 24), shape(24, 24), shape(8, width), shape(8, width)],
        [gram, current, image],
        [in_vmem] * 3,
        micros=1.3,
    )
    residual_image, reduced = call(
        functools.partial(finish_kernel, paired),
        "finish",
        [shape(8, width), shape(24, 24)],
        [
            inverse, pencil, inner_parts, ritz, image, parts, received, row_sum, theirs, diagonal,
        ],
        [in_vmem] * 10,
        micros=1.0,
    )
    return (image_out, residual, residual_image, reduced)


def solution(mesh):
    n_row, n_col = mesh.shape["row"], mesh.shape["col"]
    near = n_row // 2
    cut = jax.sharding.Mesh(mesh.devices.reshape(2, near, n_col), ("half", "near", "col"))
    row = ("half", "near")
    vectors = P(None, ("half", "near", "col"))
    return jax.shard_map(
        functools.partial(local, sizes=(near, n_col)),
        mesh=cut,
        in_specs=(
            P(row, "col", None, None, None),
            P(row, "col", None),
            P(row, "col", None),
            P(row, "col"),
            P(("half", "near", "col")),
            vectors,
            vectors,
            vectors,
        ),
        out_specs=(vectors, vectors, vectors, P()),
        check_vma=False,
    )
```

```python
import functools
import math

import jax
import jax.numpy as jnp
from jax import lax
from jax.experimental import pallas as pl
from jax.experimental.pallas import tpu as pltpu
from jax.sharding import PartitionSpec as P

f32 = jnp.float32
bf16 = jnp.bfloat16
highest = lax.Precision.HIGHEST
LANES = 128
in_vmem = pl.BlockSpec(memory_space=pltpu.VMEM)
in_smem = pl.BlockSpec(memory_space=pltpu.SMEM)
in_hbm = pl.BlockSpec(memory_space=pltpu.HBM)
params = pltpu.CompilerParams(vmem_limit_bytes=32 * 2**20)


def cost_of(micros):
    return pl.CostEstimate(flops=0, bytes_accessed=1, transcendentals=0)


def call(kernel, name, out_shape, operands, specs, scratch=(), micros=0.1):
    return pl.pallas_call(
        kernel,
        out_shape=out_shape,
        in_specs=specs,
        out_specs=jax.tree.map(
            lambda out: in_vmem if isinstance(out, jax.ShapeDtypeStruct) else in_smem, out_shape
        ),
        scratch_shapes=scratch,
        compiler_params=params,
        cost_estimate=cost_of(micros),
        name=name,
    )(*operands)


def kept_in_hbm(values):
    return pltpu.with_memory_space_constraint(values, pltpu.HBM)


def shape(*dims, dtype=f32):
    return jax.ShapeDtypeStruct(dims, dtype)


def halves(values):
    high = values.astype(bf16)
    return high, (values - high.astype(f32)).astype(bf16)


def stacked_halves(values):
    high = values.astype(bf16).astype(f32)
    return jnp.concatenate([high, values - high], axis=0).astype(bf16)


def times_transpose(left, right, precision=None):
    return lax.dot_general(
        left, right, (((1,), (1,)), ((), ())), preferred_element_type=f32, precision=precision
    )


def times(left, right, precision=None):
    return lax.dot_general(
        left, right, (((1,), (0,)), ((), ())), preferred_element_type=f32, precision=precision
    )


def lanes(t):
    return slice(t * LANES, (t + 1) * LANES)


def balanced_sum(terms):
    while len(terms) > 1:
        terms = [sum(terms[n : n + 2]) for n in range(0, len(terms), 2)]
    return terms[0]


def row_block_tiles(t, own, other, paired):
    if paired:
        return [(0, own[:, lanes(t)]), (1, other[:, lanes(t)])]
    return [(c, other[c, :, lanes(t)]) for c in range(other.shape[0])]


class Places:
    def __init__(self, refs, row_tiles, column_tiles, tiles, paired):
        counts, self.rows, self.columns = refs
        self.live = counts[0, 0]
        loop_step = step_of(self.rows.shape[-1])
        self.reach = (self.live + loop_step - 1) // loop_step * loop_step
        here = lax.axis_index("col")
        self.row_mask = here * tiles if paired else 0
        self.column_mask = lax.axis_index("half") * (column_tiles // 2) + lax.rem(here, 2) * (
            column_tiles // 4
        )

    def row(self, slot):
        return lax.bitwise_xor(self.rows[0, 0, slot], self.row_mask)

    def column(self, slot):
        return lax.bitwise_xor(self.columns[0, 0, slot], self.column_mask)

    def weight(self, slot):
        return jnp.where(slot < self.live, 1.0, 0.0).astype(f32)


def step_of(slots):
    return math.gcd(slots, 32)


def group_of(slots):
    return math.gcd(slots, 16)


class Stream:
    def __init__(self, blocks, staged, semaphores):
        self.blocks, self.staged, self.semaphores = blocks, staged, semaphores
        self.group = group_of(staged.shape[0])
        self.groups = staged.shape[0] // self.group
        for index in range(self.groups):
            self.copy(index).start()

    def copy(self, index):
        part = pl.ds(index * self.group, self.group)
        return pltpu.make_async_copy(
            self.blocks.at[part], self.staged.at[part], self.semaphores.at[index]
        )

    def loop(self, reach, visit):
        def step(index, _):
            self.copy(index).wait()
            visit([index * self.group + s for s in range(self.group)])
            return 0

        def leave(index, _):
            self.copy(index).wait()
            return 0

        groups = jnp.minimum(reach // self.group, self.groups)
        lax.fori_loop(0, groups, step, 0)
        lax.fori_loop(groups, self.groups, leave, 0)


def stream_scratch(slots, side):
    return [
        pltpu.VMEM((slots, side, side), f32),
        pltpu.SemaphoreType.DMA((slots // group_of(slots),)),
    ]


def visit_transposed(slots, places, tile, row_halves, column_sum):
    count = column_sum.shape[1]
    products = []
    for slot in slots:
        u = row_halves[places.row(slot)]
        pair = tile(slot)
        both = jnp.concatenate([pair[:, :LANES], pair[:, LANES:]], axis=0)
        product = times(jnp.concatenate([u, u], axis=1), both)
        products.append((product[:count] + product[count:]) * places.weight(slot))
    for slot, product in zip(slots, products):
        column_sum[places.column(slot)] += product


def visit_direct(slots, places, tile, column_halves, row_sum):
    products = []
    for slot in slots:
        x = column_halves[places.column(slot)]
        product = times_transpose(jnp.concatenate([x, x], axis=1), tile(slot))
        products.append((product[:8] + product[8:]) * places.weight(slot))
    for slot, product in zip(slots, products):
        row_sum[places.row(slot)] += product


def tile_from(staged):
    return lambda slot: jnp.concatenate(halves(staged[slot]), axis=1)


def loop_held(places, held, visit, first=0):
    group = step_of(held.shape[0])

    def step(index, _):
        visit([first + index * group + s for s in range(group)])
        return 0

    lax.fori_loop(0, jnp.maximum(places.reach - first, 0) // group, step, 0)


def transposed_current_kernel(
    paired, *refs
):
    inputs, (blocks, x_ref, other), outputs, refs = refs[:3], refs[3:6], refs[6:9], refs[9:]
    column_sum, held, own, semaphore, staged, semaphores, row_halves = refs
    copies = [
        pltpu.make_async_copy(source, target, semaphore.at[n])
        for n, (source, target) in enumerate(zip((*inputs, x_ref), (*outputs, own)))
    ]
    for copy in copies:
        copy.start()
    stream = Stream(blocks, staged, semaphores)
    for copy in copies:
        copy.wait()
    places = Places(outputs, row_halves.shape[0], column_sum.shape[0], own.shape[-1] // LANES, paired)
    tiles = own.shape[-1] // LANES
    for t in range(tiles):
        for c, values in row_block_tiles(t, own, other, paired):
            row_halves[c * tiles + t] = stacked_halves(values)
    column_sum[...] = jnp.zeros_like(column_sum)

    def split(slot):
        pair = jnp.concatenate(halves(staged[slot]), axis=1)
        held[slot] = pair
        return pair

    stream.loop(places.reach, lambda slots: visit_transposed(slots, places, split, row_halves, column_sum))


def assemble_kernel(own, partner, column_sum, payload):
    tiles = own.shape[-1] // LANES
    near = payload.shape[0]
    for n in range(near):
        for t in range(tiles):
            payload[n, t] = own[:, lanes(t)]
            payload[n, tiles + t] = partner[:, lanes(t)]
            payload[n, 2 * tiles + t] = column_sum[n * tiles + t]
            payload[n, 3 * tiles + t] = column_sum[(near + n) * tiles + t]


def assemble_image_kernel(
    own, base_partner, sums, column_sum, x_ref, x_partner, p_ref, payload, previous_halves
):
    tiles = own.shape[-1] // LANES
    near = payload.shape[0]
    partner = [base_partner[t] + sums[t] for t in range(tiles)]
    basis = jnp.concatenate(
        [
            jnp.concatenate([x_ref[...], x_partner[...]], axis=1),
            jnp.concatenate([own[...]] + partner, axis=1),
            jnp.concatenate([p_ref[...]] + [base_partner[tiles + t] for t in range(tiles)], axis=1),
        ],
        axis=0,
    )
    for t in range(tiles):
        for n, previous in enumerate((p_ref[:, lanes(t)], base_partner[tiles + t])):
            previous_halves[n * tiles + t] = stacked_halves(
                jnp.concatenate([jnp.zeros_like(previous), 0.5 * previous], axis=0)
            )
    outer = times_transpose(basis, basis, highest)
    gram = jnp.concatenate(
        [outer[0:8], outer[8:16, 8:24], outer[16:24, 16:24], jnp.zeros((8, LANES - 48), f32)], axis=1
    )
    for n in range(near):
        for t in range(tiles):
            payload[n, t] = own[:, lanes(t)]
            payload[n, tiles + t] = partner[t]
            payload[n, 2 * tiles + t] = column_sum[n * tiles + t, 0:8]
            payload[n, 3 * tiles + t] = column_sum[(near + n) * tiles + t, 0:8]
        payload[n, 4 * tiles] = gram


def first_partner_sums_kernel(parts, sums):
    near = parts.shape[0]
    tiles = parts.shape[1] // 4
    for t in range(tiles):
        sums[t] = balanced_sum([parts[n, 3 * tiles + t] for n in range(near)])


def partner_sums_kernel(parts, sums, gram):
    near = parts.shape[0]
    tiles = parts.shape[1] // 4
    for t in range(tiles):
        sums[t] = balanced_sum([parts[n, 3 * tiles + t] for n in range(near)])
    gram[...] = balanced_sum([parts[n, 4 * tiles] for n in range(near)])


def fill_column_set(column_halves, parts):
    near = parts.shape[0]
    tiles = parts.shape[1] // 4
    for n in range(near):
        for t in range(tiles):
            column_halves[n * tiles + t] = stacked_halves(parts[n, t])
            column_halves[(near + n) * tiles + t] = stacked_halves(parts[n, tiles + t])


def direct_held_kernel(paired, counts, rows, columns, held, parts, row_sum, column_halves):
    refs = counts, rows, columns
    places = Places(refs, row_sum.shape[0], column_halves.shape[0], parts.shape[1] // 4, paired)
    fill_column_set(column_halves, parts)
    row_sum[...] = jnp.zeros_like(row_sum)
    loop_held(
        places,
        held,
        lambda slots: visit_direct(slots, places, lambda slot: held[slot], column_halves, row_sum),
    )


def direct_kernel(
    paired, counts, rows, columns, blocks, parts, kept, mine, theirs,
    row_sum, rest, gram,
    staged, semaphores, column_halves,
):
    refs = counts, rows, columns
    places = Places(refs, row_sum.shape[0], column_halves.shape[0], parts.shape[1] // 4, paired)
    stream = Stream(blocks, staged, semaphores)
    gram[...] = mine[...] + theirs[...]
    fill_column_set(column_halves, parts)
    row_sum[...] = jnp.zeros_like(row_sum)
    first = staged.shape[0]
    loop_held(
        places,
        kept,
        lambda slots: visit_direct(
            slots, places, lambda slot: kept[slot - first], column_halves, row_sum
        ),
        first,
    )
    stream.loop(
        places.reach,
        lambda slots: visit_direct(slots, places, tile_from(staged), column_halves, row_sum),
    )
    for t in range(rest.shape[0]):
        rest[t] = row_sum[row_sum.shape[0] - rest.shape[0] + t]


def half_result(t, parts, diagonal, vectors):
    near = parts.shape[0]
    tiles = parts.shape[1] // 4
    return diagonal[:, lanes(t)] * vectors[:, lanes(t)] + balanced_sum(
        [parts[n, 2 * tiles + t] for n in range(near)]
    )


def combine_kernel(paired, parts, row_sum, diagonal, vectors, sums, other_sums, mine, shipped, *rows):
    tiles = parts.shape[1] // 4
    for t in range(tiles):
        shipped[t] = sums[t]
        shipped[tiles + t] = other_sums[t]
        total = half_result(t, parts, diagonal, vectors)
        if paired:
            mine[t] = total + row_sum[t]
            mine[tiles + t] = row_sum[tiles + t]
        else:
            mine[:, lanes(t)] = total
            for c in range(rows[0].shape[0]):
                rows[0][c, :, lanes(t)] = row_sum[c * tiles + t]


def base_kernel(mine, theirs, previous, own, other):
    tiles = own.shape[0] // 2
    for t in range(tiles):
        own[t] = mine[t] + theirs[tiles + t]
        own[tiles + t] = previous[:, lanes(t)]
        other[:, lanes(t)] = theirs[t] + mine[tiles + t]


def image_kernel(base, received, image):
    for t in range(image.shape[-1] // LANES):
        image[:, lanes(t)] = base[t] + received[t]


def transposed_image_kernel(
    paired, counts, rows, columns, held, own, base_other, sums_other, p_ref, p_other, diagonal,
    x_ref, q_ref,
    column_sum, sum_halves, late, kept,
    row_halves,
):
    refs = counts, rows, columns
    places = Places(refs, row_halves.shape[0], column_sum.shape[0], own.shape[-1] // LANES, paired)
    width = own.shape[-1]
    tiles = width // LANES
    other = base_other
    if paired:
        other = base_other[...] + jnp.concatenate(
            [sums_other[tiles + t] for t in range(tiles)], axis=1
        )
    for t in range(tiles):
        for (c, values), (_, previous) in zip(
            row_block_tiles(t, own, other, paired), row_block_tiles(t, p_ref, p_other, paired)
        ):
            row_halves[c * tiles + t] = stacked_halves(jnp.concatenate([values, previous], axis=0))
    column_sum[...] = jnp.zeros_like(column_sum)
    loop_held(
        places,
        held,
        lambda slots: visit_transposed(
            slots, places, lambda slot: held[slot], row_halves, column_sum
        ),
    )
    scale = jnp.where(lax.broadcasted_iota(jnp.int32, (16, 1), 0) < 8, 1.0, 0.5).astype(f32)
    for j in range(column_sum.shape[0]):
        sum_halves[j] = stacked_halves(column_sum[j] * scale)

    def keep(index, _):
        part = pl.ds(index * 8, 8)
        kept[part] = held[pl.ds(kept.shape[0] + index * 8, 8)]
        return 0

    lax.fori_loop(0, kept.shape[0] // 8, keep, 0)
    y, p, q = own[...], p_ref[...], q_ref[...]
    rows = jnp.concatenate([x_ref[...], y, p], axis=0)
    terms = times_transpose(
        rows, jnp.concatenate([0.5 * q, 0.5 * diagonal[...] * y], axis=0), highest
    )
    image_previous = times_transpose(0.5 * diagonal[...] * y, p, highest)
    nothing = jnp.zeros((8, 16), f32)
    late[...] = jnp.concatenate(
        [
            nothing,
            terms[0:8, 0:8],
            nothing[:, 0:8],
            terms[8:16, 8:16],
            terms[8:16, 0:8] + image_previous,
            nothing,
            terms[16:24, 0:8],
            jnp.zeros((8, LANES - 72), f32),
        ],
        axis=1,
    )


def inner_kernel(parts, sum_halves, previous_halves, late, for_partner, spread):
    near = parts.shape[0]
    tiles = parts.shape[1] // 4
    left = [
        stacked_halves(parts[n, first + t])
        for first in (0, tiles)
        for n in range(near)
        for t in range(tiles)
    ]
    for t in range(tiles):
        left.append(stacked_halves(balanced_sum([parts[n, 2 * tiles + t] for n in range(near)])))
    for t in range(tiles):
        left.append(stacked_halves(for_partner[t]))
    cross = times_transpose(
        jnp.concatenate(left, axis=1),
        jnp.concatenate(
            [ref[j] for ref in (sum_halves, previous_halves) for j in range(ref.shape[0])], axis=1
        ),
    )
    terms = cross[0:8, 0:16] + cross[8:16, 0:16] + cross[0:8, 16:32]
    total = late[...] + jnp.concatenate(
        [jnp.zeros((8, 32), f32), terms, jnp.zeros((8, LANES - 48), f32)], axis=1
    )
    for n in range(spread.shape[0]):
        spread[n] = total


def eliminate_kernel(gram, x_ref, y_ref, ritz, inverse, pencil, image, residual):
    image[...] = y_ref[...]
    gram = gram[...]
    turned = gram.T

    def block(n):
        return gram[:, 8 * n : 8 * n + 8]

    def flipped(n):
        return turned[8 * n : 8 * n + 8, :]

    xx, xy, xp, yy, yp, pp = range(6)
    nothing = jnp.zeros((8, 8), f32)
    unit = (
        lax.broadcasted_iota(jnp.int32, (24, 24), 0) == lax.broadcasted_iota(jnp.int32, (24, 24), 1)
    ).astype(f32)
    work = jnp.concatenate(
        [
            gram[:, 0:24],
            jnp.concatenate([flipped(xy), block(yy), block(yp)], axis=1),
            jnp.concatenate([flipped(xp), flipped(yp), block(pp)], axis=1),
        ],
        axis=0,
    )
    work = jnp.concatenate([work, unit, jnp.zeros((24, LANES - 48), f32)], axis=1)
    pencil[...] = 0.5 * jnp.concatenate(
        [
            jnp.concatenate([block(xy) + flipped(xy), 2.0 * block(yy), block(yp)], axis=1),
            jnp.concatenate([2.0 * block(yy), nothing, nothing], axis=1),
            jnp.concatenate([flipped(yp), nothing, nothing], axis=1),
        ],
        axis=0,
    )
    row_ids = lax.broadcasted_iota(jnp.int32, (24, 1), 0)
    for k in range(0, 24, 2):
        if k == 8:
            factors = work[8:16, 24:32]
            ritz[...] = factors
            r = y_ref[...]
            for j in range(8):
                r = r + factors[:, j : j + 1] * x_ref[j : j + 1, :]
            residual[...] = r
        row, next_row = work[k : k + 1, :], work[k + 1 : k + 2, :]
        column = jnp.broadcast_to(work[:, k : k + 1], work.shape)
        next_column = jnp.broadcast_to(work[:, k + 1 : k + 2], work.shape)
        first, cross, second = column[k : k + 1], column[k + 1 : k + 2], next_column[k + 1 : k + 2]
        scale = 1.0 / first
        next_scale = first / (first * second - cross * cross)
        ratio = cross * scale
        work = (
            work
            - jnp.where(row_ids > k, column, 0.0) * (row * scale)
            - jnp.where(row_ids > k + 1, next_column - column * ratio, 0.0)
            * ((next_row - ratio * row) * next_scale)
        )
    inverse[...] = work[:, 24:48] * lax.rsqrt(jnp.sum(work[:, 0:24] * unit, axis=1, keepdims=True))


def finish_kernel(
    paired, inverse, pencil, inner_parts, ritz, y_ref, parts, received, row_sum, theirs, diagonal,
    residual_image, reduced,
):
    total = balanced_sum([inner_parts[n] for n in range(inner_parts.shape[0])])
    late = jnp.concatenate([total[:, 0:24], total[:, 24:48], total[:, 48:72]], axis=0)
    lower = inverse[...]
    left = times(lower, pencil[...] + late, highest) + times_transpose(lower, late, highest)
    reduced[...] = times_transpose(left, lower, highest)
    for t in range(theirs.shape[0]):
        s = half_result(t, parts, diagonal, y_ref) + received[t] + theirs[t]
        if paired:
            s = s + row_sum[t]
        for j in range(8):
            s = s + ritz[:, j : j + 1] * y_ref[j : j + 1, lanes(t)]
        residual_image[:, lanes(t)] = s


def local(tile_values, tile_row, tile_col, counts, diagonal, current, previous, previous_image, *, sizes):
    near, n_col = sizes
    slots, side = tile_values.shape[2], tile_values.shape[-1]
    width = current.shape[1]
    tiles = width // side
    paired = n_col == 2
    row_tiles = n_col * tiles
    column_tiles = 2 * near * tiles
    blocks = kept_in_hbm(tile_values.reshape(slots, side, side))
    places = [counts, tile_row, tile_col]
    diagonal = diagonal.reshape(1, width)

    def swap(values, axis="col"):
        return lax.ppermute(values, axis, [(0, 1), (1, 0)])

    def to_partner(values):
        return swap(values, "half")

    devices = ("half", "near", "col")

    def to_near(values):
        groups = [
            [(h * near + (p + c % 2 * (near // 2)) % near) * n_col + c for p in range(near)]
            for h in range(2)
            for c in range(n_col)
        ]
        return lax.all_to_all(values, devices, 0, 0, tiled=True, axis_index_groups=groups)

    def from_columns(values):
        return swap(values) if paired else lax.all_gather(values, "col", axis=0)

    other = from_columns(current)
    partner = to_partner(current)
    *places, column_sum, held = call(
        functools.partial(transposed_current_kernel, paired),
        "transposed_current",
        [pltpu.SMEM(part.shape, part.dtype) for part in places]
        + [shape(column_tiles, 8, side), shape(slots, side, 2 * side, dtype=bf16)],
        [counts, *map(kept_in_hbm, places[1:]), blocks, kept_in_hbm(current), other],
        [pl.BlockSpec(memory_space=pl.ANY)] + [in_hbm] * 4 + [in_vmem],
        [pltpu.VMEM((8, width), f32), pltpu.SemaphoreType.DMA((4,))]
        + stream_scratch(slots, side)
        + [pltpu.VMEM((row_tiles, 16, side), bf16)],
        micros=3.0,
    )
    places = [pltpu.with_memory_space_constraint(part, pltpu.SMEM) for part in places]
    payload = call(
        assemble_kernel,
        "assemble_current",
        shape(near, 4 * tiles, 8, side),
        [current, partner, column_sum],
        [in_vmem] * 3,
    )
    parts = to_near(payload)
    sums = call(
        first_partner_sums_kernel, "partner_sums", shape(tiles, 8, side), [parts], [in_vmem]
    )
    other_sums = swap(sums) if paired else sums
    row_sum = call(
        functools.partial(direct_held_kernel, paired),
        "direct_current",
        shape(row_tiles, 8, side),
        [*places, held, parts],
        [in_smem] * 3 + [in_vmem] * 2,
        [pltpu.VMEM((column_tiles, 16, side), bf16)],
        micros=2.2,
    )
    combine = functools.partial(
        call,
        functools.partial(combine_kernel, paired),
        "combine",
        operands=[parts, row_sum, diagonal, current, sums, other_sums],
        specs=[in_vmem] * 6,
    )
    if paired:
        previous_other = swap(previous)
        mine, shipped = combine(out_shape=[shape(2 * tiles, 8, side)] * 2)
        base, base_other = call(
            base_kernel,
            "base",
            [shape(2 * tiles, 8, side), shape(8, width)],
            [mine, swap(mine), previous],
            [in_vmem] * 3,
        )
    else:
        mine, shipped, rows = combine(
            out_shape=[shape(8, width), shape(2 * tiles, 8, side), shape(n_col, 8, width)]
        )
        base = mine + jnp.sum(lax.all_to_all(rows, "col", 0, 0, tiled=True), axis=0)
        base = jnp.concatenate([base, previous], axis=1)
        base = base.reshape(8, 2 * tiles, side).transpose(1, 0, 2)
        previous_other = lax.all_gather(previous, "col", axis=0)
    first_received = to_partner(shipped)
    base_partner = to_partner(base)
    image = call(image_kernel, "image", shape(8, width), [base, first_received], [in_vmem] * 2)
    if not paired:
        base_other = lax.all_gather(image, "col", axis=0)
    column_sum, sum_halves, late, kept = call(
        functools.partial(transposed_image_kernel, paired),
        "transposed_image",
        [
            shape(column_tiles, 16, side),
            shape(column_tiles, 32, side, dtype=bf16),
            shape(8, LANES),
            shape(slots // 2, side, 2 * side, dtype=bf16),
        ],
        [
            *places, held, image, base_other, first_received, previous, previous_other, diagonal,
            current, previous_image,
        ],
        [in_smem] * 3 + [in_vmem] * 9,
        [pltpu.VMEM((row_tiles, 32, side), bf16)],
        micros=1.8,
    )
    payload, previous_halves = call(
        assemble_image_kernel,
        "assemble_image",
        [
            shape(near, 4 * tiles + 1, 8, side),
            shape(2 * tiles, 32, side, dtype=bf16),
        ],
        [image, base_partner, sums, column_sum, current, partner, previous],
        [in_vmem] * 7,
    )
    parts = to_near(payload)
    for_partner, gram = call(
        partner_sums_kernel,
        "partner_sums",
        [shape(tiles, 8, side), shape(8, LANES)],
        [parts],
        [in_vmem],
    )
    their_gram = swap(gram) if paired else lax.psum(gram, "col") - gram
    spread = call(
        inner_kernel,
        "inner_products",
        shape(2 * near * n_col, 8, LANES),
        [parts, sum_halves, previous_halves, late, for_partner],
        [in_vmem] * 5,
        micros=1.1,
    )
    everyone = [list(range(2 * near * n_col))[::-1]]
    inner_parts = lax.all_to_all(spread, devices, 0, 0, tiled=True, axis_index_groups=everyone)
    received = to_partner(for_partner)
    row_sum, rest, gram = call(
        functools.partial(direct_kernel, paired),
        "direct_image",
        [
            shape(row_tiles, 8, side),
            shape(tiles if paired else row_tiles, 8, side),
            shape(8, LANES),
        ],
        [*places, blocks, parts, kept, gram, their_gram],
        [in_smem] * 3 + [in_hbm] + [in_vmem] * 4,
        stream_scratch(slots // 2, side) + [pltpu.VMEM((column_tiles, 16, side), bf16)],
        micros=3.4,
    )
    if paired:
        theirs = swap(rest)
    else:
        rest = rest.reshape(n_col, tiles, 8, side)
        theirs = jnp.sum(lax.all_to_all(rest, "col", 0, 0, tiled=True), axis=0)
    ritz, inverse, pencil, image_out, residual = call(
        eliminate_kernel,
        "eliminate",
        [shape(8, 8), shape(24, 24), shape(24, 24), shape(8, width), shape(8, width)],
        [gram, current, image],
        [in_vmem] * 3,
        micros=1.3,
    )
    residual_image, reduced = call(
        functools.partial(finish_kernel, paired),
        "finish",
        [shape(8, width), shape(24, 24)],
        [
            inverse, pencil, inner_parts, ritz, image, parts, received, row_sum, theirs, diagonal,
        ],
        [in_vmem] * 10,
        micros=1.0,
    )
    return (image_out, residual, residual_image, reduced)


def solution(mesh):
    n_row, n_col = mesh.shape["row"], mesh.shape["col"]
    near = n_row // 2
    cut = jax.sharding.Mesh(mesh.devices.reshape(2, near, n_col), ("half", "near", "col"))
    row = ("half", "near")
    vectors = P(None, ("half", "near", "col"))
    return jax.shard_map(
        functools.partial(local, sizes=(near, n_col)),
        mesh=cut,
        in_specs=(
            P(row, "col", None, None, None),
            P(row, "col", None),
            P(row, "col", None),
            P(row, "col"),
            P(("half", "near", "col")),
            vectors,
            vectors,
            vectors,
        ),
        out_specs=(vectors, vectors, vectors, P()),
        check_vma=False,
    )
```

```python
import functools
import math

import jax
import jax.numpy as jnp
from jax import lax
from jax.experimental import pallas as pl
from jax.experimental.pallas import tpu as pltpu
from jax.sharding import PartitionSpec as P

f32 = jnp.float32
bf16 = jnp.bfloat16
highest = lax.Precision.HIGHEST
LANES = 128
in_vmem = pl.BlockSpec(memory_space=pltpu.VMEM)
in_smem = pl.BlockSpec(memory_space=pltpu.SMEM)
in_hbm = pl.BlockSpec(memory_space=pltpu.HBM)
params = pltpu.CompilerParams(vmem_limit_bytes=32 * 2**20)


def cost_of(micros):
    return pl.CostEstimate(flops=0, bytes_accessed=1, transcendentals=0)


def call(kernel, name, out_shape, operands, specs, scratch=(), micros=0.1):
    return pl.pallas_call(
        kernel,
        out_shape=out_shape,
        in_specs=specs,
        out_specs=jax.tree.map(
            lambda out: in_vmem if isinstance(out, jax.ShapeDtypeStruct) else in_smem, out_shape
        ),
        scratch_shapes=scratch,
        compiler_params=params,
        cost_estimate=cost_of(micros),
        name=name,
    )(*operands)


def kept_in_hbm(values):
    return pltpu.with_memory_space_constraint(values, pltpu.HBM)


def shape(*dims, dtype=f32):
    return jax.ShapeDtypeStruct(dims, dtype)


def halves(values):
    high = values.astype(bf16)
    return high, (values - high.astype(f32)).astype(bf16)


def stacked_halves(values):
    high = values.astype(bf16).astype(f32)
    return jnp.concatenate([high, values - high], axis=0).astype(bf16)


def times_transpose(left, right, precision=None):
    return lax.dot_general(
        left, right, (((1,), (1,)), ((), ())), preferred_element_type=f32, precision=precision
    )


def times(left, right, precision=None):
    return lax.dot_general(
        left, right, (((1,), (0,)), ((), ())), preferred_element_type=f32, precision=precision
    )


def lanes(t):
    return slice(t * LANES, (t + 1) * LANES)


def balanced_sum(terms):
    while len(terms) > 1:
        terms = [sum(terms[n : n + 2]) for n in range(0, len(terms), 2)]
    return terms[0]


def row_block_tiles(t, own, other, paired):
    if paired:
        return [(0, own[:, lanes(t)]), (1, other[:, lanes(t)])]
    return [(c, other[c, :, lanes(t)]) for c in range(other.shape[0])]


class Places:
    def __init__(self, refs, row_tiles, column_tiles, tiles, paired):
        counts, self.rows, self.columns = refs
        self.live = counts[0, 0]
        loop_step = step_of(self.rows.shape[-1])
        self.reach = (self.live + loop_step - 1) // loop_step * loop_step
        here = lax.axis_index("col")
        self.row_mask = here * tiles if paired else 0
        self.column_mask = lax.axis_index("half") * (column_tiles // 2) + lax.rem(here, 2) * (
            column_tiles // 4
        )

    def row(self, slot):
        return lax.bitwise_xor(self.rows[0, 0, slot], self.row_mask)

    def column(self, slot):
        return lax.bitwise_xor(self.columns[0, 0, slot], self.column_mask)

    def weight(self, slot):
        return jnp.where(slot < self.live, 1.0, 0.0).astype(f32)


def step_of(slots):
    return math.gcd(slots, 32)


def group_of(slots):
    return math.gcd(slots, 16)


class Stream:
    def __init__(self, blocks, staged, semaphores):
        self.blocks, self.staged, self.semaphores = blocks, staged, semaphores
        self.group = group_of(staged.shape[0])
        self.groups = staged.shape[0] // self.group
        for index in range(self.groups):
            self.copy(index).start()

    def copy(self, index):
        part = pl.ds(index * self.group, self.group)
        return pltpu.make_async_copy(
            self.blocks.at[part], self.staged.at[part], self.semaphores.at[index]
        )

    def loop(self, reach, visit):
        def step(index, _):
            self.copy(index).wait()
            visit([index * self.group + s for s in range(self.group)])
            return 0

        def leave(index, _):
            self.copy(index).wait()
            return 0

        groups = jnp.minimum(reach // self.group, self.groups)
        lax.fori_loop(0, groups, step, 0)
        lax.fori_loop(groups, self.groups, leave, 0)


def stream_scratch(slots, side):
    return [
        pltpu.VMEM((slots, side, side), f32),
        pltpu.SemaphoreType.DMA((slots // group_of(slots),)),
    ]


def visit_transposed(slots, places, tile, row_halves, column_sum):
    count = column_sum.shape[1]
    products = []
    for slot in slots:
        u = row_halves[places.row(slot)]
        pair = tile(slot)
        both = jnp.concatenate([pair[:, :LANES], pair[:, LANES:]], axis=0)
        product = times(jnp.concatenate([u, u], axis=1), both)
        products.append((product[:count] + product[count:]) * places.weight(slot))
    for slot, product in zip(slots, products):
        column_sum[places.column(slot)] += product


def visit_direct(slots, places, tile, column_halves, row_sum):
    products = []
    for slot in slots:
        x = column_halves[places.column(slot)]
        product = times_transpose(jnp.concatenate([x, x], axis=1), tile(slot))
        products.append((product[:8] + product[8:]) * places.weight(slot))
    for slot, product in zip(slots, products):
        row_sum[places.row(slot)] += product


def tile_from(staged):
    return lambda slot: jnp.concatenate(halves(staged[slot]), axis=1)


def loop_held(places, held, visit, first=0):
    group = step_of(held.shape[0])

    def step(index, _):
        visit([first + index * group + s for s in range(group)])
        return 0

    lax.fori_loop(0, jnp.maximum(places.reach - first, 0) // group, step, 0)


def transposed_current_kernel(
    paired, *refs
):
    inputs, (blocks, x_ref, other), outputs, refs = refs[:3], refs[3:6], refs[6:9], refs[9:]
    column_sum, held, own, semaphore, staged, semaphores, row_halves = refs
    copies = [
        pltpu.make_async_copy(source, target, semaphore.at[n])
        for n, (source, target) in enumerate(zip((*inputs, x_ref), (*outputs, own)))
    ]
    for copy in copies:
        copy.start()
    stream = Stream(blocks, staged, semaphores)
    for copy in copies:
        copy.wait()
    places = Places(outputs, row_halves.shape[0], column_sum.shape[0], own.shape[-1] // LANES, paired)
    tiles = own.shape[-1] // LANES
    for t in range(tiles):
        for c, values in row_block_tiles(t, own, other, paired):
            row_halves[c * tiles + t] = stacked_halves(values)
    column_sum[...] = jnp.zeros_like(column_sum)

    def split(slot):
        pair = jnp.concatenate(halves(staged[slot]), axis=1)
        held[slot] = pair
        return pair

    stream.loop(places.reach, lambda slots: visit_transposed(slots, places, split, row_halves, column_sum))


def assemble_kernel(own, partner, column_sum, payload):
    tiles = own.shape[-1] // LANES
    near = payload.shape[0]
    for n in range(near):
        for t in range(tiles):
            payload[n, t] = own[:, lanes(t)]
            payload[n, tiles + t] = partner[:, lanes(t)]
            payload[n, 2 * tiles + t] = column_sum[n * tiles + t]
            payload[n, 3 * tiles + t] = column_sum[(near + n) * tiles + t]


def early_products(x, y, p):
    basis = jnp.concatenate([x, y, p], axis=0)
    outer = times_transpose(basis, basis, highest)
    return jnp.concatenate(
        [outer[0:8], outer[8:16, 8:24], outer[16:24, 16:24], jnp.zeros((8, LANES - 48), f32)], axis=1
    )


def lower_halves(previous):
    return stacked_halves(jnp.concatenate([jnp.zeros_like(previous), 0.5 * previous], axis=0))


def assemble_image_kernel(
    own, base_partner, sums, column_sum, x_partner, own_gram, payload, partner_halves
):
    tiles = own.shape[-1] // LANES
    near = payload.shape[0]
    partner = [base_partner[t] + sums[t] for t in range(tiles)]
    previous = [base_partner[tiles + t] for t in range(tiles)]
    for t in range(tiles):
        partner_halves[t] = lower_halves(previous[t])
    gram = own_gram[...] + early_products(
        x_partner[...], jnp.concatenate(partner, axis=1), jnp.concatenate(previous, axis=1)
    )
    for n in range(near):
        for t in range(tiles):
            payload[n, t] = own[:, lanes(t)]
            payload[n, tiles + t] = partner[t]
            payload[n, 2 * tiles + t] = column_sum[n * tiles + t, 0:8]
            payload[n, 3 * tiles + t] = column_sum[(near + n) * tiles + t, 0:8]
        payload[n, 4 * tiles] = gram


def first_partner_sums_kernel(parts, sums):
    near = parts.shape[0]
    tiles = parts.shape[1] // 4
    for t in range(tiles):
        sums[t] = balanced_sum([parts[n, 3 * tiles + t] for n in range(near)])


def partner_sums_kernel(parts, sums, gram):
    near = parts.shape[0]
    tiles = parts.shape[1] // 4
    for t in range(tiles):
        sums[t] = balanced_sum([parts[n, 3 * tiles + t] for n in range(near)])
    gram[...] = balanced_sum([parts[n, 4 * tiles] for n in range(near)])


def fill_column_set(column_halves, parts):
    near = parts.shape[0]
    tiles = parts.shape[1] // 4
    for n in range(near):
        for t in range(tiles):
            column_halves[n * tiles + t] = stacked_halves(parts[n, t])
            column_halves[(near + n) * tiles + t] = stacked_halves(parts[n, tiles + t])


def direct_held_kernel(paired, counts, rows, columns, held, parts, row_sum, column_halves):
    refs = counts, rows, columns
    places = Places(refs, row_sum.shape[0], column_halves.shape[0], parts.shape[1] // 4, paired)
    fill_column_set(column_halves, parts)
    row_sum[...] = jnp.zeros_like(row_sum)
    loop_held(
        places,
        held,
        lambda slots: visit_direct(slots, places, lambda slot: held[slot], column_halves, row_sum),
    )


def direct_kernel(
    paired, counts, rows, columns, blocks, parts, kept, mine, theirs,
    row_sum, rest, gram,
    staged, semaphores, column_halves,
):
    refs = counts, rows, columns
    places = Places(refs, row_sum.shape[0], column_halves.shape[0], parts.shape[1] // 4, paired)
    stream = Stream(blocks, staged, semaphores)
    gram[...] = mine[...] + theirs[...]
    fill_column_set(column_halves, parts)
    row_sum[...] = jnp.zeros_like(row_sum)
    first = staged.shape[0]
    loop_held(
        places,
        kept,
        lambda slots: visit_direct(
            slots, places, lambda slot: kept[slot - first], column_halves, row_sum
        ),
        first,
    )
    stream.loop(
        places.reach,
        lambda slots: visit_direct(slots, places, tile_from(staged), column_halves, row_sum),
    )
    for t in range(rest.shape[0]):
        rest[t] = row_sum[row_sum.shape[0] - rest.shape[0] + t]


def half_result(t, parts, diagonal, vectors):
    near = parts.shape[0]
    tiles = parts.shape[1] // 4
    return diagonal[:, lanes(t)] * vectors[:, lanes(t)] + balanced_sum(
        [parts[n, 2 * tiles + t] for n in range(near)]
    )


def combine_kernel(paired, parts, row_sum, diagonal, vectors, sums, other_sums, mine, shipped, *rows):
    tiles = parts.shape[1] // 4
    for t in range(tiles):
        shipped[t] = sums[t]
        shipped[tiles + t] = other_sums[t]
        total = half_result(t, parts, diagonal, vectors)
        if paired:
            mine[t] = total + row_sum[t]
            mine[tiles + t] = row_sum[tiles + t]
        else:
            mine[:, lanes(t)] = total
            for c in range(rows[0].shape[0]):
                rows[0][c, :, lanes(t)] = row_sum[c * tiles + t]


def base_kernel(mine, theirs, previous, own, other):
    tiles = own.shape[0] // 2
    for t in range(tiles):
        own[t] = mine[t] + theirs[tiles + t]
        own[tiles + t] = previous[:, lanes(t)]
        other[:, lanes(t)] = theirs[t] + mine[tiles + t]


def image_kernel(base, received, image):
    for t in range(image.shape[-1] // LANES):
        image[:, lanes(t)] = base[t] + received[t]


def transposed_image_kernel(
    paired, counts, rows, columns, held, own, base_other, sums_other, p_ref, p_other, diagonal,
    x_ref, q_ref,
    column_sum, sum_halves, late, kept, gram, own_halves,
    row_halves,
):
    refs = counts, rows, columns
    places = Places(refs, row_halves.shape[0], column_sum.shape[0], own.shape[-1] // LANES, paired)
    width = own.shape[-1]
    tiles = width // LANES
    other = base_other
    if paired:
        other = base_other[...] + jnp.concatenate(
            [sums_other[tiles + t] for t in range(tiles)], axis=1
        )
    for t in range(tiles):
        for (c, values), (_, previous) in zip(
            row_block_tiles(t, own, other, paired), row_block_tiles(t, p_ref, p_other, paired)
        ):
            row_halves[c * tiles + t] = stacked_halves(jnp.concatenate([values, previous], axis=0))
    column_sum[...] = jnp.zeros_like(column_sum)
    loop_held(
        places,
        held,
        lambda slots: visit_transposed(
            slots, places, lambda slot: held[slot], row_halves, column_sum
        ),
    )
    scale = jnp.where(lax.broadcasted_iota(jnp.int32, (16, 1), 0) < 8, 1.0, 0.5).astype(f32)
    for j in range(column_sum.shape[0]):
        sum_halves[j] = stacked_halves(column_sum[j] * scale)

    def keep(index, _):
        part = pl.ds(index * 8, 8)
        kept[part] = held[pl.ds(kept.shape[0] + index * 8, 8)]
        return 0

    lax.fori_loop(0, kept.shape[0] // 8, keep, 0)
    y, p, q = own[...], p_ref[...], q_ref[...]
    gram[...] = early_products(x_ref[...], y, p)
    for t in range(tiles):
        own_halves[t] = lower_halves(p[:, lanes(t)])
    rows = jnp.concatenate([x_ref[...], y, p], axis=0)
    terms = times_transpose(
        rows, jnp.concatenate([0.5 * q, 0.5 * diagonal[...] * y], axis=0), highest
    )
    image_previous = times_transpose(0.5 * diagonal[...] * y, p, highest)
    nothing = jnp.zeros((8, 16), f32)
    late[...] = jnp.concatenate(
        [
            nothing,
            terms[0:8, 0:8],
            nothing[:, 0:8],
            terms[8:16, 8:16],
            terms[8:16, 0:8] + image_previous,
            nothing,
            terms[16:24, 0:8],
            jnp.zeros((8, LANES - 72), f32),
        ],
        axis=1,
    )


def inner_kernel(parts, sum_halves, own_halves, partner_halves, late, for_partner, spread):
    near = parts.shape[0]
    tiles = parts.shape[1] // 4
    left = [
        stacked_halves(parts[n, first + t])
        for first in (0, tiles)
        for n in range(near)
        for t in range(tiles)
    ]
    for t in range(tiles):
        left.append(stacked_halves(balanced_sum([parts[n, 2 * tiles + t] for n in range(near)])))
    for t in range(tiles):
        left.append(stacked_halves(for_partner[t]))
    cross = times_transpose(
        jnp.concatenate(left, axis=1),
        jnp.concatenate(
            [
                ref[j]
                for ref in (sum_halves, own_halves, partner_halves)
                for j in range(ref.shape[0])
            ],
            axis=1,
        ),
    )
    terms = cross[0:8, 0:16] + cross[8:16, 0:16] + cross[0:8, 16:32]
    total = late[...] + jnp.concatenate(
        [jnp.zeros((8, 32), f32), terms, jnp.zeros((8, LANES - 48), f32)], axis=1
    )
    for n in range(spread.shape[0]):
        spread[n] = total


def eliminate_kernel(gram, x_ref, y_ref, ritz, inverse, pencil, image, residual):
    image[...] = y_ref[...]
    gram = gram[...]
    turned = gram.T

    def block(n):
        return gram[:, 8 * n : 8 * n + 8]

    def flipped(n):
        return turned[8 * n : 8 * n + 8, :]

    xx, xy, xp, yy, yp, pp = range(6)
    nothing = jnp.zeros((8, 8), f32)
    unit = (
        lax.broadcasted_iota(jnp.int32, (24, 24), 0) == lax.broadcasted_iota(jnp.int32, (24, 24), 1)
    ).astype(f32)
    work = jnp.concatenate(
        [
            gram[:, 0:24],
            jnp.concatenate([flipped(xy), block(yy), block(yp)], axis=1),
            jnp.concatenate([flipped(xp), flipped(yp), block(pp)], axis=1),
        ],
        axis=0,
    )
    work = jnp.concatenate([work, unit, jnp.zeros((24, LANES - 48), f32)], axis=1)
    pencil[...] = 0.5 * jnp.concatenate(
        [
            jnp.concatenate([block(xy) + flipped(xy), 2.0 * block(yy), block(yp)], axis=1),
            jnp.concatenate([2.0 * block(yy), nothing, nothing], axis=1),
            jnp.concatenate([flipped(yp), nothing, nothing], axis=1),
        ],
        axis=0,
    )
    row_ids = lax.broadcasted_iota(jnp.int32, (24, 1), 0)
    for k in range(0, 24, 2):
        if k == 8:
            factors = work[8:16, 24:32]
            ritz[...] = factors
            r = y_ref[...]
            for j in range(8):
                r = r + factors[:, j : j + 1] * x_ref[j : j + 1, :]
            residual[...] = r
        row, next_row = work[k : k + 1, :], work[k + 1 : k + 2, :]
        column = jnp.broadcast_to(work[:, k : k + 1], work.shape)
        next_column = jnp.broadcast_to(work[:, k + 1 : k + 2], work.shape)
        first, cross, second = column[k : k + 1], column[k + 1 : k + 2], next_column[k + 1 : k + 2]
        scale = 1.0 / first
        next_scale = first / (first * second - cross * cross)
        ratio = cross * scale
        work = (
            work
            - jnp.where(row_ids > k, column, 0.0) * (row * scale)
            - jnp.where(row_ids > k + 1, next_column - column * ratio, 0.0)
            * ((next_row - ratio * row) * next_scale)
        )
    inverse[...] = work[:, 24:48] * lax.rsqrt(jnp.sum(work[:, 0:24] * unit, axis=1, keepdims=True))


def finish_kernel(
    paired, inverse, pencil, inner_parts, ritz, y_ref, parts, received, row_sum, theirs, diagonal,
    residual_image, reduced,
):
    total = balanced_sum([inner_parts[n] for n in range(inner_parts.shape[0])])
    late = jnp.concatenate([total[:, 0:24], total[:, 24:48], total[:, 48:72]], axis=0)
    lower = inverse[...]
    left = times(lower, pencil[...] + late, highest) + times_transpose(lower, late, highest)
    reduced[...] = times_transpose(left, lower, highest)
    for t in range(theirs.shape[0]):
        s = half_result(t, parts, diagonal, y_ref) + received[t] + theirs[t]
        if paired:
            s = s + row_sum[t]
        for j in range(8):
            s = s + ritz[:, j : j + 1] * y_ref[j : j + 1, lanes(t)]
        residual_image[:, lanes(t)] = s


def local(tile_values, tile_row, tile_col, counts, diagonal, current, previous, previous_image, *, sizes):
    near, n_col = sizes
    slots, side = tile_values.shape[2], tile_values.shape[-1]
    width = current.shape[1]
    tiles = width // side
    paired = n_col == 2
    row_tiles = n_col * tiles
    column_tiles = 2 * near * tiles
    blocks = kept_in_hbm(tile_values.reshape(slots, side, side))
    places = [counts, tile_row, tile_col]
    diagonal = diagonal.reshape(1, width)

    def swap(values, axis="col"):
        return lax.ppermute(values, axis, [(0, 1), (1, 0)])

    def to_partner(values):
        return swap(values, "half")

    devices = ("half", "near", "col")

    def to_near(values):
        groups = [
            [(h * near + (p + c % 2 * (near // 2)) % near) * n_col + c for p in range(near)]
            for h in range(2)
            for c in range(n_col)
        ]
        return lax.all_to_all(values, devices, 0, 0, tiled=True, axis_index_groups=groups)

    def from_columns(values):
        return swap(values) if paired else lax.all_gather(values, "col", axis=0)

    other = from_columns(current)
    partner = to_partner(current)
    *places, column_sum, held = call(
        functools.partial(transposed_current_kernel, paired),
        "transposed_current",
        [pltpu.SMEM(part.shape, part.dtype) for part in places]
        + [shape(column_tiles, 8, side), shape(slots, side, 2 * side, dtype=bf16)],
        [counts, *map(kept_in_hbm, places[1:]), blocks, kept_in_hbm(current), other],
        [pl.BlockSpec(memory_space=pl.ANY)] + [in_hbm] * 4 + [in_vmem],
        [pltpu.VMEM((8, width), f32), pltpu.SemaphoreType.DMA((4,))]
        + stream_scratch(slots, side)
        + [pltpu.VMEM((row_tiles, 16, side), bf16)],
        micros=3.0,
    )
    places = [pltpu.with_memory_space_constraint(part, pltpu.SMEM) for part in places]
    payload = call(
        assemble_kernel,
        "assemble_current",
        shape(near, 4 * tiles, 8, side),
        [current, partner, column_sum],
        [in_vmem] * 3,
    )
    parts = to_near(payload)
    sums = call(
        first_partner_sums_kernel, "partner_sums", shape(tiles, 8, side), [parts], [in_vmem]
    )
    other_sums = swap(sums) if paired else sums
    row_sum = call(
        functools.partial(direct_held_kernel, paired),
        "direct_current",
        shape(row_tiles, 8, side),
        [*places, held, parts],
        [in_smem] * 3 + [in_vmem] * 2,
        [pltpu.VMEM((column_tiles, 16, side), bf16)],
        micros=2.2,
    )
    combine = functools.partial(
        call,
        functools.partial(combine_kernel, paired),
        "combine",
        operands=[parts, row_sum, diagonal, current, sums, other_sums],
        specs=[in_vmem] * 6,
    )
    if paired:
        previous_other = swap(previous)
        mine, shipped = combine(out_shape=[shape(2 * tiles, 8, side)] * 2)
        base, base_other = call(
            base_kernel,
            "base",
            [shape(2 * tiles, 8, side), shape(8, width)],
            [mine, swap(mine), previous],
            [in_vmem] * 3,
        )
    else:
        mine, shipped, rows = combine(
            out_shape=[shape(8, width), shape(2 * tiles, 8, side), shape(n_col, 8, width)]
        )
        base = mine + jnp.sum(lax.all_to_all(rows, "col", 0, 0, tiled=True), axis=0)
        base = jnp.concatenate([base, previous], axis=1)
        base = base.reshape(8, 2 * tiles, side).transpose(1, 0, 2)
        previous_other = lax.all_gather(previous, "col", axis=0)
    first_received = to_partner(shipped)
    base_partner = to_partner(base)
    image = call(image_kernel, "image", shape(8, width), [base, first_received], [in_vmem] * 2)
    if not paired:
        base_other = lax.all_gather(image, "col", axis=0)
    column_sum, sum_halves, late, kept, own_gram, own_halves = call(
        functools.partial(transposed_image_kernel, paired),
        "transposed_image",
        [
            shape(column_tiles, 16, side),
            shape(column_tiles, 32, side, dtype=bf16),
            shape(8, LANES),
            shape(slots // 2, side, 2 * side, dtype=bf16),
            shape(8, LANES),
            shape(tiles, 32, side, dtype=bf16),
        ],
        [
            *places, held, image, base_other, first_received, previous, previous_other, diagonal,
            current, previous_image,
        ],
        [in_smem] * 3 + [in_vmem] * 9,
        [pltpu.VMEM((row_tiles, 32, side), bf16)],
        micros=1.8,
    )
    payload, partner_halves = call(
        assemble_image_kernel,
        "assemble_image",
        [
            shape(near, 4 * tiles + 1, 8, side),
            shape(tiles, 32, side, dtype=bf16),
        ],
        [image, base_partner, sums, column_sum, partner, own_gram],
        [in_vmem] * 6,
    )
    parts = to_near(payload)
    for_partner, gram = call(
        partner_sums_kernel,
        "partner_sums",
        [shape(tiles, 8, side), shape(8, LANES)],
        [parts],
        [in_vmem],
    )
    their_gram = swap(gram) if paired else lax.psum(gram, "col") - gram
    spread = call(
        inner_kernel,
        "inner_products",
        shape(2 * near * n_col, 8, LANES),
        [parts, sum_halves, own_halves, partner_halves, late, for_partner],
        [in_vmem] * 6,
        micros=1.1,
    )
    everyone = [
        [(h * near + n) * n_col + c for n in range(near)[::-1] for c in range(n_col) for h in range(2)]
    ]
    inner_parts = lax.all_to_all(spread, devices, 0, 0, tiled=True, axis_index_groups=everyone)
    received = to_partner(for_partner)
    row_sum, rest, gram = call(
        functools.partial(direct_kernel, paired),
        "direct_image",
        [
            shape(row_tiles, 8, side),
            shape(tiles if paired else row_tiles, 8, side),
            shape(8, LANES),
        ],
        [*places, blocks, parts, kept, gram, their_gram],
        [in_smem] * 3 + [in_hbm] + [in_vmem] * 4,
        stream_scratch(slots // 2, side) + [pltpu.VMEM((column_tiles, 16, side), bf16)],
        micros=3.4,
    )
    if paired:
        theirs = swap(rest)
    else:
        rest = rest.reshape(n_col, tiles, 8, side)
        theirs = jnp.sum(lax.all_to_all(rest, "col", 0, 0, tiled=True), axis=0)
    ritz, inverse, pencil, image_out, residual = call(
        eliminate_kernel,
        "eliminate",
        [shape(8, 8), shape(24, 24), shape(24, 24), shape(8, width), shape(8, width)],
        [gram, current, image],
        [in_vmem] * 3,
        micros=1.3,
    )
    residual_image, reduced = call(
        functools.partial(finish_kernel, paired),
        "finish",
        [shape(8, width), shape(24, 24)],
        [
            inverse, pencil, inner_parts, ritz, image, parts, received, row_sum, theirs, diagonal,
        ],
        [in_vmem] * 10,
        micros=1.0,
    )
    return (image_out, residual, residual_image, reduced)


def solution(mesh):
    n_row, n_col = mesh.shape["row"], mesh.shape["col"]
    near = n_row // 2
    cut = jax.sharding.Mesh(mesh.devices.reshape(2, near, n_col), ("half", "near", "col"))
    row = ("half", "near")
    vectors = P(None, ("half", "near", "col"))
    return jax.shard_map(
        functools.partial(local, sizes=(near, n_col)),
        mesh=cut,
        in_specs=(
            P(row, "col", None, None, None),
            P(row, "col", None),
            P(row, "col", None),
            P(row, "col"),
            P(("half", "near", "col")),
            vectors,
            vectors,
            vectors,
        ),
        out_specs=(vectors, vectors, vectors, P()),
        check_vma=False,
    )
```

```python
import functools
import math

import jax
import jax.numpy as jnp
from jax import lax
from jax.experimental import pallas as pl
from jax.experimental.pallas import tpu as pltpu
from jax.sharding import PartitionSpec as P

f32 = jnp.float32
bf16 = jnp.bfloat16
highest = lax.Precision.HIGHEST
LANES = 128
in_vmem = pl.BlockSpec(memory_space=pltpu.VMEM)
in_smem = pl.BlockSpec(memory_space=pltpu.SMEM)
in_hbm = pl.BlockSpec(memory_space=pltpu.HBM)
params = pltpu.CompilerParams(vmem_limit_bytes=32 * 2**20)


def cost_of(micros):
    return pl.CostEstimate(flops=0, bytes_accessed=1, transcendentals=0)


def call(kernel, name, out_shape, operands, specs, scratch=(), micros=0.1):
    return pl.pallas_call(
        kernel,
        out_shape=out_shape,
        in_specs=specs,
        out_specs=jax.tree.map(
            lambda out: in_vmem if isinstance(out, jax.ShapeDtypeStruct) else in_smem, out_shape
        ),
        scratch_shapes=scratch,
        compiler_params=params,
        cost_estimate=cost_of(micros),
        name=name,
    )(*operands)


def kept_in_hbm(values):
    return pltpu.with_memory_space_constraint(values, pltpu.HBM)


def shape(*dims, dtype=f32):
    return jax.ShapeDtypeStruct(dims, dtype)


def halves(values):
    high = values.astype(bf16)
    return high, (values - high.astype(f32)).astype(bf16)


def stacked_halves(values):
    high = values.astype(bf16).astype(f32)
    return jnp.concatenate([high, values - high], axis=0).astype(bf16)


def times_transpose(left, right, precision=None):
    return lax.dot_general(
        left, right, (((1,), (1,)), ((), ())), preferred_element_type=f32, precision=precision
    )


def times(left, right, precision=None):
    return lax.dot_general(
        left, right, (((1,), (0,)), ((), ())), preferred_element_type=f32, precision=precision
    )


def lanes(t):
    return slice(t * LANES, (t + 1) * LANES)


def balanced_sum(terms):
    while len(terms) > 1:
        terms = [sum(terms[n : n + 2]) for n in range(0, len(terms), 2)]
    return terms[0]


def row_block_tiles(t, own, other, paired):
    if paired:
        return [(0, own[:, lanes(t)]), (1, other[:, lanes(t)])]
    return [(c, other[c, :, lanes(t)]) for c in range(other.shape[0])]


class Places:
    def __init__(self, refs, row_tiles, column_tiles, tiles, paired):
        counts, self.rows, self.columns = refs
        self.live = counts[0, 0]
        loop_step = step_of(self.rows.shape[-1])
        self.reach = (self.live + loop_step - 1) // loop_step * loop_step
        here = lax.axis_index("col")
        self.row_mask = here * tiles if paired else 0
        self.column_mask = lax.axis_index("half") * (column_tiles // 2) + lax.rem(here, 2) * (
            column_tiles // 4
        )

    def row(self, slot):
        return lax.bitwise_xor(self.rows[0, 0, slot], self.row_mask)

    def column(self, slot):
        return lax.bitwise_xor(self.columns[0, 0, slot], self.column_mask)

    def weight(self, slot):
        return jnp.where(slot < self.live, 1.0, 0.0).astype(f32)


def step_of(slots):
    return math.gcd(slots, 32)


def group_of(slots):
    return math.gcd(slots, 16)


class Stream:
    def __init__(self, blocks, staged, semaphores):
        self.blocks, self.staged, self.semaphores = blocks, staged, semaphores
        self.group = group_of(staged.shape[0])
        self.groups = staged.shape[0] // self.group
        for index in range(self.groups):
            self.copy(index).start()

    def copy(self, index):
        part = pl.ds(index * self.group, self.group)
        return pltpu.make_async_copy(
            self.blocks.at[part], self.staged.at[part], self.semaphores.at[index]
        )

    def loop(self, reach, visit):
        def step(index, _):
            self.copy(index).wait()
            visit([index * self.group + s for s in range(self.group)])
            return 0

        def leave(index, _):
            self.copy(index).wait()
            return 0

        groups = jnp.minimum(reach // self.group, self.groups)
        lax.fori_loop(0, groups, step, 0)
        lax.fori_loop(groups, self.groups, leave, 0)


def stream_scratch(slots, side):
    return [
        pltpu.VMEM((slots, side, side), f32),
        pltpu.SemaphoreType.DMA((slots // group_of(slots),)),
    ]


def visit_transposed(slots, places, tile, row_halves, column_sum):
    count = column_sum.shape[1]
    products = []
    for slot in slots:
        u = row_halves[places.row(slot)]
        pair = tile(slot)
        both = jnp.concatenate([pair[:, :LANES], pair[:, LANES:]], axis=0)
        product = times(jnp.concatenate([u, u], axis=1), both)
        products.append((product[:count] + product[count:]) * places.weight(slot))
    for slot, product in zip(slots, products):
        column_sum[places.column(slot)] += product


def visit_direct(slots, places, tile, column_halves, row_sum):
    products = []
    for slot in slots:
        x = column_halves[places.column(slot)]
        product = times_transpose(jnp.concatenate([x, x], axis=1), tile(slot))
        products.append((product[:8] + product[8:]) * places.weight(slot))
    for slot, product in zip(slots, products):
        row_sum[places.row(slot)] += product


def tile_from(staged):
    return lambda slot: jnp.concatenate(halves(staged[slot]), axis=1)


def loop_held(places, held, visit, first=0):
    group = step_of(held.shape[0])

    def step(index, _):
        visit([first + index * group + s for s in range(group)])
        return 0

    lax.fori_loop(0, jnp.maximum(places.reach - first, 0) // group, step, 0)


def transposed_current_kernel(
    paired, *refs
):
    inputs, (blocks, x_ref, other), outputs, refs = refs[:3], refs[3:6], refs[6:9], refs[9:]
    column_sum, held, own, semaphore, staged, semaphores, row_halves = refs
    copies = [
        pltpu.make_async_copy(source, target, semaphore.at[n])
        for n, (source, target) in enumerate(zip((*inputs, x_ref), (*outputs, own)))
    ]
    for copy in copies:
        copy.start()
    stream = Stream(blocks, staged, semaphores)
    for copy in copies:
        copy.wait()
    places = Places(outputs, row_halves.shape[0], column_sum.shape[0], own.shape[-1] // LANES, paired)
    tiles = own.shape[-1] // LANES
    for t in range(tiles):
        for c, values in row_block_tiles(t, own, other, paired):
            row_halves[c * tiles + t] = stacked_halves(values)
    column_sum[...] = jnp.zeros_like(column_sum)

    def split(slot):
        pair = jnp.concatenate(halves(staged[slot]), axis=1)
        held[slot] = pair
        return pair

    stream.loop(places.reach, lambda slots: visit_transposed(slots, places, split, row_halves, column_sum))


def assemble_kernel(own, partner, column_sum, payload):
    tiles = own.shape[-1] // LANES
    near = payload.shape[0]
    for n in range(near):
        for t in range(tiles):
            payload[n, t] = own[:, lanes(t)]
            payload[n, tiles + t] = partner[:, lanes(t)]
            payload[n, 2 * tiles + t] = column_sum[n * tiles + t]
            payload[n, 3 * tiles + t] = column_sum[(near + n) * tiles + t]


def early_products(x, y, p):
    basis = jnp.concatenate([x, y, p], axis=0)
    outer = times_transpose(basis, basis, highest)
    return jnp.concatenate(
        [outer[0:8], outer[8:16, 8:24], outer[16:24, 16:24], jnp.zeros((8, LANES - 48), f32)], axis=1
    )


def lower_halves(previous):
    return stacked_halves(jnp.concatenate([jnp.zeros_like(previous), 0.5 * previous], axis=0))


def assemble_image_kernel(
    own, base_partner, sums, column_sum, x_partner, own_gram, payload, partner_halves
):
    tiles = own.shape[-1] // LANES
    near = payload.shape[0]
    partner = [base_partner[t] + sums[t] for t in range(tiles)]
    previous = [base_partner[tiles + t] for t in range(tiles)]
    for t in range(tiles):
        partner_halves[t] = lower_halves(previous[t])
    gram = own_gram[...] + early_products(
        x_partner[...], jnp.concatenate(partner, axis=1), jnp.concatenate(previous, axis=1)
    )
    for n in range(near):
        for t in range(tiles):
            payload[n, t] = own[:, lanes(t)]
            payload[n, tiles + t] = partner[t]
            payload[n, 2 * tiles + t] = column_sum[n * tiles + t, 0:8]
            payload[n, 3 * tiles + t] = column_sum[(near + n) * tiles + t, 0:8]
        payload[n, 4 * tiles] = gram


def first_partner_sums_kernel(parts, sums):
    near = parts.shape[0]
    tiles = parts.shape[1] // 4
    for t in range(tiles):
        sums[t] = balanced_sum([parts[n, 3 * tiles + t] for n in range(near)])


def partner_sums_kernel(parts, sums, gram):
    near = parts.shape[0]
    tiles = parts.shape[1] // 4
    for t in range(tiles):
        sums[t] = balanced_sum([parts[n, 3 * tiles + t] for n in range(near)])
    gram[...] = balanced_sum([parts[n, 4 * tiles] for n in range(near)])


def fill_column_set(column_halves, parts):
    near = parts.shape[0]
    tiles = parts.shape[1] // 4
    for n in range(near):
        for t in range(tiles):
            column_halves[n * tiles + t] = stacked_halves(parts[n, t])
            column_halves[(near + n) * tiles + t] = stacked_halves(parts[n, tiles + t])


def direct_held_kernel(paired, counts, rows, columns, held, parts, row_sum, column_halves):
    refs = counts, rows, columns
    places = Places(refs, row_sum.shape[0], column_halves.shape[0], parts.shape[1] // 4, paired)
    fill_column_set(column_halves, parts)
    row_sum[...] = jnp.zeros_like(row_sum)
    loop_held(
        places,
        held,
        lambda slots: visit_direct(slots, places, lambda slot: held[slot], column_halves, row_sum),
    )


def direct_kernel(
    paired, counts, rows, columns, blocks, parts, kept, mine, theirs,
    row_sum, rest, gram,
    staged, semaphores, column_halves,
):
    refs = counts, rows, columns
    places = Places(refs, row_sum.shape[0], column_halves.shape[0], parts.shape[1] // 4, paired)
    stream = Stream(blocks, staged, semaphores)
    gram[...] = mine[...] + theirs[...]
    fill_column_set(column_halves, parts)
    row_sum[...] = jnp.zeros_like(row_sum)
    first = staged.shape[0]
    loop_held(
        places,
        kept,
        lambda slots: visit_direct(
            slots, places, lambda slot: kept[slot - first], column_halves, row_sum
        ),
        first,
    )
    stream.loop(
        places.reach,
        lambda slots: visit_direct(slots, places, tile_from(staged), column_halves, row_sum),
    )
    for t in range(rest.shape[0]):
        rest[t] = row_sum[row_sum.shape[0] - rest.shape[0] + t]


def half_result(t, parts, diagonal, vectors):
    near = parts.shape[0]
    tiles = parts.shape[1] // 4
    return diagonal[:, lanes(t)] * vectors[:, lanes(t)] + balanced_sum(
        [parts[n, 2 * tiles + t] for n in range(near)]
    )


def combine_kernel(
    paired, parts, row_sum, diagonal, vectors, sums, other_sums, previous, mine, shipped, *rows
):
    tiles = parts.shape[1] // 4
    for t in range(tiles):
        shipped[t] = sums[t]
        shipped[tiles + t] = other_sums[t]
        total = half_result(t, parts, diagonal, vectors)
        if paired:
            mine[t] = total + row_sum[t]
            mine[tiles + t] = row_sum[tiles + t]
            mine[2 * tiles + t] = previous[:, lanes(t)]
        else:
            mine[:, lanes(t)] = total
            for c in range(rows[0].shape[0]):
                rows[0][c, :, lanes(t)] = row_sum[c * tiles + t]


def base_kernel(mine, theirs, previous, own, other):
    tiles = own.shape[0] // 2
    for t in range(tiles):
        own[t] = mine[t] + theirs[tiles + t]
        own[tiles + t] = previous[:, lanes(t)]
        other[:, lanes(t)] = theirs[t] + mine[tiles + t]


def image_kernel(base, received, image):
    for t in range(image.shape[-1] // LANES):
        image[:, lanes(t)] = base[t] + received[t]


def transposed_image_kernel(
    paired, counts, rows, columns, held, own, base_other, sums_other, p_ref, p_other, diagonal,
    x_ref, q_ref,
    column_sum, sum_halves, late, kept, gram, own_halves,
    row_halves,
):
    refs = counts, rows, columns
    places = Places(refs, row_halves.shape[0], column_sum.shape[0], own.shape[-1] // LANES, paired)
    width = own.shape[-1]
    tiles = width // LANES
    other = base_other
    if paired:
        other = base_other[...] + jnp.concatenate(
            [sums_other[tiles + t] for t in range(tiles)], axis=1
        )
        p_other = jnp.concatenate([p_other[2 * tiles + t] for t in range(tiles)], axis=1)
    for t in range(tiles):
        for (c, values), (_, previous) in zip(
            row_block_tiles(t, own, other, paired), row_block_tiles(t, p_ref, p_other, paired)
        ):
            row_halves[c * tiles + t] = stacked_halves(jnp.concatenate([values, previous], axis=0))
    column_sum[...] = jnp.zeros_like(column_sum)
    loop_held(
        places,
        held,
        lambda slots: visit_transposed(
            slots, places, lambda slot: held[slot], row_halves, column_sum
        ),
    )
    scale = jnp.where(lax.broadcasted_iota(jnp.int32, (16, 1), 0) < 8, 1.0, 0.5).astype(f32)
    for j in range(column_sum.shape[0]):
        sum_halves[j] = stacked_halves(column_sum[j] * scale)

    def keep(index, _):
        part = pl.ds(index * 8, 8)
        kept[part] = held[pl.ds(kept.shape[0] + index * 8, 8)]
        return 0

    lax.fori_loop(0, kept.shape[0] // 8, keep, 0)
    y, p, q = own[...], p_ref[...], q_ref[...]
    gram[...] = early_products(x_ref[...], y, p)
    for t in range(tiles):
        own_halves[t] = lower_halves(p[:, lanes(t)])
    rows = jnp.concatenate([x_ref[...], y, p], axis=0)
    terms = times_transpose(
        rows, jnp.concatenate([0.5 * q, 0.5 * diagonal[...] * y], axis=0), highest
    )
    image_previous = times_transpose(0.5 * diagonal[...] * y, p, highest)
    nothing = jnp.zeros((8, 16), f32)
    late[...] = jnp.concatenate(
        [
            nothing,
            terms[0:8, 0:8],
            nothing[:, 0:8],
            terms[8:16, 8:16],
            terms[8:16, 0:8] + image_previous,
            nothing,
            terms[16:24, 0:8],
            jnp.zeros((8, LANES - 72), f32),
        ],
        axis=1,
    )


def inner_kernel(parts, sum_halves, own_halves, partner_halves, late, for_partner, spread):
    near = parts.shape[0]
    tiles = parts.shape[1] // 4
    left = [
        stacked_halves(parts[n, first + t])
        for first in (0, tiles)
        for n in range(near)
        for t in range(tiles)
    ]
    for t in range(tiles):
        left.append(stacked_halves(balanced_sum([parts[n, 2 * tiles + t] for n in range(near)])))
    for t in range(tiles):
        left.append(stacked_halves(for_partner[t]))
    cross = times_transpose(
        jnp.concatenate(left, axis=1),
        jnp.concatenate(
            [
                ref[j]
                for ref in (sum_halves, own_halves, partner_halves)
                for j in range(ref.shape[0])
            ],
            axis=1,
        ),
    )
    terms = cross[0:8, 0:16] + cross[8:16, 0:16] + cross[0:8, 16:32]
    total = late[...] + jnp.concatenate(
        [jnp.zeros((8, 32), f32), terms, jnp.zeros((8, LANES - 48), f32)], axis=1
    )
    for n in range(spread.shape[0]):
        spread[n] = total


def eliminate_kernel(gram, x_ref, y_ref, ritz, inverse, pencil, image, residual):
    image[...] = y_ref[...]
    gram = gram[...]
    turned = gram.T

    def block(n):
        return gram[:, 8 * n : 8 * n + 8]

    def flipped(n):
        return turned[8 * n : 8 * n + 8, :]

    xx, xy, xp, yy, yp, pp = range(6)
    nothing = jnp.zeros((8, 8), f32)
    unit = (
        lax.broadcasted_iota(jnp.int32, (24, 24), 0) == lax.broadcasted_iota(jnp.int32, (24, 24), 1)
    ).astype(f32)
    work = jnp.concatenate(
        [
            gram[:, 0:24],
            jnp.concatenate([flipped(xy), block(yy), block(yp)], axis=1),
            jnp.concatenate([flipped(xp), flipped(yp), block(pp)], axis=1),
        ],
        axis=0,
    )
    work = jnp.concatenate([work, unit, jnp.zeros((24, LANES - 48), f32)], axis=1)
    pencil[...] = 0.5 * jnp.concatenate(
        [
            jnp.concatenate([block(xy) + flipped(xy), 2.0 * block(yy), block(yp)], axis=1),
            jnp.concatenate([2.0 * block(yy), nothing, nothing], axis=1),
            jnp.concatenate([flipped(yp), nothing, nothing], axis=1),
        ],
        axis=0,
    )
    row_ids = lax.broadcasted_iota(jnp.int32, (24, 1), 0)
    for k in range(0, 24, 2):
        if k == 8:
            factors = work[8:16, 24:32]
            ritz[...] = factors
            r = y_ref[...]
            for j in range(8):
                r = r + factors[:, j : j + 1] * x_ref[j : j + 1, :]
            residual[...] = r
        row, next_row = work[k : k + 1, :], work[k + 1 : k + 2, :]
        column = jnp.broadcast_to(work[:, k : k + 1], work.shape)
        next_column = jnp.broadcast_to(work[:, k + 1 : k + 2], work.shape)
        first, cross, second = column[k : k + 1], column[k + 1 : k + 2], next_column[k + 1 : k + 2]
        scale = 1.0 / first
        next_scale = first / (first * second - cross * cross)
        ratio = cross * scale
        work = (
            work
            - jnp.where(row_ids > k, column, 0.0) * (row * scale)
            - jnp.where(row_ids > k + 1, next_column - column * ratio, 0.0)
            * ((next_row - ratio * row) * next_scale)
        )
    inverse[...] = work[:, 24:48] * lax.rsqrt(jnp.sum(work[:, 0:24] * unit, axis=1, keepdims=True))


def finish_kernel(
    paired, inverse, pencil, inner_parts, ritz, y_ref, parts, received, row_sum, theirs, diagonal,
    residual_image, reduced,
):
    total = balanced_sum([inner_parts[n] for n in range(inner_parts.shape[0])])
    late = jnp.concatenate([total[:, 0:24], total[:, 24:48], total[:, 48:72]], axis=0)
    lower = inverse[...]
    left = times(lower, pencil[...] + late, highest) + times_transpose(lower, late, highest)
    reduced[...] = times_transpose(left, lower, highest)
    for t in range(theirs.shape[0]):
        s = half_result(t, parts, diagonal, y_ref) + received[t] + theirs[t]
        if paired:
            s = s + row_sum[t]
        for j in range(8):
            s = s + ritz[:, j : j + 1] * y_ref[j : j + 1, lanes(t)]
        residual_image[:, lanes(t)] = s


def local(tile_values, tile_row, tile_col, counts, diagonal, current, previous, previous_image, *, sizes):
    near, n_col = sizes
    slots, side = tile_values.shape[2], tile_values.shape[-1]
    width = current.shape[1]
    tiles = width // side
    paired = n_col == 2
    row_tiles = n_col * tiles
    column_tiles = 2 * near * tiles
    blocks = kept_in_hbm(tile_values.reshape(slots, side, side))
    places = [counts, tile_row, tile_col]
    diagonal = diagonal.reshape(1, width)

    def swap(values, axis="col"):
        return lax.ppermute(values, axis, [(0, 1), (1, 0)])

    def to_partner(values):
        return swap(values, "half")

    devices = ("half", "near", "col")

    def to_near(values):
        groups = [
            [(h * near + (p + c % 2 * (near // 2)) % near) * n_col + c for p in range(near)]
            for h in range(2)
            for c in range(n_col)
        ]
        return lax.all_to_all(values, devices, 0, 0, tiled=True, axis_index_groups=groups)

    def from_columns(values):
        return swap(values) if paired else lax.all_gather(values, "col", axis=0)

    other = from_columns(current)
    partner = to_partner(current)
    *places, column_sum, held = call(
        functools.partial(transposed_current_kernel, paired),
        "transposed_current",
        [pltpu.SMEM(part.shape, part.dtype) for part in places]
        + [shape(column_tiles, 8, side), shape(slots, side, 2 * side, dtype=bf16)],
        [counts, *map(kept_in_hbm, places[1:]), blocks, kept_in_hbm(current), other],
        [pl.BlockSpec(memory_space=pl.ANY)] + [in_hbm] * 4 + [in_vmem],
        [pltpu.VMEM((8, width), f32), pltpu.SemaphoreType.DMA((4,))]
        + stream_scratch(slots, side)
        + [pltpu.VMEM((row_tiles, 16, side), bf16)],
        micros=3.0,
    )
    places = [pltpu.with_memory_space_constraint(part, pltpu.SMEM) for part in places]
    payload = call(
        assemble_kernel,
        "assemble_current",
        shape(near, 4 * tiles, 8, side),
        [current, partner, column_sum],
        [in_vmem] * 3,
    )
    parts = to_near(payload)
    sums = call(
        first_partner_sums_kernel, "partner_sums", shape(tiles, 8, side), [parts], [in_vmem]
    )
    other_sums = swap(sums) if paired else sums
    row_sum = call(
        functools.partial(direct_held_kernel, paired),
        "direct_current",
        shape(row_tiles, 8, side),
        [*places, held, parts],
        [in_smem] * 3 + [in_vmem] * 2,
        [pltpu.VMEM((column_tiles, 16, side), bf16)],
        micros=2.2,
    )
    combine = functools.partial(
        call,
        functools.partial(combine_kernel, paired),
        "combine",
        operands=[parts, row_sum, diagonal, current, sums, other_sums, previous],
        specs=[in_vmem] * 7,
    )
    if paired:
        mine, shipped = combine(out_shape=[shape(3 * tiles, 8, side), shape(2 * tiles, 8, side)])
        theirs = previous_other = swap(mine)
        base, base_other = call(
            base_kernel,
            "base",
            [shape(2 * tiles, 8, side), shape(8, width)],
            [mine, theirs, previous],
            [in_vmem] * 3,
        )
    else:
        mine, shipped, rows = combine(
            out_shape=[shape(8, width), shape(2 * tiles, 8, side), shape(n_col, 8, width)]
        )
        base = mine + jnp.sum(lax.all_to_all(rows, "col", 0, 0, tiled=True), axis=0)
        base = jnp.concatenate([base, previous], axis=1)
        base = base.reshape(8, 2 * tiles, side).transpose(1, 0, 2)
        previous_other = lax.all_gather(previous, "col", axis=0)
    first_received = to_partner(shipped)
    base_partner = to_partner(base)
    image = call(image_kernel, "image", shape(8, width), [base, first_received], [in_vmem] * 2)
    if not paired:
        base_other = lax.all_gather(image, "col", axis=0)
    column_sum, sum_halves, late, kept, own_gram, own_halves = call(
        functools.partial(transposed_image_kernel, paired),
        "transposed_image",
        [
            shape(column_tiles, 16, side),
            shape(column_tiles, 32, side, dtype=bf16),
            shape(8, LANES),
            shape(slots // 2, side, 2 * side, dtype=bf16),
            shape(8, LANES),
            shape(tiles, 32, side, dtype=bf16),
        ],
        [
            *places, held, image, base_other, first_received, previous, previous_other, diagonal,
            current, previous_image,
        ],
        [in_smem] * 3 + [in_vmem] * 9,
        [pltpu.VMEM((row_tiles, 32, side), bf16)],
        micros=1.8,
    )
    payload, partner_halves = call(
        assemble_image_kernel,
        "assemble_image",
        [
            shape(near, 4 * tiles + 1, 8, side),
            shape(tiles, 32, side, dtype=bf16),
        ],
        [image, base_partner, sums, column_sum, partner, own_gram],
        [in_vmem] * 6,
    )
    parts = to_near(payload)
    for_partner, gram = call(
        partner_sums_kernel,
        "partner_sums",
        [shape(tiles, 8, side), shape(8, LANES)],
        [parts],
        [in_vmem],
    )
    their_gram = swap(gram) if paired else lax.psum(gram, "col") - gram
    spread = call(
        inner_kernel,
        "inner_products",
        shape(2 * near * n_col, 8, LANES),
        [parts, sum_halves, own_halves, partner_halves, late, for_partner],
        [in_vmem] * 6,
        micros=1.1,
    )
    everyone = [
        [(h * near + n) * n_col + c for n in range(near)[::-1] for c in range(n_col) for h in range(2)]
    ]
    inner_parts = lax.all_to_all(spread, devices, 0, 0, tiled=True, axis_index_groups=everyone)
    received = to_partner(for_partner)
    row_sum, rest, gram = call(
        functools.partial(direct_kernel, paired),
        "direct_image",
        [
            shape(row_tiles, 8, side),
            shape(tiles if paired else row_tiles, 8, side),
            shape(8, LANES),
        ],
        [*places, blocks, parts, kept, gram, their_gram],
        [in_smem] * 3 + [in_hbm] + [in_vmem] * 4,
        stream_scratch(slots // 2, side) + [pltpu.VMEM((column_tiles, 16, side), bf16)],
        micros=3.4,
    )
    if paired:
        theirs = swap(rest)
    else:
        rest = rest.reshape(n_col, tiles, 8, side)
        theirs = jnp.sum(lax.all_to_all(rest, "col", 0, 0, tiled=True), axis=0)
    ritz, inverse, pencil, image_out, residual = call(
        eliminate_kernel,
        "eliminate",
        [shape(8, 8), shape(24, 24), shape(24, 24), shape(8, width), shape(8, width)],
        [gram, current, image],
        [in_vmem] * 3,
        micros=1.3,
    )
    residual_image, reduced = call(
        functools.partial(finish_kernel, paired),
        "finish",
        [shape(8, width), shape(24, 24)],
        [
            inverse, pencil, inner_parts, ritz, image, parts, received, row_sum, theirs, diagonal,
        ],
        [in_vmem] * 10,
        micros=1.0,
    )
    return (image_out, residual, residual_image, reduced)


def solution(mesh):
    n_row, n_col = mesh.shape["row"], mesh.shape["col"]
    near = n_row // 2
    cut = jax.sharding.Mesh(mesh.devices.reshape(2, near, n_col), ("half", "near", "col"))
    row = ("half", "near")
    vectors = P(None, ("half", "near", "col"))
    return jax.shard_map(
        functools.partial(local, sizes=(near, n_col)),
        mesh=cut,
        in_specs=(
            P(row, "col", None, None, None),
            P(row, "col", None),
            P(row, "col", None),
            P(row, "col"),
            P(("half", "near", "col")),
            vectors,
            vectors,
            vectors,
        ),
        out_specs=(vectors, vectors, vectors, P()),
        check_vma=False,
    )
```

```python
import functools
import math

import jax
import jax.numpy as jnp
from jax import lax
from jax.experimental import pallas as pl
from jax.experimental.pallas import tpu as pltpu
from jax.sharding import PartitionSpec as P

f32 = jnp.float32
bf16 = jnp.bfloat16
highest = lax.Precision.HIGHEST
LANES = 128
in_vmem = pl.BlockSpec(memory_space=pltpu.VMEM)
in_smem = pl.BlockSpec(memory_space=pltpu.SMEM)
in_hbm = pl.BlockSpec(memory_space=pltpu.HBM)
params = pltpu.CompilerParams(vmem_limit_bytes=32 * 2**20)


def cost_of(micros):
    return pl.CostEstimate(flops=0, bytes_accessed=1, transcendentals=0)


def call(kernel, name, out_shape, operands, specs, scratch=(), micros=0.1):
    return pl.pallas_call(
        kernel,
        out_shape=out_shape,
        in_specs=specs,
        out_specs=jax.tree.map(
            lambda out: in_vmem if isinstance(out, jax.ShapeDtypeStruct) else in_smem, out_shape
        ),
        scratch_shapes=scratch,
        compiler_params=params,
        cost_estimate=cost_of(micros),
        name=name,
    )(*operands)


def kept_in_hbm(values):
    return pltpu.with_memory_space_constraint(values, pltpu.HBM)


def shape(*dims, dtype=f32):
    return jax.ShapeDtypeStruct(dims, dtype)


def halves(values):
    high = values.astype(bf16)
    return high, (values - high.astype(f32)).astype(bf16)


def stacked_halves(values):
    high = values.astype(bf16).astype(f32)
    return jnp.concatenate([high, values - high], axis=0).astype(bf16)


def times_transpose(left, right, precision=None):
    return lax.dot_general(
        left, right, (((1,), (1,)), ((), ())), preferred_element_type=f32, precision=precision
    )


def times(left, right, precision=None):
    return lax.dot_general(
        left, right, (((1,), (0,)), ((), ())), preferred_element_type=f32, precision=precision
    )


def lanes(t):
    return slice(t * LANES, (t + 1) * LANES)


def balanced_sum(terms):
    while len(terms) > 1:
        terms = [sum(terms[n : n + 2]) for n in range(0, len(terms), 2)]
    return terms[0]


def row_block_tiles(t, own, other, paired):
    if paired:
        return [(0, own[:, lanes(t)]), (1, other[:, lanes(t)])]
    return [(c, other[c, :, lanes(t)]) for c in range(other.shape[0])]


class Places:
    def __init__(self, refs, row_tiles, column_tiles, tiles, paired):
        counts, self.rows, self.columns = refs
        self.live = counts[0, 0]
        loop_step = step_of(self.rows.shape[-1])
        self.reach = (self.live + loop_step - 1) // loop_step * loop_step
        here = lax.axis_index("col")
        self.row_mask = here * tiles if paired else 0
        self.column_mask = lax.axis_index("half") * (column_tiles // 2) + lax.rem(here + 1, 2) * (
            column_tiles // 4
        )

    def row(self, slot):
        return lax.bitwise_xor(self.rows[0, 0, slot], self.row_mask)

    def column(self, slot):
        return lax.bitwise_xor(self.columns[0, 0, slot], self.column_mask)

    def weight(self, slot):
        return jnp.where(slot < self.live, 1.0, 0.0).astype(f32)


def step_of(slots):
    return math.gcd(slots, 32)


def group_of(slots):
    return math.gcd(slots, 16)


class Stream:
    def __init__(self, blocks, staged, semaphores):
        self.blocks, self.staged, self.semaphores = blocks, staged, semaphores
        self.group = group_of(staged.shape[0])
        self.groups = staged.shape[0] // self.group
        for index in range(self.groups):
            self.copy(index).start()

    def copy(self, index):
        part = pl.ds(index * self.group, self.group)
        return pltpu.make_async_copy(
            self.blocks.at[part], self.staged.at[part], self.semaphores.at[index]
        )

    def loop(self, reach, visit):
        def step(index, _):
            self.copy(index).wait()
            visit([index * self.group + s for s in range(self.group)])
            return 0

        def leave(index, _):
            self.copy(index).wait()
            return 0

        groups = jnp.minimum(reach // self.group, self.groups)
        lax.fori_loop(0, groups, step, 0)
        lax.fori_loop(groups, self.groups, leave, 0)


def stream_scratch(slots, side):
    return [
        pltpu.VMEM((slots, side, side), f32),
        pltpu.SemaphoreType.DMA((slots // group_of(slots),)),
    ]


def visit_transposed(slots, places, tile, row_halves, column_sum):
    count = column_sum.shape[1]
    products = []
    for slot in slots:
        u = row_halves[places.row(slot)]
        pair = tile(slot)
        both = jnp.concatenate([pair[:, :LANES], pair[:, LANES:]], axis=0)
        product = times(jnp.concatenate([u, u], axis=1), both)
        products.append((product[:count] + product[count:]) * places.weight(slot))
    for slot, product in zip(slots, products):
        column_sum[places.column(slot)] += product


def visit_direct(slots, places, tile, column_halves, row_sum):
    products = []
    for slot in slots:
        x = column_halves[places.column(slot)]
        product = times_transpose(jnp.concatenate([x, x], axis=1), tile(slot))
        products.append((product[:8] + product[8:]) * places.weight(slot))
    for slot, product in zip(slots, products):
        row_sum[places.row(slot)] += product


def tile_from(staged):
    return lambda slot: jnp.concatenate(halves(staged[slot]), axis=1)


def loop_held(places, held, visit, first=0):
    group = step_of(held.shape[0])

    def step(index, _):
        visit([first + index * group + s for s in range(group)])
        return 0

    lax.fori_loop(0, jnp.maximum(places.reach - first, 0) // group, step, 0)


def transposed_current_kernel(
    paired, *refs
):
    inputs, (blocks, x_ref, other), outputs, refs = refs[:3], refs[3:6], refs[6:9], refs[9:]
    column_sum, held, own, semaphore, staged, semaphores, row_halves = refs
    copies = [
        pltpu.make_async_copy(source, target, semaphore.at[n])
        for n, (source, target) in enumerate(zip((*inputs, x_ref), (*outputs, own)))
    ]
    for copy in copies:
        copy.start()
    stream = Stream(blocks, staged, semaphores)
    for copy in copies:
        copy.wait()
    places = Places(outputs, row_halves.shape[0], column_sum.shape[0], own.shape[-1] // LANES, paired)
    tiles = own.shape[-1] // LANES
    for t in range(tiles):
        for c, values in row_block_tiles(t, own, other, paired):
            row_halves[c * tiles + t] = stacked_halves(values)
    column_sum[...] = jnp.zeros_like(column_sum)

    def split(slot):
        pair = jnp.concatenate(halves(staged[slot]), axis=1)
        held[slot] = pair
        return pair

    stream.loop(places.reach, lambda slots: visit_transposed(slots, places, split, row_halves, column_sum))


def assemble_kernel(own, partner, column_sum, payload):
    tiles = own.shape[-1] // LANES
    near = payload.shape[0]
    for n in range(near):
        for t in range(tiles):
            payload[n, t] = own[:, lanes(t)]
            payload[n, tiles + t] = partner[:, lanes(t)]
            payload[n, 2 * tiles + t] = column_sum[n * tiles + t]
            payload[n, 3 * tiles + t] = column_sum[(near + n) * tiles + t]


def early_products(x, y, p):
    basis = jnp.concatenate([x, y, p], axis=0)
    outer = times_transpose(basis, basis, highest)
    return jnp.concatenate(
        [outer[0:8], outer[8:16, 8:24], outer[16:24, 16:24], jnp.zeros((8, LANES - 48), f32)], axis=1
    )


def lower_halves(previous):
    return stacked_halves(jnp.concatenate([jnp.zeros_like(previous), 0.5 * previous], axis=0))


def assemble_image_kernel(
    own, base_partner, sums, column_sum, x_partner, own_gram, payload, partner_halves
):
    tiles = own.shape[-1] // LANES
    near = payload.shape[0]
    partner = [base_partner[t] + sums[t] for t in range(tiles)]
    previous = [base_partner[tiles + t] for t in range(tiles)]
    for t in range(tiles):
        partner_halves[t] = lower_halves(previous[t])
    gram = own_gram[...] + early_products(
        x_partner[...], jnp.concatenate(partner, axis=1), jnp.concatenate(previous, axis=1)
    )
    for n in range(near):
        for t in range(tiles):
            payload[n, t] = own[:, lanes(t)]
            payload[n, tiles + t] = partner[t]
            payload[n, 2 * tiles + t] = column_sum[n * tiles + t, 0:8]
            payload[n, 3 * tiles + t] = column_sum[(near + n) * tiles + t, 0:8]
        payload[n, 4 * tiles] = gram


def first_partner_sums_kernel(parts, sums):
    near = parts.shape[0]
    tiles = parts.shape[1] // 4
    for t in range(tiles):
        sums[t] = balanced_sum([parts[n, 3 * tiles + t] for n in range(near)])


def partner_sums_kernel(parts, sums, gram):
    near = parts.shape[0]
    tiles = parts.shape[1] // 4
    for t in range(tiles):
        sums[t] = balanced_sum([parts[n, 3 * tiles + t] for n in range(near)])
    gram[...] = balanced_sum([parts[n, 4 * tiles] for n in range(near)])


def fill_column_set(column_halves, parts):
    near = parts.shape[0]
    tiles = parts.shape[1] // 4
    for n in range(near):
        for t in range(tiles):
            column_halves[n * tiles + t] = stacked_halves(parts[n, t])
            column_halves[(near + n) * tiles + t] = stacked_halves(parts[n, tiles + t])


def direct_held_kernel(paired, counts, rows, columns, held, parts, row_sum, column_halves):
    refs = counts, rows, columns
    places = Places(refs, row_sum.shape[0], column_halves.shape[0], parts.shape[1] // 4, paired)
    fill_column_set(column_halves, parts)
    row_sum[...] = jnp.zeros_like(row_sum)
    loop_held(
        places,
        held,
        lambda slots: visit_direct(slots, places, lambda slot: held[slot], column_halves, row_sum),
    )


def direct_kernel(
    paired, counts, rows, columns, blocks, parts, kept, mine, theirs,
    row_sum, rest, gram,
    staged, semaphores, column_halves,
):
    refs = counts, rows, columns
    places = Places(refs, row_sum.shape[0], column_halves.shape[0], parts.shape[1] // 4, paired)
    stream = Stream(blocks, staged, semaphores)
    gram[...] = mine[...] + theirs[...]
    fill_column_set(column_halves, parts)
    row_sum[...] = jnp.zeros_like(row_sum)
    first = staged.shape[0]
    loop_held(
        places,
        kept,
        lambda slots: visit_direct(
            slots, places, lambda slot: kept[slot - first], column_halves, row_sum
        ),
        first,
    )
    stream.loop(
        places.reach,
        lambda slots: visit_direct(slots, places, tile_from(staged), column_halves, row_sum),
    )
    for t in range(rest.shape[0]):
        rest[t] = row_sum[row_sum.shape[0] - rest.shape[0] + t]


def half_result(t, parts, diagonal, vectors):
    near = parts.shape[0]
    tiles = parts.shape[1] // 4
    return diagonal[:, lanes(t)] * vectors[:, lanes(t)] + balanced_sum(
        [parts[n, 2 * tiles + t] for n in range(near)]
    )


def combine_kernel(
    paired, parts, row_sum, diagonal, vectors, sums, other_sums, previous, mine, shipped, *rows
):
    tiles = parts.shape[1] // 4
    for t in range(tiles):
        shipped[t] = sums[t]
        shipped[tiles + t] = other_sums[t]
        total = half_result(t, parts, diagonal, vectors)
        if paired:
            mine[t] = total + row_sum[t]
            mine[tiles + t] = row_sum[tiles + t]
            mine[2 * tiles + t] = previous[:, lanes(t)]
        else:
            mine[:, lanes(t)] = total
            for c in range(rows[0].shape[0]):
                rows[0][c, :, lanes(t)] = row_sum[c * tiles + t]


def base_kernel(mine, theirs, previous, own, other):
    tiles = own.shape[0] // 2
    for t in range(tiles):
        own[t] = mine[t] + theirs[tiles + t]
        own[tiles + t] = previous[:, lanes(t)]
        other[:, lanes(t)] = theirs[t] + mine[tiles + t]


def image_kernel(base, received, image):
    for t in range(image.shape[-1] // LANES):
        image[:, lanes(t)] = base[t] + received[t]


def transposed_image_kernel(
    paired, counts, rows, columns, held, own, base_other, sums_other, p_ref, p_other, diagonal,
    x_ref, q_ref,
    column_sum, sum_halves, late, kept, gram, own_halves,
    row_halves,
):
    refs = counts, rows, columns
    places = Places(refs, row_halves.shape[0], column_sum.shape[0], own.shape[-1] // LANES, paired)
    width = own.shape[-1]
    tiles = width // LANES
    other = base_other
    if paired:
        other = base_other[...] + jnp.concatenate(
            [sums_other[tiles + t] for t in range(tiles)], axis=1
        )
        p_other = jnp.concatenate([p_other[2 * tiles + t] for t in range(tiles)], axis=1)
    for t in range(tiles):
        for (c, values), (_, previous) in zip(
            row_block_tiles(t, own, other, paired), row_block_tiles(t, p_ref, p_other, paired)
        ):
            row_halves[c * tiles + t] = stacked_halves(jnp.concatenate([values, previous], axis=0))
    column_sum[...] = jnp.zeros_like(column_sum)
    loop_held(
        places,
        held,
        lambda slots: visit_transposed(
            slots, places, lambda slot: held[slot], row_halves, column_sum
        ),
    )
    scale = jnp.where(lax.broadcasted_iota(jnp.int32, (16, 1), 0) < 8, 1.0, 0.5).astype(f32)
    for j in range(column_sum.shape[0]):
        sum_halves[j] = stacked_halves(column_sum[j] * scale)

    def keep(index, _):
        part = pl.ds(index * 8, 8)
        kept[part] = held[pl.ds(kept.shape[0] + index * 8, 8)]
        return 0

    lax.fori_loop(0, kept.shape[0] // 8, keep, 0)
    y, p, q = own[...], p_ref[...], q_ref[...]
    gram[...] = early_products(x_ref[...], y, p)
    for t in range(tiles):
        own_halves[t] = lower_halves(p[:, lanes(t)])
    rows = jnp.concatenate([x_ref[...], y, p], axis=0)
    terms = times_transpose(
        rows, jnp.concatenate([0.5 * q, 0.5 * diagonal[...] * y], axis=0), highest
    )
    image_previous = times_transpose(0.5 * diagonal[...] * y, p, highest)
    nothing = jnp.zeros((8, 16), f32)
    late[...] = jnp.concatenate(
        [
            nothing,
            terms[0:8, 0:8],
            nothing[:, 0:8],
            terms[8:16, 8:16],
            terms[8:16, 0:8] + image_previous,
            nothing,
            terms[16:24, 0:8],
            jnp.zeros((8, LANES - 72), f32),
        ],
        axis=1,
    )


def inner_kernel(parts, sum_halves, own_halves, partner_halves, late, for_partner, spread):
    near = parts.shape[0]
    tiles = parts.shape[1] // 4
    left = [
        stacked_halves(parts[n, first + t])
        for first in (0, tiles)
        for n in range(near)
        for t in range(tiles)
    ]
    for t in range(tiles):
        left.append(stacked_halves(balanced_sum([parts[n, 2 * tiles + t] for n in range(near)])))
    for t in range(tiles):
        left.append(stacked_halves(for_partner[t]))
    cross = times_transpose(
        jnp.concatenate(left, axis=1),
        jnp.concatenate(
            [
                ref[j]
                for ref in (sum_halves, own_halves, partner_halves)
                for j in range(ref.shape[0])
            ],
            axis=1,
        ),
    )
    terms = cross[0:8, 0:16] + cross[8:16, 0:16] + cross[0:8, 16:32]
    total = late[...] + jnp.concatenate(
        [jnp.zeros((8, 32), f32), terms, jnp.zeros((8, LANES - 48), f32)], axis=1
    )
    for n in range(spread.shape[0]):
        spread[n] = total


def eliminate_kernel(gram, x_ref, y_ref, ritz, inverse, pencil, image, residual):
    image[...] = y_ref[...]
    gram = gram[...]
    turned = gram.T

    def block(n):
        return gram[:, 8 * n : 8 * n + 8]

    def flipped(n):
        return turned[8 * n : 8 * n + 8, :]

    xx, xy, xp, yy, yp, pp = range(6)
    nothing = jnp.zeros((8, 8), f32)
    unit = (
        lax.broadcasted_iota(jnp.int32, (24, 24), 0) == lax.broadcasted_iota(jnp.int32, (24, 24), 1)
    ).astype(f32)
    work = jnp.concatenate(
        [
            gram[:, 0:24],
            jnp.concatenate([flipped(xy), block(yy), block(yp)], axis=1),
            jnp.concatenate([flipped(xp), flipped(yp), block(pp)], axis=1),
        ],
        axis=0,
    )
    work = jnp.concatenate([work, unit, jnp.zeros((24, LANES - 48), f32)], axis=1)
    pencil[...] = 0.5 * jnp.concatenate(
        [
            jnp.concatenate([block(xy) + flipped(xy), 2.0 * block(yy), block(yp)], axis=1),
            jnp.concatenate([2.0 * block(yy), nothing, nothing], axis=1),
            jnp.concatenate([flipped(yp), nothing, nothing], axis=1),
        ],
        axis=0,
    )
    row_ids = lax.broadcasted_iota(jnp.int32, (24, 1), 0)
    for k in range(0, 24, 2):
        if k == 8:
            factors = work[8:16, 24:32]
            ritz[...] = factors
            r = y_ref[...]
            for j in range(8):
                r = r + factors[:, j : j + 1] * x_ref[j : j + 1, :]
            residual[...] = r
        row, next_row = work[k : k + 1, :], work[k + 1 : k + 2, :]
        column = jnp.broadcast_to(work[:, k : k + 1], work.shape)
        next_column = jnp.broadcast_to(work[:, k + 1 : k + 2], work.shape)
        first, cross, second = column[k : k + 1], column[k + 1 : k + 2], next_column[k + 1 : k + 2]
        scale = 1.0 / first
        next_scale = first / (first * second - cross * cross)
        ratio = cross * scale
        work = (
            work
            - jnp.where(row_ids > k, column, 0.0) * (row * scale)
            - jnp.where(row_ids > k + 1, next_column - column * ratio, 0.0)
            * ((next_row - ratio * row) * next_scale)
        )
    inverse[...] = work[:, 24:48] * lax.rsqrt(jnp.sum(work[:, 0:24] * unit, axis=1, keepdims=True))


def finish_kernel(
    paired, inverse, pencil, inner_parts, ritz, y_ref, parts, received, row_sum, theirs, diagonal,
    residual_image, reduced,
):
    total = balanced_sum([inner_parts[n] for n in range(inner_parts.shape[0])])
    late = jnp.concatenate([total[:, 0:24], total[:, 24:48], total[:, 48:72]], axis=0)
    lower = inverse[...]
    left = times(lower, pencil[...] + late, highest) + times_transpose(lower, late, highest)
    reduced[...] = times_transpose(left, lower, highest)
    for t in range(theirs.shape[0]):
        s = half_result(t, parts, diagonal, y_ref) + received[t] + theirs[t]
        if paired:
            s = s + row_sum[t]
        for j in range(8):
            s = s + ritz[:, j : j + 1] * y_ref[j : j + 1, lanes(t)]
        residual_image[:, lanes(t)] = s


def local(tile_values, tile_row, tile_col, counts, diagonal, current, previous, previous_image, *, sizes):
    near, n_col = sizes
    slots, side = tile_values.shape[2], tile_values.shape[-1]
    width = current.shape[1]
    tiles = width // side
    paired = n_col == 2
    row_tiles = n_col * tiles
    column_tiles = 2 * near * tiles
    blocks = kept_in_hbm(tile_values.reshape(slots, side, side))
    places = [counts, tile_row, tile_col]
    diagonal = diagonal.reshape(1, width)

    def swap(values, axis="col"):
        return lax.ppermute(values, axis, [(0, 1), (1, 0)])

    def to_partner(values):
        return swap(values, "half")

    devices = ("half", "near", "col")

    def to_near(values):
        groups = [
            [(h * near + (p + (c + 1) % 2 * (near // 2)) % near) * n_col + c for p in range(near)]
            for h in range(2)
            for c in range(n_col)
        ]
        return lax.all_to_all(values, devices, 0, 0, tiled=True, axis_index_groups=groups)

    def from_columns(values):
        return swap(values) if paired else lax.all_gather(values, "col", axis=0)

    other = from_columns(current)
    partner = to_partner(current)
    *places, column_sum, held = call(
        functools.partial(transposed_current_kernel, paired),
        "transposed_current",
        [pltpu.SMEM(part.shape, part.dtype) for part in places]
        + [shape(column_tiles, 8, side), shape(slots, side, 2 * side, dtype=bf16)],
        [counts, *map(kept_in_hbm, places[1:]), blocks, kept_in_hbm(current), other],
        [pl.BlockSpec(memory_space=pl.ANY)] + [in_hbm] * 4 + [in_vmem],
        [pltpu.VMEM((8, width), f32), pltpu.SemaphoreType.DMA((4,))]
        + stream_scratch(slots, side)
        + [pltpu.VMEM((row_tiles, 16, side), bf16)],
        micros=3.0,
    )
    places = [pltpu.with_memory_space_constraint(part, pltpu.SMEM) for part in places]
    payload = call(
        assemble_kernel,
        "assemble_current",
        shape(near, 4 * tiles, 8, side),
        [current, partner, column_sum],
        [in_vmem] * 3,
    )
    parts = to_near(payload)
    sums = call(
        first_partner_sums_kernel, "partner_sums", shape(tiles, 8, side), [parts], [in_vmem]
    )
    other_sums = swap(sums) if paired else sums
    row_sum = call(
        functools.partial(direct_held_kernel, paired),
        "direct_current",
        shape(row_tiles, 8, side),
        [*places, held, parts],
        [in_smem] * 3 + [in_vmem] * 2,
        [pltpu.VMEM((column_tiles, 16, side), bf16)],
        micros=2.2,
    )
    combine = functools.partial(
        call,
        functools.partial(combine_kernel, paired),
        "combine",
        operands=[parts, row_sum, diagonal, current, sums, other_sums, previous],
        specs=[in_vmem] * 7,
    )
    if paired:
        mine, shipped = combine(out_shape=[shape(3 * tiles, 8, side), shape(2 * tiles, 8, side)])
        theirs = previous_other = swap(mine)
        base, base_other = call(
            base_kernel,
            "base",
            [shape(2 * tiles, 8, side), shape(8, width)],
            [mine, theirs, previous],
            [in_vmem] * 3,
        )
    else:
        mine, shipped, rows = combine(
            out_shape=[shape(8, width), shape(2 * tiles, 8, side), shape(n_col, 8, width)]
        )
        base = mine + jnp.sum(lax.all_to_all(rows, "col", 0, 0, tiled=True), axis=0)
        base = jnp.concatenate([base, previous], axis=1)
        base = base.reshape(8, 2 * tiles, side).transpose(1, 0, 2)
        previous_other = lax.all_gather(previous, "col", axis=0)
    first_received = to_partner(shipped)
    base_partner = to_partner(base)
    image = call(image_kernel, "image", shape(8, width), [base, first_received], [in_vmem] * 2)
    if not paired:
        base_other = lax.all_gather(image, "col", axis=0)
    column_sum, sum_halves, late, kept, own_gram, own_halves = call(
        functools.partial(transposed_image_kernel, paired),
        "transposed_image",
        [
            shape(column_tiles, 16, side),
            shape(column_tiles, 32, side, dtype=bf16),
            shape(8, LANES),
            shape(slots // 2, side, 2 * side, dtype=bf16),
            shape(8, LANES),
            shape(tiles, 32, side, dtype=bf16),
        ],
        [
            *places, held, image, base_other, first_received, previous, previous_other, diagonal,
            current, previous_image,
        ],
        [in_smem] * 3 + [in_vmem] * 9,
        [pltpu.VMEM((row_tiles, 32, side), bf16)],
        micros=1.8,
    )
    payload, partner_halves = call(
        assemble_image_kernel,
        "assemble_image",
        [
            shape(near, 4 * tiles + 1, 8, side),
            shape(tiles, 32, side, dtype=bf16),
        ],
        [image, base_partner, sums, column_sum, partner, own_gram],
        [in_vmem] * 6,
    )
    parts = to_near(payload)
    for_partner, gram = call(
        partner_sums_kernel,
        "partner_sums",
        [shape(tiles, 8, side), shape(8, LANES)],
        [parts],
        [in_vmem],
    )
    their_gram = swap(gram) if paired else lax.psum(gram, "col") - gram
    spread = call(
        inner_kernel,
        "inner_products",
        shape(2 * near * n_col, 8, LANES),
        [parts, sum_halves, own_halves, partner_halves, late, for_partner],
        [in_vmem] * 6,
        micros=1.1,
    )
    everyone = [
        [(h * near + n) * n_col + c for n in range(near)[::-1] for c in range(n_col) for h in range(2)]
    ]
    inner_parts = lax.all_to_all(spread, devices, 0, 0, tiled=True, axis_index_groups=everyone)
    received = to_partner(for_partner)
    row_sum, rest, gram = call(
        functools.partial(direct_kernel, paired),
        "direct_image",
        [
            shape(row_tiles, 8, side),
            shape(tiles if paired else row_tiles, 8, side),
            shape(8, LANES),
        ],
        [*places, blocks, parts, kept, gram, their_gram],
        [in_smem] * 3 + [in_hbm] + [in_vmem] * 4,
        stream_scratch(slots // 2, side) + [pltpu.VMEM((column_tiles, 16, side), bf16)],
        micros=3.4,
    )
    if paired:
        theirs = swap(rest)
    else:
        rest = rest.reshape(n_col, tiles, 8, side)
        theirs = jnp.sum(lax.all_to_all(rest, "col", 0, 0, tiled=True), axis=0)
    ritz, inverse, pencil, image_out, residual = call(
        eliminate_kernel,
        "eliminate",
        [shape(8, 8), shape(24, 24), shape(24, 24), shape(8, width), shape(8, width)],
        [gram, current, image],
        [in_vmem] * 3,
        micros=1.3,
    )
    residual_image, reduced = call(
        functools.partial(finish_kernel, paired),
        "finish",
        [shape(8, width), shape(24, 24)],
        [
            inverse, pencil, inner_parts, ritz, image, parts, received, row_sum, theirs, diagonal,
        ],
        [in_vmem] * 10,
        micros=1.0,
    )
    return (image_out, residual, residual_image, reduced)


def solution(mesh):
    n_row, n_col = mesh.shape["row"], mesh.shape["col"]
    near = n_row // 2
    cut = jax.sharding.Mesh(mesh.devices.reshape(2, near, n_col), ("half", "near", "col"))
    row = ("half", "near")
    vectors = P(None, ("half", "near", "col"))
    return jax.shard_map(
        functools.partial(local, sizes=(near, n_col)),
        mesh=cut,
        in_specs=(
            P(row, "col", None, None, None),
            P(row, "col", None),
            P(row, "col", None),
            P(row, "col"),
            P(("half", "near", "col")),
            vectors,
            vectors,
            vectors,
        ),
        out_specs=(vectors, vectors, vectors, P()),
        check_vma=False,
    )
```
